512 devices in a mesh: src: 32 (over z, core), tgt: 16 (over y, x).
Axes of the slice: x: 4, y: 4, z: 16, core: 2. Of those that a mesh axis runs over, the one named last changes fastest.
Arguments:
- source_embed: bfloat16 [512, 128, 128], P('src', None, 'tgt'), may hold values from -4 to 4
- target_embed: bfloat16 [256, 128, 128], P('tgt', None, 'src'), may hold values from -4 to 4
- source_mass: float32 [512, 128], P('src'), may hold values from 10 to 14
- target_mass: float32 [256, 128], P('tgt'), may hold values from 10 to 14
- target_start: float32 [256, 128], P('tgt'), may hold values from -6 to 6
- block_pairs: int32 [32, 16, 128, 2], P('src', 'tgt'), may hold values from 0 to 15, as said below
- counts: int32 [32, 16], P('src', 'tgt'), may hold values from 16 to 128, as said below
Outputs:
- sender_log_scaling: float32 [512, 128], P('src')
- target_dual_potential: float32 [256, 128], P('tgt')
The draws below stay inside these ranges and needn't reach their ends.
Inputs may be any that keep to these rules, and one draw needn't show every extreme that they name: `block_pairs`: entry 0 of a slot is a local source block (below 16), entry 1 a local target block (below 16). The live slots of a device name distinct pairs; its first 16 slots name each of its target blocks once and each of its source blocks at least once. Slots at or past the device's count are not kept and hold arbitrary block numbers. `counts`: some device has all 128 slots live in every draw.
All inputs are finite; a program needn't handle non-finite values.
Results may differ from the reference program's by a relative error of at most 0.0003.
Values may be sent and summed in bfloat16 or wider, within the bound.
No kernel may reach another device: no remote copies, remote signals or barrier semaphores. Data moves between devices by JAX's collectives and lax.ppermute only.
A program may use at most 64 MiB of HBM per device.

```python
import jax
import jax.numpy as jnp
from jax import lax

D = 128
BLK = 128
ITERS = 2
SB_DEV = 16
TB_DEV = 16
PAIRS = 128
SBLOCKS = 512
TBLOCKS = 256
N_SRC = 32
N_TGT = 16


def device_shifts(key):
    return jax.random.randint(jax.random.fold_in(key, 7), (N_SRC, N_TGT), 0, TB_DEV)


def draw_block_pairs(key, part):
    shifts = device_shifts(key).reshape(-1)
    grid_cell_index = lax.iota(jnp.int32, SB_DEV * TB_DEV)
    source_block = grid_cell_index // TB_DEV
    target_block = grid_cell_index % TB_DEV
    subkeys = jax.random.split(jax.random.fold_in(key, 8), N_SRC * N_TGT)

    def one_device(subkey, device_shift):
        offset = (target_block - device_shift) % TB_DEV
        leading = source_block == offset % SB_DEV
        ranking = jax.random.permutation(subkey, SB_DEV * TB_DEV).astype(jnp.int32)
        similarity_matrix = jnp.where(leading, ranking, SB_DEV * TB_DEV + ranking)
        ordering = jnp.argsort(similarity_matrix)[:PAIRS]
        return jnp.stack([source_block[ordering], target_block[ordering]], axis=1)
    enrolled_pairs = jax.vmap(one_device)(subkeys, shifts)
    return enrolled_pairs.reshape(N_SRC, N_TGT, PAIRS, 2).astype(jnp.int32)


def draw_counts(key, part):
    rolled = jax.random.randint(jax.random.fold_in(key, 9), (N_SRC * N_TGT,), 0, 17)
    loads = TB_DEV + (PAIRS - TB_DEV) * rolled * rolled * rolled // 4096
    hottest = jax.random.randint(jax.random.fold_in(key, 10), (), 0, N_SRC * N_TGT)
    loads = jnp.where(lax.iota(jnp.int32, N_SRC * N_TGT) == hottest, PAIRS, loads)
    return loads.reshape(N_SRC, N_TGT).astype(jnp.int32)


def embeddings(key):
    source_key = jax.random.fold_in(key, 21)
    target_key = jax.random.fold_in(key, 22)
    source_draw = jnp.clip(jax.random.normal(source_key, (SBLOCKS, BLK, D), jnp.float32), -4.0, 4.0)
    target_draw = jnp.clip(jax.random.normal(target_key, (TBLOCKS, BLK, D), jnp.float32), -4.0, 4.0)
    return (source_draw, target_draw)


def draw_source_embed(key, part):
    return embeddings(key)[0].astype(jnp.bfloat16)


def draw_target_embed(key, part):
    return embeddings(key)[1].astype(jnp.bfloat16)


def level_of(key, dims, shards, low, high):
    level, own = 1.0, jax.random.fold_in(key, 6)
    for dim, blocks in shards:
        steps = jnp.exp(jax.random.uniform(jax.random.fold_in(own, dim), (blocks,), jnp.float32, low / len(shards), high / len(shards)))
        level = level * jnp.repeat(steps, dims[dim] // blocks).reshape([-1 if axis == dim else 1 for axis in range(len(dims))])
    return level


def gaussian(stream_key, dims, deviation, most, pieces=(), held_as=jnp.bfloat16):
    result = deviation * jax.random.normal(stream_key, dims, jnp.float32)
    if pieces:
        result = result * level_of(stream_key, dims, pieces, -0.22, 0.18)
    return jnp.clip(result, -most, most).astype(held_as)


def setup_inputs(seed: int = 0) -> dict:
    seeds = jax.random.split(jax.random.key(seed), 8)
    source_embed = draw_source_embed(jax.random.fold_in(seeds[7], 71), 0)
    target_embed = draw_target_embed(jax.random.fold_in(seeds[7], 71), 0)
    source_mass = jnp.clip(10.0 + 4.0 * jax.random.uniform(seeds[2], (SBLOCKS, BLK), jnp.float32) ** level_of(seeds[2], (SBLOCKS, BLK), ((0, 32),), -0.2, 0.2), 10.0, 14.0)
    target_mass = jnp.clip(10.0 + 4.0 * jax.random.uniform(seeds[3], (TBLOCKS, BLK), jnp.float32) ** level_of(seeds[3], (TBLOCKS, BLK), ((0, 16),), -0.2, 0.2), 10.0, 14.0)
    target_start = gaussian(seeds[4], (TBLOCKS, BLK), 1.0, 6.0, ((0, 16),), jnp.float32)
    block_pairs = draw_block_pairs(jax.random.fold_in(seeds[7], 71), 0)
    counts = draw_counts(jax.random.fold_in(seeds[7], 71), 0)
    return dict(source_embed=source_embed, target_embed=target_embed, source_mass=source_mass, target_mass=target_mass, target_start=target_start, block_pairs=block_pairs, counts=counts)


smoothing_epsilon = 4.0
empty_peak = -1e30
list_batch = 64


def kept_list(block_pairs, counts):
    layout = block_pairs.shape[:3]
    device_src = lax.broadcasted_iota(jnp.int32, layout, 0)
    device_tgt = lax.broadcasted_iota(jnp.int32, layout, 1)
    slot_ids = lax.broadcasted_iota(jnp.int32, layout, 2)
    live = (slot_ids < counts[:, :, None]).reshape(-1)
    source_ids = (device_src * SB_DEV + block_pairs[..., 0]).reshape(-1).astype(jnp.int32)
    target_ids = (device_tgt * TB_DEV + block_pairs[..., 1]).reshape(-1).astype(jnp.int32)
    ordering = jnp.argsort(jnp.where(live, 0, 1).astype(jnp.int32), stable=True)
    total = jnp.sum(live.astype(jnp.int32)).astype(jnp.int32)
    padding = jnp.zeros((list_batch,), jnp.int32)
    source_ids = jnp.concatenate([source_ids[ordering], padding])
    target_ids = jnp.concatenate([target_ids[ordering], padding])
    live = jnp.concatenate([live[ordering], jnp.zeros((list_batch,), bool)])
    return source_ids, target_ids, live, total


def absorb(maxima, totals, targets, block_peak, block_total):
    raised = maxima.at[targets].max(block_peak)
    totals = totals * jnp.exp(maxima - raised)
    totals = totals.at[targets].add(block_total * jnp.exp(block_peak - raised[targets]))
    return raised, totals


def half_step(local_side, far_side, potential, local_ids, far_ids, live, total, log_mass):
    def group(counter, running):
        maxima, totals = running
        offset = (counter * list_batch).astype(jnp.int32)
        near = lax.dynamic_slice_in_dim(local_ids, offset, list_batch)
        distant = lax.dynamic_slice_in_dim(far_ids, offset, list_batch)
        usable = lax.dynamic_slice_in_dim(live, offset, list_batch)
        query_frame_vectors = local_side[near].astype(jnp.float32)
        reply_frame_vectors = far_side[distant].astype(jnp.float32)
        similarity_matrix = jnp.einsum("fdg,fwg->fdw", query_frame_vectors, reply_frame_vectors, precision=lax.Precision.HIGHEST) / smoothing_epsilon
        similarity_matrix = similarity_matrix + potential[distant][:, None, :]
        block_peak = jnp.max(similarity_matrix, axis=2)
        block_total = jnp.sum(jnp.exp(similarity_matrix - block_peak[:, :, None]), axis=2)
        block_peak = jnp.where(usable[:, None], block_peak, empty_peak)
        block_total = jnp.where(usable[:, None], block_total, 0.0)
        return absorb(maxima, totals, near, block_peak, block_total)

    groups = ((total + list_batch - 1) // list_batch).astype(jnp.int32)
    start_max = jnp.full(log_mass.shape, empty_peak, jnp.float32)
    start_sum = jnp.zeros(log_mass.shape, jnp.float32)
    maxima, totals = lax.fori_loop(jnp.int32(0), groups, group, (start_max, start_sum))
    return log_mass - (maxima + jnp.log(totals))


def reference(source_embed, target_embed, source_mass, target_mass, target_start, block_pairs, counts):
    source_ids, target_ids, live, total = kept_list(block_pairs, counts)
    target_dual_potential = target_start
    sender_log_scaling = source_mass
    for iteration in range(ITERS):
        sender_log_scaling = half_step(source_embed, target_embed, target_dual_potential, source_ids, target_ids, live, total, source_mass)
        target_dual_potential = half_step(target_embed, source_embed, sender_log_scaling, target_ids, source_ids, live, total, target_mass)
    return sender_log_scaling, target_dual_potential
```

```python
import functools
import math

import jax
import jax.numpy as jnp
from jax import lax
from jax.experimental import pallas as pl
from jax.experimental.pallas import tpu as pltpu
from jax.sharding import Mesh
from jax.sharding import PartitionSpec as P

ITERS = 2
SRC = ("z", "c")

smoothing_epsilon = 4.0
empty_peak = -1e30
log2e = 1.0 / math.log(2.0)
to_log2 = log2e / smoothing_epsilon
group = 4
pot_most = 20.0
sum_least = 4.3e-18
sum_most = 5e34


def log_sum_exp(pieces):
    peak = functools.reduce(jnp.maximum, pieces)
    total = functools.reduce(jnp.add, [jnp.exp(piece - peak) for piece in pieces])
    return peak + jnp.log(total)


def scores(rows, columns):
    return lax.dot_general(
        rows, columns, (((1,), (0,)), ((), ())), preferred_element_type=jnp.float32
    )


def over_slots(count, body):
    whole = count // group

    @pl.loop(0, whole)
    def _(step):
        for lane in range(group):
            body(step * group + lane)

    @pl.loop(whole * group, count)
    def _(slot):
        body(slot)


def within(potential, sums):
    fine = (
        (jnp.abs(potential) <= pot_most) & (sums >= sum_least) & (sums <= sum_most)
    )
    return jnp.min(jnp.where(fine, 1.0, 0.0)) > 0.5


def rows_kept(sums, row_of):
    for block in range(sums.shape[0]):
        sums[block : block + 1, :] = row_of(block)


def exact_rows(count, pairs, rows, columns, potential, peak, total, sums):
    peak[...] = jnp.full_like(peak, empty_peak)
    total[...] = jnp.zeros_like(total)

    @pl.loop(0, count)
    def _(slot):
        source, target = pairs[0, slot], pairs[1, slot]
        value = scores(rows[source], columns[target]) * to_log2
        value = value + potential[pl.ds(target, 1), :] * log2e
        raised = jnp.maximum(peak[source], value)
        total[source] = total[source] * jnp.exp2(peak[source] - raised) + jnp.exp2(
            value - raised
        )
        peak[source] = raised

    def one(block):
        tall, across = peak[block].T, total[block].T
        most = jnp.max(tall, axis=0, keepdims=True)
        summed = jnp.sum(across * jnp.exp2(tall - most), axis=0, keepdims=True)
        return most / log2e + jnp.log(summed)

    rows_kept(sums, one)


def exact_columns(count, pairs, rows, columns, potential, wide, peak, total, sums):
    peak[...] = jnp.full_like(peak, empty_peak)
    total[...] = jnp.zeros_like(total)
    for block in range(wide.shape[0]):
        wide[block] = jnp.broadcast_to(potential[block : block + 1, :], wide.shape[1:]).T

    @pl.loop(0, count)
    def _(slot):
        source, target = pairs[0, slot], pairs[1, slot]
        value = scores(rows[source], columns[target]) * to_log2
        value = value + wide[source] * log2e
        raised = jnp.maximum(peak[target], value)
        total[target] = total[target] * jnp.exp2(peak[target] - raised) + jnp.exp2(
            value - raised
        )
        peak[target] = raised

    def one(block):
        most = jnp.max(peak[block], axis=0, keepdims=True)
        summed = jnp.sum(total[block] * jnp.exp2(peak[block] - most), axis=0, keepdims=True)
        return most / log2e + jnp.log(summed)

    rows_kept(sums, one)


def spread(partial, sums):
    partial[...] = jnp.broadcast_to(sums[...][None], partial.shape)


def row_pass(count, pairs, rows, columns, potential, kernel_of, weights, total, peak, sums, partial):
    weights[...] = jnp.exp(potential[...])
    total[...] = jnp.zeros_like(total)

    def body(slot):
        source, target = pairs[0, slot], pairs[1, slot]
        total[source] = total[source] + kernel_of(slot, source, target) * weights[
            pl.ds(target, 1), :
        ]

    over_slots(count, body)
    rows_kept(sums, lambda block: jnp.sum(total[block].T, axis=0, keepdims=True))
    fine = within(potential[...], sums[...])

    @pl.when(fine)
    def _():
        sums[...] = jnp.log(sums[...])

    @pl.when(jnp.logical_not(fine))
    def _():
        exact_rows(count, pairs, rows, columns, potential, peak, total, sums)

    spread(partial, sums)


def first_kernel(
    count_ref, pairs, source, target, start, cached, rows, columns, partial,
    wide_source, wide_target, weights, total, peak, sums,
):
    blocks = source.shape[1]
    features = source.shape[2]
    for device in range(source.shape[0]):
        wide_source[:, pl.ds(device * features, features), :] = source[device].astype(
            jnp.float32
        )
    cores, rings, _, parts, _ = target.shape
    for ring in range(rings):
        for core in range(cores):
            at = (ring * cores + core) * parts
            wide_target[:, pl.ds(at, parts), :] = target[core, ring].astype(jnp.float32)
    for block in range(blocks):
        rows[block] = wide_source[block].T.astype(jnp.bfloat16)
        columns[block] = wide_target[block].astype(jnp.bfloat16)

    def kernel_of(slot, source, target):
        value = jnp.exp2(scores(rows[source], columns[target]) * to_log2)
        cached[slot] = value
        return value

    row_pass(
        count_ref[0], pairs, rows, columns, start, kernel_of, weights, total, peak, sums, partial
    )


def column_kernel(
    count_ref, pairs, cached, rows, columns, gathered, mass, scaling, partial,
    wide, slim, total, peak, sums,
):
    count = count_ref[0]
    scaling[...] = mass[...] - log_sum_exp([gathered[k] for k in range(gathered.shape[0])])
    weights = jnp.exp(scaling[...])
    for block in range(wide.shape[0]):
        wide[block] = jnp.broadcast_to(weights[block : block + 1, :], wide.shape[1:]).T
    slim[...] = jnp.zeros_like(slim)

    def body(slot):
        source, target = pairs[0, slot], pairs[1, slot]
        value = cached[slot] * wide[source]
        value = value.reshape(-1, 8, value.shape[-1])
        slim[target] = slim[target] + jnp.sum(value, axis=0)

    over_slots(count, body)
    rows_kept(sums, lambda block: jnp.sum(slim[block], axis=0, keepdims=True))
    fine = within(scaling[...], sums[...])

    @pl.when(fine)
    def _():
        sums[...] = jnp.log(sums[...])

    @pl.when(jnp.logical_not(fine))
    def _():
        exact_columns(count, pairs, rows, columns, scaling, wide, peak, total, sums)

    partial[...] = sums[...]


def row_kernel(
    count_ref, pairs, cached, rows, columns, gathered, mass, partial,
    potential, weights, total, peak, sums,
):
    potential[...] = mass[...] - log_sum_exp([gathered[k] for k in range(gathered.shape[0])])
    row_pass(
        count_ref[0], pairs, rows, columns, potential,
        lambda slot, source, target: cached[slot],
        weights, total, peak, sums, partial,
    )


def called(body, outs, scratch, *operands):
    smem = pl.BlockSpec(memory_space=pltpu.SMEM)
    vmem = pl.BlockSpec(memory_space=pltpu.VMEM)
    return pl.pallas_call(
        body,
        out_shape=outs,
        in_specs=[smem, smem] + [vmem] * (len(operands) - 2),
        out_specs=[vmem] * len(outs),
        scratch_shapes=scratch,
        compiler_params=pltpu.CompilerParams(vmem_limit_bytes=40 * 1024 * 1024),
    )(*operands)


def copies(x, axis):
    return jnp.broadcast_to(x[None], (lax.axis_size(axis), *x.shape))


def exchanged(x, axis):
    return lax.all_to_all(x, axis, 0, 0, tiled=True)


def on_device(
    source_embed, target_embed, source_mass, target_mass, target_start, block_pairs, counts
):
    f32, bf16 = jnp.float32, jnp.bfloat16
    slots = block_pairs.shape[2]
    pairs = block_pairs.reshape(slots, 2).T
    count = counts.reshape(1)
    source_blocks, frames, _ = source_embed.shape
    target_blocks = target_embed.shape[0]
    columns_gathered = exchanged(copies(jnp.swapaxes(target_embed, 1, 2), "z"), "z")
    source = exchanged(copies(jnp.swapaxes(source_embed, 1, 2), "tgt"), "tgt")
    target = lax.all_gather(columns_gathered, "c")
    across = lax.axis_size("tgt")
    features = across * source_embed.shape[2]
    line = jax.ShapeDtypeStruct((source_blocks, frames), f32)
    many = jax.ShapeDtypeStruct((across, source_blocks, frames), f32)
    square = pltpu.VMEM((source_blocks, frames, frames), f32)
    flat = pltpu.VMEM((source_blocks, frames), f32)
    cached, rows, columns, partial = called(
        first_kernel,
        [
            pltpu.VMEM((slots, frames, frames), f32),
            pltpu.VMEM((source_blocks, frames, features), bf16),
            pltpu.VMEM((target_blocks, features, frames), bf16),
            many,
        ],
        [
            pltpu.VMEM((source_blocks, features, frames), f32),
            pltpu.VMEM((target_blocks, features, frames), f32),
            flat, square, square, flat,
        ],
        count, pairs, source, target, target_start,
    )
    kept = [count, pairs]
    kept += [pltpu.with_memory_space_constraint(x, pltpu.VMEM) for x in (cached, rows, columns)]
    for iteration in range(ITERS):
        scaling, partial = called(
            column_kernel,
            [line, line],
            [square, pltpu.VMEM((target_blocks, 8, frames), f32), square, square, flat],
            *kept, exchanged(partial, "tgt"), source_mass,
        )
        both = lax.all_gather(partial, "c")
        merged = log_sum_exp([both[0], both[1]])
        gathered = exchanged(copies(merged, "z"), "z")
        if iteration < ITERS - 1:
            (partial,) = called(
                row_kernel,
                [many],
                [flat, flat, square, square, flat],
                *kept, gathered, target_mass,
            )
    potential = target_mass - log_sum_exp([gathered[k] for k in range(gathered.shape[0])])
    return scaling, potential


def solution(mesh):
    split = Mesh(mesh.devices.reshape(16, 2, mesh.shape["tgt"]), ("z", "c", "tgt"))
    placed = (
        P(SRC, None, "tgt"),
        P("tgt", None, SRC),
        P(SRC, None),
        P("tgt", None),
        P("tgt", None),
        P(SRC, "tgt", None, None),
        P(SRC, "tgt"),
    )
    return jax.shard_map(
        on_device,
        mesh=split,
        in_specs=placed,
        out_specs=(P(SRC, None), P("tgt", None)),
        check_vma=False,
    )
```

```python
import functools
import math

import jax
import jax.numpy as jnp
from jax import lax
from jax.experimental import pallas as pl
from jax.experimental.pallas import tpu as pltpu
from jax.sharding import Mesh
from jax.sharding import PartitionSpec as P

ITERS = 2
SRC = ("z", "c")

smoothing_epsilon = 4.0
empty_peak = -1e30
log2e = 1.0 / math.log(2.0)
to_log2 = log2e / smoothing_epsilon
group = 4
pot_most = 20.0
sum_least = 4.3e-18
sum_most = 5e34


def log_sum_exp(pieces):
    peak = functools.reduce(jnp.maximum, pieces)
    total = functools.reduce(jnp.add, [jnp.exp(piece - peak) for piece in pieces])
    return peak + jnp.log(total)


def scores(rows, columns):
    return lax.dot_general(
        rows, columns, (((1,), (0,)), ((), ())), preferred_element_type=jnp.float32
    )


def over_slots(count, body):
    whole = count // group

    @pl.loop(0, whole)
    def _(step):
        for lane in range(group):
            body(step * group + lane)

    @pl.loop(whole * group, count)
    def _(slot):
        body(slot)


def within(potential, sums):
    fine = (
        (jnp.abs(potential) <= pot_most) & (sums >= sum_least) & (sums <= sum_most)
    )
    return jnp.min(jnp.where(fine, 1.0, 0.0)) > 0.5


def rows_kept(sums, row_of):
    for block in range(sums.shape[0]):
        sums[block : block + 1, :] = row_of(block)


def exact_rows(count, pairs, rows, columns, potential, peak, total, sums):
    peak[...] = jnp.full_like(peak, empty_peak)
    total[...] = jnp.zeros_like(total)

    @pl.loop(0, count)
    def _(slot):
        source, target = pairs[0, slot], pairs[1, slot]
        value = scores(rows[source], columns[target]) * to_log2
        value = value + potential[pl.ds(target, 1), :] * log2e
        raised = jnp.maximum(peak[source], value)
        total[source] = total[source] * jnp.exp2(peak[source] - raised) + jnp.exp2(
            value - raised
        )
        peak[source] = raised

    def one(block):
        tall, across = peak[block].T, total[block].T
        most = jnp.max(tall, axis=0, keepdims=True)
        summed = jnp.sum(across * jnp.exp2(tall - most), axis=0, keepdims=True)
        return most / log2e + jnp.log(summed)

    rows_kept(sums, one)


def exact_columns(count, pairs, rows, columns, potential, wide, peak, total, sums):
    peak[...] = jnp.full_like(peak, empty_peak)
    total[...] = jnp.zeros_like(total)
    for block in range(wide.shape[0]):
        wide[block] = jnp.broadcast_to(potential[block : block + 1, :], wide.shape[1:]).T

    @pl.loop(0, count)
    def _(slot):
        source, target = pairs[0, slot], pairs[1, slot]
        value = scores(rows[source], columns[target]) * to_log2
        value = value + wide[source] * log2e
        raised = jnp.maximum(peak[target], value)
        total[target] = total[target] * jnp.exp2(peak[target] - raised) + jnp.exp2(
            value - raised
        )
        peak[target] = raised

    def one(block):
        most = jnp.max(peak[block], axis=0, keepdims=True)
        summed = jnp.sum(total[block] * jnp.exp2(peak[block] - most), axis=0, keepdims=True)
        return most / log2e + jnp.log(summed)

    rows_kept(sums, one)


def spread(partial, sums):
    partial[...] = jnp.broadcast_to(sums[...][None], partial.shape)


def row_pass(count, pairs, rows, columns, potential, kernel_of, weights, total, peak, sums, partial):
    weights[...] = jnp.exp(potential[...])
    total[...] = jnp.zeros_like(total)

    def body(slot):
        source, target = pairs[0, slot], pairs[1, slot]
        total[source] = total[source] + kernel_of(slot, source, target) * weights[
            pl.ds(target, 1), :
        ]

    over_slots(count, body)
    rows_kept(sums, lambda block: jnp.sum(total[block].T, axis=0, keepdims=True))
    fine = within(potential[...], sums[...])

    @pl.when(fine)
    def _():
        sums[...] = jnp.log(sums[...])

    @pl.when(jnp.logical_not(fine))
    def _():
        exact_rows(count, pairs, rows, columns, potential, peak, total, sums)

    spread(partial, sums)


def first_kernel(
    count_ref, pairs, source, target, start, cached, rows, columns, partial,
    wide_source, wide_target, weights, total, peak, sums,
):
    blocks = source.shape[1]
    features = source.shape[2]
    for device in range(source.shape[0]):
        wide_source[:, pl.ds(device * features, features), :] = source[device].astype(
            jnp.float32
        )
    cores, rings, _, parts, _ = target.shape
    for ring in range(rings):
        for core in range(cores):
            at = (ring * cores + core) * parts
            wide_target[:, pl.ds(at, parts), :] = target[core, ring].astype(jnp.float32)
    for block in range(blocks):
        rows[block] = wide_source[block].T.astype(jnp.bfloat16)
        columns[block] = wide_target[block].astype(jnp.bfloat16)

    def kernel_of(slot, source, target):
        value = jnp.exp2(scores(rows[source], columns[target]) * to_log2)
        cached[slot] = value
        return value

    row_pass(
        count_ref[0], pairs, rows, columns, start, kernel_of, weights, total, peak, sums, partial
    )


def column_kernel(
    count_ref, pairs, cached, rows, columns, gathered, mass, scaling, partial,
    wide, slim, total, peak, sums,
):
    count = count_ref[0]
    scaling[...] = mass[...] - log_sum_exp([gathered[k] for k in range(gathered.shape[0])])
    weights = jnp.exp(scaling[...])
    for block in range(wide.shape[0]):
        wide[block] = jnp.broadcast_to(weights[block : block + 1, :], wide.shape[1:]).T
    slim[...] = jnp.zeros_like(slim)

    def body(slot):
        source, target = pairs[0, slot], pairs[1, slot]
        value = cached[slot] * wide[source]
        value = value.reshape(-1, 8, value.shape[-1])
        slim[target] = slim[target] + jnp.sum(value, axis=0)

    over_slots(count, body)
    rows_kept(sums, lambda block: jnp.sum(slim[block], axis=0, keepdims=True))
    fine = within(scaling[...], sums[...])

    @pl.when(fine)
    def _():
        sums[...] = jnp.log(sums[...])

    @pl.when(jnp.logical_not(fine))
    def _():
        exact_columns(count, pairs, rows, columns, scaling, wide, peak, total, sums)

    partial[...] = sums[...]


def row_kernel(
    count_ref, pairs, cached, rows, columns, gathered, mass, partial,
    potential, weights, total, peak, sums,
):
    potential[...] = mass[...] - log_sum_exp([gathered[k] for k in range(gathered.shape[0])])
    row_pass(
        count_ref[0], pairs, rows, columns, potential,
        lambda slot, source, target: cached[slot],
        weights, total, peak, sums, partial,
    )


def called(body, outs, scratch, *operands):
    smem = pl.BlockSpec(memory_space=pltpu.SMEM)
    vmem = pl.BlockSpec(memory_space=pltpu.VMEM)
    return pl.pallas_call(
        body,
        out_shape=outs,
        in_specs=[smem, smem] + [vmem] * (len(operands) - 2),
        out_specs=[vmem] * len(outs),
        scratch_shapes=scratch,
        compiler_params=pltpu.CompilerParams(vmem_limit_bytes=40 * 1024 * 1024),
    )(*operands)


def copies(x, axis):
    return jnp.broadcast_to(x[None], (lax.axis_size(axis), *x.shape))


def exchanged(x, axis):
    return lax.all_to_all(x, axis, 0, 0, tiled=True)


def on_device(
    source_embed, target_embed, source_mass, target_mass, target_start, block_pairs, counts
):
    f32, bf16 = jnp.float32, jnp.bfloat16
    slots = block_pairs.shape[2]
    pairs = block_pairs.reshape(slots, 2).T
    count = counts.reshape(1)
    source_blocks, frames, _ = source_embed.shape
    target_blocks = target_embed.shape[0]
    columns_gathered = exchanged(copies(jnp.swapaxes(target_embed, 1, 2), "z"), "z")
    source = lax.all_gather(jnp.swapaxes(source_embed, 1, 2), "tgt")
    target = lax.all_gather(columns_gathered, "c")
    across = lax.axis_size("tgt")
    features = across * source_embed.shape[2]
    line = jax.ShapeDtypeStruct((source_blocks, frames), f32)
    many = jax.ShapeDtypeStruct((across, source_blocks, frames), f32)
    square = pltpu.VMEM((source_blocks, frames, frames), f32)
    flat = pltpu.VMEM((source_blocks, frames), f32)
    cached, rows, columns, partial = called(
        first_kernel,
        [
            pltpu.VMEM((slots, frames, frames), f32),
            pltpu.VMEM((source_blocks, frames, features), bf16),
            pltpu.VMEM((target_blocks, features, frames), bf16),
            many,
        ],
        [
            pltpu.VMEM((source_blocks, features, frames), f32),
            pltpu.VMEM((target_blocks, features, frames), f32),
            flat, square, square, flat,
        ],
        count, pairs, source, target, target_start,
    )
    kept = [count, pairs]
    kept += [pltpu.with_memory_space_constraint(x, pltpu.VMEM) for x in (cached, rows, columns)]
    for iteration in range(ITERS):
        scaling, partial = called(
            column_kernel,
            [line, line],
            [square, pltpu.VMEM((target_blocks, 8, frames), f32), square, square, flat],
            *kept, exchanged(partial, "tgt"), source_mass,
        )
        both = lax.all_gather(partial, "c")
        merged = log_sum_exp([both[0], both[1]])
        gathered = exchanged(copies(merged, "z"), "z")
        if iteration < ITERS - 1:
            (partial,) = called(
                row_kernel,
                [many],
                [flat, flat, square, square, flat],
                *kept, gathered, target_mass,
            )
    potential = target_mass - log_sum_exp([gathered[k] for k in range(gathered.shape[0])])
    return scaling, potential


def solution(mesh):
    split = Mesh(mesh.devices.reshape(16, 2, mesh.shape["tgt"]), ("z", "c", "tgt"))
    placed = (
        P(SRC, None, "tgt"),
        P("tgt", None, SRC),
        P(SRC, None),
        P("tgt", None),
        P("tgt", None),
        P(SRC, "tgt", None, None),
        P(SRC, "tgt"),
    )
    return jax.shard_map(
        on_device,
        mesh=split,
        in_specs=placed,
        out_specs=(P(SRC, None), P("tgt", None)),
        check_vma=False,
    )
```

```python
import functools
import math

import jax
import jax.numpy as jnp
from jax import lax
from jax.experimental import pallas as pl
from jax.experimental.pallas import tpu as pltpu
from jax.sharding import Mesh
from jax.sharding import PartitionSpec as P

ITERS = 2
SRC = ("z", "c")

smoothing_epsilon = 4.0
empty_peak = -1e30
log2e = 1.0 / math.log(2.0)
to_log2 = log2e / smoothing_epsilon
group = 16
light_group = 8
pot_most = 20.0
sum_least = 4.3e-18
sum_most = 5e34


def log_sum_exp(pieces):
    peak = functools.reduce(jnp.maximum, pieces)
    total = functools.reduce(jnp.add, [jnp.exp(piece - peak) for piece in pieces])
    return peak + jnp.log(total)


def scores(rows, columns):
    return lax.dot_general(
        rows, columns, (((1,), (0,)), ((), ())), preferred_element_type=jnp.float32
    )


def over_slots(count, size, body):
    whole = count // size

    @pl.loop(0, whole)
    def _(step):
        for lane in range(size):
            body(step * size + lane, None)

    @pl.when(whole * size < count)
    def _():
        for lane in range(size):
            slot = whole * size + lane
            body(slot, slot < count)


def kept_only(value, live):
    return value if live is None else jnp.where(live, value, 0.0)


def within(potential, sums):
    fine = (
        (jnp.abs(potential) <= pot_most) & (sums >= sum_least) & (sums <= sum_most)
    )
    return jnp.min(jnp.where(fine, 1.0, 0.0)) > 0.5


def rows_kept(sums, row_of):
    for block in range(sums.shape[0]):
        sums[block : block + 1, :] = row_of(block)


def exact_rows(count, pairs, rows, columns, potential, peak, total, sums):
    peak[...] = jnp.full_like(peak, empty_peak)
    total[...] = jnp.zeros_like(total)

    @pl.loop(0, count)
    def _(slot):
        source, target = pairs[0, slot], pairs[1, slot]
        value = scores(rows[source], columns[target]) * to_log2
        value = value + potential[pl.ds(target, 1), :] * log2e
        raised = jnp.maximum(peak[source], value)
        total[source] = total[source] * jnp.exp2(peak[source] - raised) + jnp.exp2(
            value - raised
        )
        peak[source] = raised

    def one(block):
        tall, across = peak[block].T, total[block].T
        most = jnp.max(tall, axis=0, keepdims=True)
        summed = jnp.sum(across * jnp.exp2(tall - most), axis=0, keepdims=True)
        return most / log2e + jnp.log(summed)

    rows_kept(sums, one)


def exact_columns(count, pairs, rows, columns, potential, wide, peak, total, sums):
    peak[...] = jnp.full_like(peak, empty_peak)
    total[...] = jnp.zeros_like(total)
    for block in range(wide.shape[0]):
        wide[block] = jnp.broadcast_to(potential[block : block + 1, :], wide.shape[1:]).T

    @pl.loop(0, count)
    def _(slot):
        source, target = pairs[0, slot], pairs[1, slot]
        value = scores(rows[source], columns[target]) * to_log2
        value = value + wide[source] * log2e
        raised = jnp.maximum(peak[target], value)
        total[target] = total[target] * jnp.exp2(peak[target] - raised) + jnp.exp2(
            value - raised
        )
        peak[target] = raised

    def one(block):
        most = jnp.max(peak[block], axis=0, keepdims=True)
        summed = jnp.sum(total[block] * jnp.exp2(peak[block] - most), axis=0, keepdims=True)
        return most / log2e + jnp.log(summed)

    rows_kept(sums, one)


def spread(partial, sums):
    partial[...] = jnp.broadcast_to(sums[...][None], partial.shape)


def row_pass(size, count, pairs, rows, columns, potential, kernel_of, weights, total, peak, sums, partial):
    weights[...] = jnp.exp(potential[...])
    total[...] = jnp.zeros_like(total)

    def body(slot, live):
        source, target = pairs[0, slot], pairs[1, slot]
        value = kernel_of(slot, source, target) * weights[pl.ds(target, 1), :]
        total[source] = total[source] + kept_only(value, live)

    over_slots(count, size, body)
    rows_kept(sums, lambda block: jnp.sum(total[block].T, axis=0, keepdims=True))
    fine = within(potential[...], sums[...])

    @pl.when(fine)
    def _():
        sums[...] = jnp.log(sums[...])

    @pl.when(jnp.logical_not(fine))
    def _():
        exact_rows(count, pairs, rows, columns, potential, peak, total, sums)

    spread(partial, sums)


def first_kernel(
    count_ref, far_pairs, far_start, far_source_mass, far_target_mass, source, target,
    cached, rows, columns, near_pairs, source_mass, target_mass, partial,
    pairs, start, arrived, wide_source, wide_target, weights, total, peak, sums,
):
    moves = fetches(
        (far_pairs, far_start, far_pairs, far_source_mass, far_target_mass),
        (pairs, start, near_pairs, source_mass, target_mass),
        arrived,
    )
    blocks = source.shape[1]
    features = source.shape[2]
    for device in range(source.shape[0]):
        wide_source[:, pl.ds(device * features, features), :] = source[device].astype(
            jnp.float32
        )
    cores, rings, _, parts, _ = target.shape
    for ring in range(rings):
        for core in range(cores):
            at = (ring * cores + core) * parts
            wide_target[:, pl.ds(at, parts), :] = target[core, ring].astype(jnp.float32)
    for block in range(blocks):
        rows[block] = wide_source[block].T.astype(jnp.bfloat16)
        columns[block] = wide_target[block].astype(jnp.bfloat16)

    for move in moves[:2]:
        move.wait()

    def kernel_of(slot, source, target):
        value = jnp.exp2(scores(rows[source], columns[target]) * to_log2)
        cached[slot] = value
        return value

    row_pass(
        group, count_ref[0], pairs, rows, columns, start, kernel_of, weights, total, peak, sums, partial
    )
    for move in moves[2:]:
        move.wait()


def column_kernel(
    count_ref, near_pairs, mass, cached, rows, columns, gathered, scaling, partial,
    pairs, arrived, wide, slim, total, peak, sums,
):
    moves = fetches((near_pairs,), (pairs,), arrived)
    count = count_ref[0]
    reached = log_sum_exp([gathered[k] for k in range(gathered.shape[0])])
    for move in moves:
        move.wait()
    scaling[...] = mass[...] - reached
    weights = jnp.exp(scaling[...])
    for block in range(wide.shape[0]):
        wide[block] = jnp.broadcast_to(weights[block : block + 1, :], wide.shape[1:]).T
    slim[...] = jnp.zeros_like(slim)

    def body(slot, live):
        source, target = pairs[0, slot], pairs[1, slot]
        value = cached[slot] * wide[source]
        value = jnp.sum(value.reshape(-1, 8, value.shape[-1]), axis=0)
        slim[target] = slim[target] + kept_only(value, live)

    over_slots(count, light_group, body)
    rows_kept(sums, lambda block: jnp.sum(slim[block], axis=0, keepdims=True))
    fine = within(scaling[...], sums[...])

    @pl.when(fine)
    def _():
        sums[...] = jnp.log(sums[...])

    @pl.when(jnp.logical_not(fine))
    def _():
        exact_columns(count, pairs, rows, columns, scaling, wide, peak, total, sums)

    partial[...] = sums[...]


def row_kernel(
    count_ref, near_pairs, mass, cached, rows, columns, gathered, partial,
    pairs, arrived, potential, weights, total, peak, sums,
):
    moves = fetches((near_pairs,), (pairs,), arrived)
    reached = log_sum_exp([gathered[k] for k in range(gathered.shape[0])])
    for move in moves:
        move.wait()
    potential[...] = mass[...] - reached
    row_pass(
        light_group, count_ref[0], pairs, rows, columns, potential,
        lambda slot, source, target: cached[slot],
        weights, total, peak, sums, partial,
    )


def called(body, outs, scratch, *operands, far=0):
    smem = pl.BlockSpec(memory_space=pltpu.SMEM)
    vmem = pl.BlockSpec(memory_space=pltpu.VMEM)
    anywhere = pl.BlockSpec(memory_space=pl.ANY)
    count, *rest = operands
    spaces = [pltpu.HBM] * far + [pltpu.VMEM] * (len(rest) - far)
    held = [pltpu.with_memory_space_constraint(x, space) for x, space in zip(rest, spaces)]
    return pl.pallas_call(
        body,
        out_shape=outs,
        in_specs=[smem] + [anywhere] * far + [vmem] * (len(rest) - far),
        out_specs=[vmem] * len(outs),
        scratch_shapes=scratch,
        compiler_params=pltpu.CompilerParams(vmem_limit_bytes=40 * 1024 * 1024),
    )(count, *held)


def fetches(sources, places, arrived):
    moves = [
        pltpu.make_async_copy(source, place, arrived.at[k])
        for k, (source, place) in enumerate(zip(sources, places))
    ]
    for move in moves:
        move.start()
    return moves


def copies(x, axis):
    return jnp.broadcast_to(x[None], (lax.axis_size(axis), *x.shape))


def exchanged(x, axis):
    return lax.all_to_all(x, axis, 0, 0, tiled=True)


def local_chain(source, target, start, source_mass, target_mass, pairs, count, over_tgt, over_src):
    f32, bf16 = jnp.float32, jnp.bfloat16
    slots = pairs.shape[1]
    across, source_blocks, depth, frames = source.shape
    target_blocks = target.shape[2]
    features = across * depth
    line = jax.ShapeDtypeStruct((source_blocks, frames), f32)
    many = jax.ShapeDtypeStruct((across, source_blocks, frames), f32)
    square = pltpu.VMEM((source_blocks, frames, frames), f32)
    flat = pltpu.VMEM((source_blocks, frames), f32)
    copied = pltpu.VMEM(pairs.shape, jnp.int32)
    listed = pltpu.SMEM(pairs.shape, jnp.int32)
    arrivals = pltpu.SemaphoreType.DMA
    *kept, near_pairs, source_mass, target_mass, partial = called(
        first_kernel,
        [
            pltpu.VMEM((slots, frames, frames), f32),
            pltpu.VMEM((source_blocks, frames, features), bf16),
            pltpu.VMEM((target_blocks, features, frames), bf16),
            copied, flat, flat, many,
        ],
        [
            listed, flat, arrivals((5,)),
            pltpu.VMEM((source_blocks, features, frames), f32),
            pltpu.VMEM((target_blocks, features, frames), f32),
            flat, square, square, flat,
        ],
        count, pairs, start, source_mass, target_mass, source, target,
        far=4,
    )
    for iteration in range(ITERS):
        scaling, partial = called(
            column_kernel,
            [line, line],
            [
                listed, arrivals((1,)), square,
                pltpu.VMEM((target_blocks, 8, frames), f32), square, square, flat,
            ],
            count, near_pairs, source_mass, *kept, over_tgt(partial),
        )
        gathered = over_src(partial)
        if iteration < ITERS - 1:
            (partial,) = called(
                row_kernel,
                [many],
                [listed, arrivals((1,)), flat, flat, square, square, flat],
                count, near_pairs, target_mass, *kept, gathered,
            )
    potential = target_mass - log_sum_exp([gathered[k] for k in range(gathered.shape[0])])
    return scaling, potential


def over_src(partial):
    both = lax.all_gather(partial, "c")
    return exchanged(copies(log_sum_exp([both[0], both[1]]), "z"), "z")


def on_device(
    source_embed, target_embed, source_mass, target_mass, target_start, block_pairs, counts
):
    pairs = block_pairs.reshape(block_pairs.shape[2], 2).T
    columns = exchanged(copies(jnp.swapaxes(target_embed, 1, 2), "z"), "z")
    return local_chain(
        lax.all_gather(jnp.swapaxes(source_embed, 1, 2), "tgt"),
        lax.all_gather(columns, "c"),
        target_start, source_mass, target_mass, pairs, counts.reshape(1),
        lambda partial: exchanged(partial, "tgt"), over_src,
    )


def solution(mesh):
    split = Mesh(mesh.devices.reshape(16, 2, mesh.shape["tgt"]), ("z", "c", "tgt"))
    placed = (
        P(SRC, None, "tgt"),
        P("tgt", None, SRC),
        P(SRC, None),
        P("tgt", None),
        P("tgt", None),
        P(SRC, "tgt", None, None),
        P(SRC, "tgt"),
    )
    return jax.shard_map(
        on_device,
        mesh=split,
        in_specs=placed,
        out_specs=(P(SRC, None), P("tgt", None)),
        check_vma=False,
    )
```

```python
import functools
import math

import jax
import jax.numpy as jnp
from jax import lax
from jax.experimental import pallas as pl
from jax.experimental.pallas import tpu as pltpu
from jax.sharding import Mesh
from jax.sharding import PartitionSpec as P

ITERS = 2
SRC = ("z", "c")
TGT = ("y", "x")

smoothing_epsilon = 4.0
empty_peak = -1e30
log2e = 1.0 / math.log(2.0)
to_log2 = log2e / smoothing_epsilon
group = 16
light_group = 8
pot_most = 20.0
sum_least = 4.3e-18
sum_most = 5e34


def log_sum_exp(pieces):
    peak = functools.reduce(jnp.maximum, pieces)
    total = functools.reduce(jnp.add, [jnp.exp(piece - peak) for piece in pieces])
    return peak + jnp.log(total)


def scores(rows, columns):
    return lax.dot_general(
        rows, columns, (((1,), (0,)), ((), ())), preferred_element_type=jnp.float32
    )


def over_slots(count, size, body):
    whole = count // size

    @pl.loop(0, whole)
    def _(step):
        for lane in range(size):
            body(step * size + lane, None)

    @pl.when(whole * size < count)
    def _():
        for lane in range(size):
            slot = whole * size + lane
            body(slot, slot < count)


def kept_only(value, live):
    return value if live is None else jnp.where(live, value, 0.0)


def within(potential, sums):
    fine = (
        (jnp.abs(potential) <= pot_most) & (sums >= sum_least) & (sums <= sum_most)
    )
    return jnp.min(jnp.where(fine, 1.0, 0.0)) > 0.5


def rows_kept(sums, row_of):
    for block in range(sums.shape[0]):
        sums[block : block + 1, :] = row_of(block)


def exact_rows(count, pairs, rows, columns, potential, peak, total, sums):
    peak[...] = jnp.full_like(peak, empty_peak)
    total[...] = jnp.zeros_like(total)

    @pl.loop(0, count)
    def _(slot):
        source, target = pairs[0, slot], pairs[1, slot]
        value = scores(rows[source], columns[target]) * to_log2
        value = value + potential[pl.ds(target, 1), :] * log2e
        raised = jnp.maximum(peak[source], value)
        total[source] = total[source] * jnp.exp2(peak[source] - raised) + jnp.exp2(
            value - raised
        )
        peak[source] = raised

    def one(block):
        tall, across = peak[block].T, total[block].T
        most = jnp.max(tall, axis=0, keepdims=True)
        summed = jnp.sum(across * jnp.exp2(tall - most), axis=0, keepdims=True)
        return most / log2e + jnp.log(summed)

    rows_kept(sums, one)


def exact_columns(count, pairs, rows, columns, potential, wide, peak, total, sums):
    peak[...] = jnp.full_like(peak, empty_peak)
    total[...] = jnp.zeros_like(total)
    for block in range(wide.shape[0]):
        wide[block] = jnp.broadcast_to(potential[block : block + 1, :], wide.shape[1:]).T

    @pl.loop(0, count)
    def _(slot):
        source, target = pairs[0, slot], pairs[1, slot]
        value = scores(rows[source], columns[target]) * to_log2
        value = value + wide[source] * log2e
        raised = jnp.maximum(peak[target], value)
        total[target] = total[target] * jnp.exp2(peak[target] - raised) + jnp.exp2(
            value - raised
        )
        peak[target] = raised

    def one(block):
        most = jnp.max(peak[block], axis=0, keepdims=True)
        summed = jnp.sum(total[block] * jnp.exp2(peak[block] - most), axis=0, keepdims=True)
        return most / log2e + jnp.log(summed)

    rows_kept(sums, one)


def spread(partial, sums):
    partial[...] = jnp.broadcast_to(sums[...][None], partial.shape)


def row_pass(size, count, pairs, rows, columns, potential, kernel_of, weights, total, peak, sums, partial):
    weights[...] = jnp.exp(potential[...])
    total[...] = jnp.zeros_like(total)

    def body(slot, live):
        source, target = pairs[0, slot], pairs[1, slot]
        value = kernel_of(slot, source, target) * weights[pl.ds(target, 1), :]
        total[source] = total[source] + kept_only(value, live)

    over_slots(count, size, body)
    rows_kept(sums, lambda block: jnp.sum(total[block].T, axis=0, keepdims=True))
    fine = within(potential[...], sums[...])

    @pl.when(fine)
    def _():
        sums[...] = jnp.log(sums[...])

    @pl.when(jnp.logical_not(fine))
    def _():
        exact_rows(count, pairs, rows, columns, potential, peak, total, sums)

    spread(partial, sums)


def first_kernel(
    count_ref, far_pairs, far_start, far_source_mass, far_target_mass, source, target,
    cached, rows, columns, near_pairs, source_mass, target_mass, partial,
    pairs, start, arrived, wide_source, wide_target, weights, total, peak, sums,
):
    moves = fetches(
        (far_pairs, far_start, far_pairs, far_source_mass, far_target_mass),
        (pairs, start, near_pairs, source_mass, target_mass),
        arrived,
    )
    blocks = source.shape[1]
    features = source.shape[2]
    for device in range(source.shape[0]):
        wide_source[:, pl.ds(device * features, features), :] = source[device].astype(
            jnp.float32
        )
    cores, rings, _, parts, _ = target.shape
    for ring in range(rings):
        for core in range(cores):
            at = (ring * cores + core) * parts
            wide_target[:, pl.ds(at, parts), :] = target[core, ring].astype(jnp.float32)
    for block in range(blocks):
        rows[block] = wide_source[block].T.astype(jnp.bfloat16)
        columns[block] = wide_target[block].astype(jnp.bfloat16)

    for move in moves[:2]:
        move.wait()

    def kernel_of(slot, source, target):
        value = jnp.exp2(scores(rows[source], columns[target]) * to_log2)
        cached[slot] = value
        return value

    row_pass(
        group, count_ref[0], pairs, rows, columns, start, kernel_of, weights, total, peak, sums, partial
    )
    for move in moves[2:]:
        move.wait()


def column_kernel(
    count_ref, near_pairs, mass, cached, rows, columns, gathered, scaling, partial,
    pairs, arrived, wide, slim, total, peak, sums,
):
    moves = fetches((near_pairs,), (pairs,), arrived)
    count = count_ref[0]
    reached = log_sum_exp([gathered[k] for k in range(gathered.shape[0])])
    for move in moves:
        move.wait()
    scaling[...] = mass[...] - reached
    weights = jnp.exp(scaling[...])
    for block in range(wide.shape[0]):
        wide[block] = jnp.broadcast_to(weights[block : block + 1, :], wide.shape[1:]).T
    slim[...] = jnp.zeros_like(slim)

    def body(slot, live):
        source, target = pairs[0, slot], pairs[1, slot]
        value = cached[slot] * wide[source]
        value = jnp.sum(value.reshape(-1, 8, value.shape[-1]), axis=0)
        slim[target] = slim[target] + kept_only(value, live)

    over_slots(count, light_group, body)
    rows_kept(sums, lambda block: jnp.sum(slim[block], axis=0, keepdims=True))
    fine = within(scaling[...], sums[...])

    @pl.when(fine)
    def _():
        sums[...] = jnp.log(sums[...])

    @pl.when(jnp.logical_not(fine))
    def _():
        exact_columns(count, pairs, rows, columns, scaling, wide, peak, total, sums)

    partial[...] = sums[...]


def row_kernel(
    count_ref, near_pairs, mass, cached, rows, columns, gathered, partial,
    pairs, arrived, potential, weights, total, peak, sums,
):
    moves = fetches((near_pairs,), (pairs,), arrived)
    reached = log_sum_exp([gathered[k] for k in range(gathered.shape[0])])
    for move in moves:
        move.wait()
    potential[...] = mass[...] - reached
    row_pass(
        light_group, count_ref[0], pairs, rows, columns, potential,
        lambda slot, source, target: cached[slot],
        weights, total, peak, sums, partial,
    )


def called(body, outs, scratch, *operands, far=0):
    smem = pl.BlockSpec(memory_space=pltpu.SMEM)
    vmem = pl.BlockSpec(memory_space=pltpu.VMEM)
    anywhere = pl.BlockSpec(memory_space=pl.ANY)
    count, *rest = operands
    spaces = [pltpu.HBM] * far + [pltpu.VMEM] * (len(rest) - far)
    held = [pltpu.with_memory_space_constraint(x, space) for x, space in zip(rest, spaces)]
    return pl.pallas_call(
        body,
        out_shape=outs,
        in_specs=[smem] + [anywhere] * far + [vmem] * (len(rest) - far),
        out_specs=[vmem] * len(outs),
        scratch_shapes=scratch,
        compiler_params=pltpu.CompilerParams(vmem_limit_bytes=40 * 1024 * 1024),
    )(count, *held)


def fetches(sources, places, arrived):
    moves = [
        pltpu.make_async_copy(source, place, arrived.at[k])
        for k, (source, place) in enumerate(zip(sources, places))
    ]
    for move in moves:
        move.start()
    return moves


def copies(x, axis):
    return jnp.broadcast_to(x[None], (lax.axis_size(axis), *x.shape))


def exchanged(x, axis):
    return lax.all_to_all(x, axis, 0, 0, tiled=True)


def local_chain(source, target, start, source_mass, target_mass, pairs, count, over_tgt, over_src):
    f32, bf16 = jnp.float32, jnp.bfloat16
    slots = pairs.shape[1]
    across, source_blocks, depth, frames = source.shape
    target_blocks = target.shape[2]
    features = across * depth
    line = jax.ShapeDtypeStruct((source_blocks, frames), f32)
    many = jax.ShapeDtypeStruct((across, source_blocks, frames), f32)
    square = pltpu.VMEM((source_blocks, frames, frames), f32)
    flat = pltpu.VMEM((source_blocks, frames), f32)
    copied = pltpu.VMEM(pairs.shape, jnp.int32)
    listed = pltpu.SMEM(pairs.shape, jnp.int32)
    arrivals = pltpu.SemaphoreType.DMA
    *kept, near_pairs, source_mass, target_mass, partial = called(
        first_kernel,
        [
            pltpu.VMEM((slots, frames, frames), f32),
            pltpu.VMEM((source_blocks, frames, features), bf16),
            pltpu.VMEM((target_blocks, features, frames), bf16),
            copied, flat, flat, many,
        ],
        [
            listed, flat, arrivals((5,)),
            pltpu.VMEM((source_blocks, features, frames), f32),
            pltpu.VMEM((target_blocks, features, frames), f32),
            flat, square, square, flat,
        ],
        count, pairs, start, source_mass, target_mass, source, target,
        far=4,
    )
    for iteration in range(ITERS):
        scaling, partial = called(
            column_kernel,
            [line, line],
            [
                listed, arrivals((1,)), square,
                pltpu.VMEM((target_blocks, 8, frames), f32), square, square, flat,
            ],
            count, near_pairs, source_mass, *kept, over_tgt(partial),
        )
        gathered = over_src(partial)
        if iteration < ITERS - 1:
            (partial,) = called(
                row_kernel,
                [many],
                [listed, arrivals((1,)), flat, flat, square, square, flat],
                count, near_pairs, target_mass, *kept, gathered,
            )
    potential = target_mass - log_sum_exp([gathered[k] for k in range(gathered.shape[0])])
    return scaling, potential


def over_src(partial):
    both = lax.all_gather(partial, "c")
    return exchanged(copies(log_sum_exp([both[0], both[1]]), "z"), "z")


def on_device(
    source_embed, target_embed, source_mass, target_mass, target_start, block_pairs, counts
):
    pairs = block_pairs.reshape(block_pairs.shape[2], 2).T
    source = exchanged(copies(jnp.swapaxes(source_embed, 1, 2), "x"), "x")
    source = lax.all_gather(source, "y", tiled=True)
    columns = exchanged(copies(jnp.swapaxes(target_embed, 1, 2), "z"), "z")
    return local_chain(
        source,
        lax.all_gather(columns, "c"),
        target_start, source_mass, target_mass, pairs, counts.reshape(1),
        lambda partial: exchanged(partial, TGT), over_src,
    )


def solution(mesh):
    split = Mesh(mesh.devices.reshape(16, 2, 4, 4), (*SRC, *TGT))
    placed = (
        P(SRC, None, TGT),
        P(TGT, None, SRC),
        P(SRC, None),
        P(TGT, None),
        P(TGT, None),
        P(SRC, TGT, None, None),
        P(SRC, TGT),
    )
    return jax.shard_map(
        on_device,
        mesh=split,
        in_specs=placed,
        out_specs=(P(SRC, None), P(TGT, None)),
        check_vma=False,
    )
```

```python
import functools
import math

import jax
import jax.numpy as jnp
from jax import lax
from jax.experimental import pallas as pl
from jax.experimental.pallas import tpu as pltpu
from jax.sharding import Mesh
from jax.sharding import PartitionSpec as P

ITERS = 2
SRC = ("z", "c")

smoothing_epsilon = 4.0
empty_peak = -1e30
log2e = 1.0 / math.log(2.0)
to_log2 = log2e / smoothing_epsilon
group = 16
light_group = 8
pot_most = 20.0
sum_least = 4.3e-18
sum_most = 5e34


def log_sum_exp(pieces):
    peak = functools.reduce(jnp.maximum, pieces)
    total = functools.reduce(jnp.add, [jnp.exp(piece - peak) for piece in pieces])
    return peak + jnp.log(total)


def scores(rows, columns):
    return lax.dot_general(
        rows, columns, (((1,), (0,)), ((), ())), preferred_element_type=jnp.float32
    )


def over_slots(count, size, body):
    whole = count // size

    @pl.loop(0, whole)
    def _(step):
        for lane in range(size):
            body(step * size + lane, None)

    @pl.when(whole * size < count)
    def _():
        for lane in range(size):
            slot = whole * size + lane
            body(slot, slot < count)


def kept_only(value, live):
    return value if live is None else jnp.where(live, value, 0.0)


def within(potential, sums):
    fine = (
        (jnp.abs(potential) <= pot_most) & (sums >= sum_least) & (sums <= sum_most)
    )
    return jnp.min(jnp.where(fine, 1.0, 0.0)) > 0.5


def rows_kept(sums, row_of):
    for block in range(sums.shape[0]):
        sums[block : block + 1, :] = row_of(block)


def exact_rows(count, pairs, rows, columns, potential, peak, total, sums):
    peak[...] = jnp.full_like(peak, empty_peak)
    total[...] = jnp.zeros_like(total)

    @pl.loop(0, count)
    def _(slot):
        source, target = pairs[0, slot], pairs[1, slot]
        value = scores(rows[source], columns[target]) * to_log2
        value = value + potential[pl.ds(target, 1), :] * log2e
        raised = jnp.maximum(peak[source], value)
        total[source] = total[source] * jnp.exp2(peak[source] - raised) + jnp.exp2(
            value - raised
        )
        peak[source] = raised

    def one(block):
        tall, across = peak[block].T, total[block].T
        most = jnp.max(tall, axis=0, keepdims=True)
        summed = jnp.sum(across * jnp.exp2(tall - most), axis=0, keepdims=True)
        return most / log2e + jnp.log(summed)

    rows_kept(sums, one)


def exact_columns(count, pairs, rows, columns, potential, wide, peak, total, sums):
    peak[...] = jnp.full_like(peak, empty_peak)
    total[...] = jnp.zeros_like(total)
    for block in range(wide.shape[0]):
        wide[block] = jnp.broadcast_to(potential[block : block + 1, :], wide.shape[1:]).T

    @pl.loop(0, count)
    def _(slot):
        source, target = pairs[0, slot], pairs[1, slot]
        value = scores(rows[source], columns[target]) * to_log2
        value = value + wide[source] * log2e
        raised = jnp.maximum(peak[target], value)
        total[target] = total[target] * jnp.exp2(peak[target] - raised) + jnp.exp2(
            value - raised
        )
        peak[target] = raised

    def one(block):
        most = jnp.max(peak[block], axis=0, keepdims=True)
        summed = jnp.sum(total[block] * jnp.exp2(peak[block] - most), axis=0, keepdims=True)
        return most / log2e + jnp.log(summed)

    rows_kept(sums, one)


def spread(partial, sums):
    partial[...] = jnp.broadcast_to(sums[...][None], partial.shape)


def row_pass(size, count, pairs, rows, columns, potential, kernel_of, weights, total, peak, sums, partial):
    weights[...] = jnp.exp(potential[...])
    total[...] = jnp.zeros_like(total)

    def body(slot, live):
        source, target = pairs[0, slot], pairs[1, slot]
        value = kernel_of(slot, source, target) * weights[pl.ds(target, 1), :]
        total[source] = total[source] + kept_only(value, live)

    over_slots(count, size, body)
    rows_kept(sums, lambda block: jnp.sum(total[block].T, axis=0, keepdims=True))
    fine = within(potential[...], sums[...])

    @pl.when(fine)
    def _():
        sums[...] = jnp.log(sums[...])

    @pl.when(jnp.logical_not(fine))
    def _():
        exact_rows(count, pairs, rows, columns, potential, peak, total, sums)

    spread(partial, sums)


def first_kernel(
    count_ref, far_pairs, far_start, far_source_mass, far_target_mass, source, target,
    cached, rows, columns, pairs, source_mass, target_mass, partial,
    start, arrived, wide_source, wide_target, weights, total, peak, sums,
):
    moves = fetches(
        (far_pairs, far_start, far_source_mass, far_target_mass),
        (pairs, start, source_mass, target_mass),
        arrived,
    )
    blocks = source.shape[1]
    features = source.shape[2]
    for device in range(source.shape[0]):
        wide_source[:, pl.ds(device * features, features), :] = source[device].astype(
            jnp.float32
        )
    cores, rings, _, parts, _ = target.shape
    for ring in range(rings):
        for core in range(cores):
            at = (ring * cores + core) * parts
            wide_target[:, pl.ds(at, parts), :] = target[core, ring].astype(jnp.float32)
    for block in range(blocks):
        rows[block] = wide_source[block].T.astype(jnp.bfloat16)
        columns[block] = wide_target[block].astype(jnp.bfloat16)

    for move in moves[:2]:
        move.wait()

    def kernel_of(slot, source, target):
        value = jnp.exp2(scores(rows[source], columns[target]) * to_log2)
        cached[slot] = value
        return value

    row_pass(
        group, count_ref[0], pairs, rows, columns, start, kernel_of, weights, total, peak, sums, partial
    )
    for move in moves[2:]:
        move.wait()


def column_kernel(
    count_ref, pairs, mass, cached, rows, columns, gathered, partial, scaling,
    wide, slim, total, peak, sums,
):
    count = count_ref[0]
    reached = log_sum_exp([gathered[k] for k in range(gathered.shape[0])])
    scaling[...] = mass[...] - reached
    weights = jnp.exp(scaling[...])
    for block in range(wide.shape[0]):
        wide[block] = jnp.broadcast_to(weights[block : block + 1, :], wide.shape[1:]).T
    slim[...] = jnp.zeros_like(slim)

    def body(slot, live):
        source, target = pairs[0, slot], pairs[1, slot]
        value = cached[slot] * wide[source]
        value = jnp.sum(value.reshape(-1, 8, value.shape[-1]), axis=0)
        slim[target] = slim[target] + kept_only(value, live)

    over_slots(count, light_group, body)
    rows_kept(sums, lambda block: jnp.sum(slim[block], axis=0, keepdims=True))
    fine = within(scaling[...], sums[...])

    @pl.when(fine)
    def _():
        sums[...] = jnp.log(sums[...])

    @pl.when(jnp.logical_not(fine))
    def _():
        exact_columns(count, pairs, rows, columns, scaling, wide, peak, total, sums)

    partial[...] = sums[...]


def row_kernel(
    count_ref, pairs, mass, cached, rows, columns, gathered, partial,
    potential, weights, total, peak, sums,
):
    reached = log_sum_exp([gathered[k] for k in range(gathered.shape[0])])
    potential[...] = mass[...] - reached
    row_pass(
        light_group, count_ref[0], pairs, rows, columns, potential,
        lambda slot, source, target: cached[slot],
        weights, total, peak, sums, partial,
    )


def called(body, outs, scratch, *operands, far=0):
    count, *rest = operands
    places = [
        pltpu.HBM if k < far else pltpu.SMEM if jnp.issubdtype(x.dtype, jnp.integer) else pltpu.VMEM
        for k, x in enumerate(rest)
    ]
    held = [pltpu.with_memory_space_constraint(x, place) for x, place in zip(rest, places)]
    given = [
        pltpu.SMEM if jnp.issubdtype(x.dtype, jnp.integer) else pltpu.VMEM for x in outs
    ]
    return pl.pallas_call(
        body,
        out_shape=outs,
        in_specs=[pl.BlockSpec(memory_space=pltpu.SMEM)]
        + [pl.BlockSpec(memory_space=pl.ANY if x is pltpu.HBM else x) for x in places],
        out_specs=[pl.BlockSpec(memory_space=x) for x in given],
        scratch_shapes=scratch,
        compiler_params=pltpu.CompilerParams(vmem_limit_bytes=40 * 1024 * 1024),
    )(count, *held)


def fetches(sources, places, arrived):
    moves = [
        pltpu.make_async_copy(source, place, arrived.at[k])
        for k, (source, place) in enumerate(zip(sources, places))
    ]
    for move in moves:
        move.start()
    return moves


def copies(x, axis):
    return jnp.broadcast_to(x[None], (lax.axis_size(axis), *x.shape))


def exchanged(x, axis):
    return lax.all_to_all(x, axis, 0, 0, tiled=True)


def local_chain(source, target, start, source_mass, target_mass, pairs, count, over_tgt, over_src):
    f32, bf16 = jnp.float32, jnp.bfloat16
    slots = pairs.shape[1]
    across, source_blocks, depth, frames = source.shape
    target_blocks = target.shape[2]
    features = across * depth
    many = jax.ShapeDtypeStruct((across, source_blocks, frames), f32)
    square = pltpu.VMEM((source_blocks, frames, frames), f32)
    flat = pltpu.VMEM((source_blocks, frames), f32)
    listed = pltpu.SMEM(pairs.shape, jnp.int32)
    arrivals = pltpu.SemaphoreType.DMA
    *kept, pairs, source_mass, target_mass, partial = called(
        first_kernel,
        [
            pltpu.VMEM((slots, frames, frames), f32),
            pltpu.VMEM((source_blocks, frames, features), bf16),
            pltpu.VMEM((target_blocks, features, frames), bf16),
            listed, flat, flat, many,
        ],
        [
            flat, arrivals((4,)),
            pltpu.VMEM((source_blocks, features, frames), f32),
            pltpu.VMEM((target_blocks, features, frames), f32),
            flat, square, square, flat,
        ],
        count, pairs, start, source_mass, target_mass, source, target,
        far=4,
    )
    for iteration in range(ITERS):
        last = iteration == ITERS - 1
        results = called(
            column_kernel,
            [flat, flat] if last else [flat],
            [flat][last:]
            + [square, pltpu.VMEM((target_blocks, 8, frames), f32), square, square, flat],
            count, pairs, source_mass, *kept, over_tgt(partial),
        )
        partial, scaling = results[0], results[-1]
        gathered = over_src(partial)
        if not last:
            (partial,) = called(
                row_kernel,
                [many],
                [flat, flat, square, square, flat],
                count, pairs, target_mass, *kept, gathered,
            )
    potential = target_mass - log_sum_exp([gathered[k] for k in range(gathered.shape[0])])
    return scaling, potential


def over_src(partial):
    both = lax.all_gather(partial, "c")
    return exchanged(copies(log_sum_exp([both[0], both[1]]), "z"), "z")


def on_device(
    source_embed, target_embed, source_mass, target_mass, target_start, block_pairs, counts
):
    pairs = block_pairs.reshape(block_pairs.shape[2], 2).T
    columns = exchanged(copies(jnp.swapaxes(target_embed, 1, 2), "z"), "z")
    return local_chain(
        lax.all_gather(jnp.swapaxes(source_embed, 1, 2), "tgt"),
        lax.all_gather(columns, "c"),
        target_start, source_mass, target_mass, pairs, counts.reshape(1),
        lambda partial: exchanged(partial, "tgt"), over_src,
    )


def solution(mesh):
    split = Mesh(mesh.devices.reshape(16, 2, mesh.shape["tgt"]), ("z", "c", "tgt"))
    placed = (
        P(SRC, None, "tgt"),
        P("tgt", None, SRC),
        P(SRC, None),
        P("tgt", None),
        P("tgt", None),
        P(SRC, "tgt", None, None),
        P(SRC, "tgt"),
    )
    return jax.shard_map(
        on_device,
        mesh=split,
        in_specs=placed,
        out_specs=(P(SRC, None), P("tgt", None)),
        check_vma=False,
    )
```

```python
import functools
import math

import jax
import jax.numpy as jnp
from jax import lax
from jax.experimental import pallas as pl
from jax.experimental.pallas import tpu as pltpu
from jax.sharding import Mesh
from jax.sharding import PartitionSpec as P

ITERS = 2
SRC = ("z", "c")
TGT = ("y", "x")

smoothing_epsilon = 4.0
empty_peak = -1e30
log2e = 1.0 / math.log(2.0)
to_log2 = log2e / smoothing_epsilon
group = 16
light_group = 8
pot_most = 20.0
sum_least = 4.3e-18
sum_most = 5e34


def log_sum_exp(pieces):
    peak = functools.reduce(jnp.maximum, pieces)
    total = functools.reduce(jnp.add, [jnp.exp(piece - peak) for piece in pieces])
    return peak + jnp.log(total)


def scores(rows, columns):
    return lax.dot_general(
        rows, columns, (((1,), (0,)), ((), ())), preferred_element_type=jnp.float32
    )


def over_slots(count, size, body):
    whole = count // size

    @pl.loop(0, whole)
    def _(step):
        for lane in range(size):
            body(step * size + lane, None)

    @pl.when(whole * size < count)
    def _():
        for lane in range(size):
            slot = whole * size + lane
            body(slot, slot < count)


def kept_only(value, live):
    return value if live is None else jnp.where(live, value, 0.0)


def within(potential, sums):
    fine = (
        (jnp.abs(potential) <= pot_most) & (sums >= sum_least) & (sums <= sum_most)
    )
    return jnp.min(jnp.where(fine, 1.0, 0.0)) > 0.5


def rows_kept(sums, row_of):
    for block in range(sums.shape[0]):
        sums[block : block + 1, :] = row_of(block)


def exact_rows(count, pairs, rows, columns, potential, peak, total, sums):
    peak[...] = jnp.full_like(peak, empty_peak)
    total[...] = jnp.zeros_like(total)

    @pl.loop(0, count)
    def _(slot):
        source, target = pairs[0, slot], pairs[1, slot]
        value = scores(rows[source], columns[target]) * to_log2
        value = value + potential[pl.ds(target, 1), :] * log2e
        raised = jnp.maximum(peak[source], value)
        total[source] = total[source] * jnp.exp2(peak[source] - raised) + jnp.exp2(
            value - raised
        )
        peak[source] = raised

    def one(block):
        tall, across = peak[block].T, total[block].T
        most = jnp.max(tall, axis=0, keepdims=True)
        summed = jnp.sum(across * jnp.exp2(tall - most), axis=0, keepdims=True)
        return most / log2e + jnp.log(summed)

    rows_kept(sums, one)


def exact_columns(count, pairs, rows, columns, potential, wide, peak, total, sums):
    peak[...] = jnp.full_like(peak, empty_peak)
    total[...] = jnp.zeros_like(total)
    for block in range(wide.shape[0]):
        wide[block] = jnp.broadcast_to(potential[block : block + 1, :], wide.shape[1:]).T

    @pl.loop(0, count)
    def _(slot):
        source, target = pairs[0, slot], pairs[1, slot]
        value = scores(rows[source], columns[target]) * to_log2
        value = value + wide[source] * log2e
        raised = jnp.maximum(peak[target], value)
        total[target] = total[target] * jnp.exp2(peak[target] - raised) + jnp.exp2(
            value - raised
        )
        peak[target] = raised

    def one(block):
        most = jnp.max(peak[block], axis=0, keepdims=True)
        summed = jnp.sum(total[block] * jnp.exp2(peak[block] - most), axis=0, keepdims=True)
        return most / log2e + jnp.log(summed)

    rows_kept(sums, one)


def spread(partial, sums):
    partial[...] = jnp.broadcast_to(sums[...][None], partial.shape)


def row_pass(size, count, pairs, rows, columns, potential, kernel_of, weights, total, peak, sums, partial):
    weights[...] = jnp.exp(potential[...])
    total[...] = jnp.zeros_like(total)

    def body(slot, live):
        source, target = pairs[0, slot], pairs[1, slot]
        value = kernel_of(slot, source, target) * weights[pl.ds(target, 1), :]
        total[source] = total[source] + kept_only(value, live)

    over_slots(count, size, body)
    rows_kept(sums, lambda block: jnp.sum(total[block].T, axis=0, keepdims=True))
    fine = within(potential[...], sums[...])

    @pl.when(fine)
    def _():
        sums[...] = jnp.log(sums[...])

    @pl.when(jnp.logical_not(fine))
    def _():
        exact_rows(count, pairs, rows, columns, potential, peak, total, sums)

    spread(partial, sums)


def first_kernel(
    count_ref, far_pairs, far_start, far_source_mass, far_target_mass, source, target,
    cached, rows, columns, pairs, source_mass, target_mass, partial,
    start, arrived, wide_source, wide_target, weights, total, peak, sums,
):
    moves = fetches(
        (far_pairs, far_start, far_source_mass, far_target_mass),
        (pairs, start, source_mass, target_mass),
        arrived,
    )
    blocks = source.shape[1]
    features = source.shape[2]
    for device in range(source.shape[0]):
        wide_source[:, pl.ds(device * features, features), :] = source[device].astype(
            jnp.float32
        )
    cores, rings, lines, frames = target.shape
    parts = lines // blocks
    for ring in range(rings):
        for core in range(cores):
            at = (ring * cores + core) * parts
            piece = target[core, ring].astype(jnp.float32)
            wide_target[:, pl.ds(at, parts), :] = piece.reshape(blocks, parts, frames)
    for block in range(blocks):
        rows[block] = wide_source[block].T.astype(jnp.bfloat16)
        columns[block] = wide_target[block].astype(jnp.bfloat16)

    for move in moves[:2]:
        move.wait()

    def kernel_of(slot, source, target):
        value = jnp.exp2(scores(rows[source], columns[target]) * to_log2)
        cached[slot] = value
        return value

    row_pass(
        group, count_ref[0], pairs, rows, columns, start, kernel_of, weights, total, peak, sums, partial
    )
    for move in moves[2:]:
        move.wait()


def column_kernel(
    count_ref, pairs, mass, cached, rows, columns, gathered, partial, *refs,
):
    *result, scaling, wide, slim, total, peak, sums, arrived = refs
    count = count_ref[0]
    reached = log_sum_exp([gathered[k] for k in range(gathered.shape[0])])
    scaling[...] = mass[...] - reached
    moves = fetches([scaling] * len(result), result, arrived)
    weights = jnp.exp(scaling[...])
    for block in range(wide.shape[0]):
        wide[block] = jnp.broadcast_to(weights[block : block + 1, :], wide.shape[1:]).T
    slim[...] = jnp.zeros_like(slim)

    def body(slot, live):
        source, target = pairs[0, slot], pairs[1, slot]
        value = cached[slot] * wide[source]
        value = jnp.sum(value.reshape(-1, 8, value.shape[-1]), axis=0)
        slim[target] = slim[target] + kept_only(value, live)

    over_slots(count, light_group, body)
    rows_kept(sums, lambda block: jnp.sum(slim[block], axis=0, keepdims=True))
    fine = within(scaling[...], sums[...])

    @pl.when(fine)
    def _():
        sums[...] = jnp.log(sums[...])

    @pl.when(jnp.logical_not(fine))
    def _():
        exact_columns(count, pairs, rows, columns, scaling, wide, peak, total, sums)

    partial[...] = sums[...]
    for move in moves:
        move.wait()


def row_kernel(
    count_ref, pairs, mass, cached, rows, columns, gathered, partial,
    potential, weights, total, peak, sums,
):
    reached = log_sum_exp([gathered[k] for k in range(gathered.shape[0])])
    potential[...] = mass[...] - reached
    row_pass(
        light_group, count_ref[0], pairs, rows, columns, potential,
        lambda slot, source, target: cached[slot],
        weights, total, peak, sums, partial,
    )


def spaces_of(out):
    space = getattr(out, "memory_space", pltpu.VMEM)
    return pl.ANY if space == pltpu.HBM else space


def called(body, outs, scratch, *operands, far=0):
    count, *rest = operands
    places = [
        pltpu.HBM if k < far else pltpu.SMEM if jnp.issubdtype(x.dtype, jnp.integer) else pltpu.VMEM
        for k, x in enumerate(rest)
    ]
    held = [pltpu.with_memory_space_constraint(x, place) for x, place in zip(rest, places)]
    return pl.pallas_call(
        body,
        out_shape=outs,
        in_specs=[pl.BlockSpec(memory_space=pltpu.SMEM)]
        + [pl.BlockSpec(memory_space=pl.ANY if x is pltpu.HBM else x) for x in places],
        out_specs=[pl.BlockSpec(memory_space=spaces_of(x)) for x in outs],
        scratch_shapes=scratch,
        compiler_params=pltpu.CompilerParams(vmem_limit_bytes=40 * 1024 * 1024),
    )(count, *held)


def fetches(sources, places, arrived):
    moves = [
        pltpu.make_async_copy(source, place, arrived.at[k])
        for k, (source, place) in enumerate(zip(sources, places))
    ]
    for move in moves:
        move.start()
    return moves


def copies(x, axis):
    return jnp.broadcast_to(x[None], (lax.axis_size(axis), *x.shape))


def exchanged(x, axis):
    return lax.all_to_all(x, axis, 0, 0, tiled=True)


def local_chain(source, target, start, source_mass, target_mass, pairs, count, over_tgt, over_src):
    f32, bf16 = jnp.float32, jnp.bfloat16
    slots = pairs.shape[1]
    across, source_blocks, depth, frames = source.shape
    features = across * depth
    target_blocks = target.shape[0] * target.shape[1] * target.shape[2] // features
    many = jax.ShapeDtypeStruct((across, source_blocks, frames), f32)
    square = pltpu.VMEM((source_blocks, frames, frames), f32)
    flat = pltpu.VMEM((source_blocks, frames), f32)
    listed = pltpu.SMEM(pairs.shape, jnp.int32)
    arrivals = pltpu.SemaphoreType.DMA
    *kept, pairs, source_mass, target_mass, partial = called(
        first_kernel,
        [
            pltpu.VMEM((slots, frames, frames), f32),
            pltpu.VMEM((source_blocks, frames, features), bf16),
            pltpu.VMEM((target_blocks, features, frames), bf16),
            listed, flat, flat, many,
        ],
        [
            flat, arrivals((4,)),
            pltpu.VMEM((source_blocks, features, frames), f32),
            pltpu.VMEM((target_blocks, features, frames), f32),
            flat, square, square, flat,
        ],
        count, pairs, start, source_mass, target_mass, source, target,
        far=4,
    )
    for iteration in range(ITERS):
        last = iteration == ITERS - 1
        results = called(
            column_kernel,
            [flat, pltpu.HBM((source_blocks, frames), f32)] if last else [flat],
            [
                flat, square, pltpu.VMEM((target_blocks, 8, frames), f32), square, square,
                flat, arrivals((1,)),
            ],
            count, pairs, source_mass, *kept, over_tgt(partial),
        )
        partial, scaling = results[0], results[-1]
        gathered = over_src(partial)
        if not last:
            (partial,) = called(
                row_kernel,
                [many],
                [flat, flat, square, square, flat],
                count, pairs, target_mass, *kept, gathered,
            )
    potential = target_mass - log_sum_exp([gathered[k] for k in range(gathered.shape[0])])
    return scaling, potential


def over_src(partial):
    both = lax.all_gather(partial, "c")
    return exchanged(copies(log_sum_exp([both[0], both[1]]), "z"), "z")


def copying_kernel(source, target, sources, targets, near, arrived):
    moves = fetches([source] * sources.shape[0] + [target], [*sources_of(sources), near], arrived)
    moves[-1].wait()
    flat = near[...].astype(jnp.float32).reshape(targets.shape[1:]).astype(targets.dtype)
    targets[...] = jnp.broadcast_to(flat[None], targets.shape)
    for move in moves[:-1]:
        move.wait()


def sources_of(ref):
    return [ref.at[k] for k in range(ref.shape[0])]


def copies_of_both(source, target):
    across, rings = lax.axis_size("x"), lax.axis_size("z")
    lines = target.shape[0] * target.shape[1]
    return pl.pallas_call(
        copying_kernel,
        out_shape=[
            jax.ShapeDtypeStruct((across, *source.shape), source.dtype),
            jax.ShapeDtypeStruct((rings, lines, target.shape[2]), target.dtype),
        ],
        in_specs=[pl.BlockSpec(memory_space=pl.ANY)] * 2,
        out_specs=[
            pl.BlockSpec(memory_space=pl.ANY),
            pl.BlockSpec(memory_space=pltpu.VMEM),
        ],
        scratch_shapes=[
            pltpu.VMEM(target.shape, target.dtype),
            pltpu.SemaphoreType.DMA((across + 1,)),
        ],
    )(*(pltpu.with_memory_space_constraint(one, pltpu.HBM) for one in (source, target)))


def on_device(
    source_embed, target_embed, source_mass, target_mass, target_start, block_pairs, counts
):
    pairs = block_pairs.reshape(block_pairs.shape[2], 2).T
    sources, targets = copies_of_both(
        jnp.swapaxes(source_embed, 1, 2), jnp.swapaxes(target_embed, 1, 2)
    )
    source = lax.all_gather(exchanged(sources, "x"), "y", tiled=True)
    target = lax.all_gather(exchanged(targets, "z"), "c")
    return local_chain(
        source, target, target_start, source_mass, target_mass, pairs, counts.reshape(1),
        lambda partial: exchanged(partial, TGT), over_src,
    )


def solution(mesh):
    split = Mesh(mesh.devices.reshape(16, 2, 4, 4), (*SRC, *TGT))
    placed = (
        P(SRC, None, TGT),
        P(TGT, None, SRC),
        P(SRC, None),
        P(TGT, None),
        P(TGT, None),
        P(SRC, TGT, None, None),
        P(SRC, TGT),
    )
    return jax.shard_map(
        on_device,
        mesh=split,
        in_specs=placed,
        out_specs=(P(SRC, None), P(TGT, None)),
        check_vma=False,
    )
```

```python
import functools
import math

import jax
import jax.numpy as jnp
from jax import lax
from jax.experimental import pallas as pl
from jax.experimental.pallas import tpu as pltpu
from jax.sharding import Mesh
from jax.sharding import PartitionSpec as P

ITERS = 2
SRC = ("z", "c")
TGT = ("y", "x")

smoothing_epsilon = 4.0
empty_peak = -1e30
log2e = 1.0 / math.log(2.0)
to_log2 = log2e / smoothing_epsilon
group = 16
light_group = 8
pot_most = 20.0
sum_least = 4.3e-18
sum_most = 5e34


def log_sum_exp(pieces):
    peak = functools.reduce(jnp.maximum, pieces)
    total = functools.reduce(jnp.add, [jnp.exp(piece - peak) for piece in pieces])
    return peak + jnp.log(total)


def scores(rows, columns):
    return lax.dot_general(
        rows, columns, (((1,), (0,)), ((), ())), preferred_element_type=jnp.float32
    )


def over_slots(count, size, body):
    whole = count // size

    @pl.loop(0, whole)
    def _(step):
        for lane in range(size):
            body(step * size + lane, None)

    @pl.when(whole * size < count)
    def _():
        for lane in range(size):
            slot = whole * size + lane
            body(slot, slot < count)


def kept_only(value, live):
    return value if live is None else jnp.where(live, value, 0.0)


def within(potential, sums):
    fine = (
        (jnp.abs(potential) <= pot_most) & (sums >= sum_least) & (sums <= sum_most)
    )
    return jnp.min(jnp.where(fine, 1.0, 0.0)) > 0.5


def rows_kept(sums, row_of):
    for block in range(sums.shape[0]):
        sums[block : block + 1, :] = row_of(block)


def exact_rows(count, pairs, rows, columns, potential, peak, total, sums):
    peak[...] = jnp.full_like(peak, empty_peak)
    total[...] = jnp.zeros_like(total)

    @pl.loop(0, count)
    def _(slot):
        source, target = pairs[0, slot], pairs[1, slot]
        value = scores(rows[source], columns[target]) * to_log2
        value = value + potential[pl.ds(target, 1), :] * log2e
        raised = jnp.maximum(peak[source], value)
        total[source] = total[source] * jnp.exp2(peak[source] - raised) + jnp.exp2(
            value - raised
        )
        peak[source] = raised

    def one(block):
        tall, across = peak[block].T, total[block].T
        most = jnp.max(tall, axis=0, keepdims=True)
        summed = jnp.sum(across * jnp.exp2(tall - most), axis=0, keepdims=True)
        return most / log2e + jnp.log(summed)

    rows_kept(sums, one)


def exact_columns(count, pairs, rows, columns, potential, wide, peak, total, sums):
    peak[...] = jnp.full_like(peak, empty_peak)
    total[...] = jnp.zeros_like(total)
    for block in range(wide.shape[0]):
        wide[block] = jnp.broadcast_to(potential[block : block + 1, :], wide.shape[1:]).T

    @pl.loop(0, count)
    def _(slot):
        source, target = pairs[0, slot], pairs[1, slot]
        value = scores(rows[source], columns[target]) * to_log2
        value = value + wide[source] * log2e
        raised = jnp.maximum(peak[target], value)
        total[target] = total[target] * jnp.exp2(peak[target] - raised) + jnp.exp2(
            value - raised
        )
        peak[target] = raised

    def one(block):
        most = jnp.max(peak[block], axis=0, keepdims=True)
        summed = jnp.sum(total[block] * jnp.exp2(peak[block] - most), axis=0, keepdims=True)
        return most / log2e + jnp.log(summed)

    rows_kept(sums, one)


def spread(partial, sums):
    partial[...] = jnp.broadcast_to(sums[...][None], partial.shape)


def row_pass(size, count, pairs, rows, columns, potential, kernel_of, weights, total, peak, sums, partial):
    weights[...] = jnp.exp(potential[...])
    total[...] = jnp.zeros_like(total)

    def body(slot, live):
        source, target = pairs[0, slot], pairs[1, slot]
        value = kernel_of(slot, source, target) * weights[pl.ds(target, 1), :]
        total[source] = total[source] + kept_only(value, live)

    over_slots(count, size, body)
    rows_kept(sums, lambda block: jnp.sum(total[block].T, axis=0, keepdims=True))
    fine = within(potential[...], sums[...])

    @pl.when(fine)
    def _():
        sums[...] = jnp.log(sums[...])

    @pl.when(jnp.logical_not(fine))
    def _():
        exact_rows(count, pairs, rows, columns, potential, peak, total, sums)

    spread(partial, sums)


def source_kernel(
    far_pairs, far_start, far_source_mass, far_target_mass, source,
    rows, pairs, start, source_mass, target_mass, wide, arrived,
):
    moves = fetches(
        (far_pairs, far_start, far_source_mass, far_target_mass),
        (pairs, start, source_mass, target_mass),
        arrived,
    )
    features = source.shape[2]
    for device in range(source.shape[0]):
        wide[:, pl.ds(device * features, features), :] = source[device].astype(jnp.float32)
    for block in range(source.shape[1]):
        rows[block] = wide[block].T.astype(rows.dtype)
    for move in moves:
        move.wait()


def first_kernel(
    count_ref, pairs, start, rows, target, cached, columns, partial,
    wide, weights, total, peak, sums,
):
    cores, rings, lines, frames = target.shape
    blocks = columns.shape[0]
    parts = lines // blocks
    for ring in range(rings):
        for core in range(cores):
            at = (ring * cores + core) * parts
            piece = target[core, ring].astype(jnp.float32)
            wide[:, pl.ds(at, parts), :] = piece.reshape(blocks, parts, frames)
    for block in range(blocks):
        columns[block] = wide[block].astype(columns.dtype)

    def kernel_of(slot, source, target):
        value = jnp.exp2(scores(rows[source], columns[target]) * to_log2)
        cached[slot] = value
        return value

    row_pass(
        group, count_ref[0], pairs, rows, columns, start, kernel_of,
        weights, total, peak, sums, partial,
    )


def column_kernel(
    count_ref, pairs, mass, cached, rows, columns, gathered, partial, *refs,
):
    *result, scaling, wide, slim, total, peak, sums, arrived = refs
    count = count_ref[0]
    reached = log_sum_exp([gathered[k] for k in range(gathered.shape[0])])
    scaling[...] = mass[...] - reached
    moves = fetches([scaling] * len(result), result, arrived)
    weights = jnp.exp(scaling[...])
    for block in range(wide.shape[0]):
        wide[block] = jnp.broadcast_to(weights[block : block + 1, :], wide.shape[1:]).T
    slim[...] = jnp.zeros_like(slim)

    def body(slot, live):
        source, target = pairs[0, slot], pairs[1, slot]
        value = cached[slot] * wide[source]
        value = jnp.sum(value.reshape(-1, 8, value.shape[-1]), axis=0)
        slim[target] = slim[target] + kept_only(value, live)

    over_slots(count, light_group, body)
    rows_kept(sums, lambda block: jnp.sum(slim[block], axis=0, keepdims=True))
    fine = within(scaling[...], sums[...])

    @pl.when(fine)
    def _():
        sums[...] = jnp.log(sums[...])

    @pl.when(jnp.logical_not(fine))
    def _():
        exact_columns(count, pairs, rows, columns, scaling, wide, peak, total, sums)

    partial[...] = sums[...]
    for move in moves:
        move.wait()


def row_kernel(
    count_ref, pairs, mass, cached, rows, columns, gathered, partial,
    potential, weights, total, peak, sums,
):
    reached = log_sum_exp([gathered[k] for k in range(gathered.shape[0])])
    potential[...] = mass[...] - reached
    row_pass(
        light_group, count_ref[0], pairs, rows, columns, potential,
        lambda slot, source, target: cached[slot],
        weights, total, peak, sums, partial,
    )


def spaces_of(out):
    space = getattr(out, "memory_space", pltpu.VMEM)
    return pl.ANY if space == pltpu.HBM else space


def called(body, outs, scratch, *operands, far=0):
    places = [
        pltpu.HBM if k < far else pltpu.SMEM if jnp.issubdtype(x.dtype, jnp.integer) else pltpu.VMEM
        for k, x in enumerate(operands)
    ]
    held = [
        x if x.size == 1 else pltpu.with_memory_space_constraint(x, place)
        for x, place in zip(operands, places)
    ]
    return pl.pallas_call(
        body,
        out_shape=outs,
        in_specs=[pl.BlockSpec(memory_space=pl.ANY if x is pltpu.HBM else x) for x in places],
        out_specs=[pl.BlockSpec(memory_space=spaces_of(x)) for x in outs],
        scratch_shapes=scratch,
        compiler_params=pltpu.CompilerParams(vmem_limit_bytes=40 * 1024 * 1024),
    )(*held)


def fetches(sources, places, arrived):
    moves = [
        pltpu.make_async_copy(source, place, arrived.at[k])
        for k, (source, place) in enumerate(zip(sources, places))
    ]
    for move in moves:
        move.start()
    return moves


def copies(x, axis):
    return jnp.broadcast_to(x[None], (lax.axis_size(axis), *x.shape))


def exchanged(x, axis):
    return lax.all_to_all(x, axis, 0, 0, tiled=True)


def local_chain(source, target, start, source_mass, target_mass, pairs, count, over_tgt, over_src):
    f32, bf16 = jnp.float32, jnp.bfloat16
    slots = pairs.shape[1]
    across, source_blocks, depth, frames = source.shape
    features = across * depth
    target_blocks = target.shape[0] * target.shape[1] * target.shape[2] // features
    many = jax.ShapeDtypeStruct((across, source_blocks, frames), f32)
    square = pltpu.VMEM((source_blocks, frames, frames), f32)
    flat = pltpu.VMEM((source_blocks, frames), f32)
    listed = pltpu.SMEM(pairs.shape, jnp.int32)
    arrivals = pltpu.SemaphoreType.DMA
    rows, pairs, start, source_mass, target_mass = called(
        source_kernel,
        [pltpu.VMEM((source_blocks, frames, features), bf16), listed, flat, flat, flat],
        [pltpu.VMEM((source_blocks, features, frames), f32), arrivals((4,))],
        pairs, start, source_mass, target_mass, source,
        far=4,
    )
    cached, columns, partial = called(
        first_kernel,
        [
            pltpu.VMEM((slots, frames, frames), f32),
            pltpu.VMEM((target_blocks, features, frames), bf16),
            many,
        ],
        [
            pltpu.VMEM((target_blocks, features, frames), f32),
            flat, square, square, flat,
        ],
        count, pairs, start, rows, target,
    )
    kept = [cached, rows, columns]
    for iteration in range(ITERS):
        last = iteration == ITERS - 1
        results = called(
            column_kernel,
            [flat, pltpu.HBM((source_blocks, frames), f32)] if last else [flat],
            [
                flat, square, pltpu.VMEM((target_blocks, 8, frames), f32), square, square,
                flat, arrivals((1,)),
            ],
            count, pairs, source_mass, *kept, over_tgt(partial),
        )
        partial, scaling = results[0], results[-1]
        gathered = over_src(partial)
        if not last:
            (partial,) = called(
                row_kernel,
                [many],
                [flat, flat, square, square, flat],
                count, pairs, target_mass, *kept, gathered,
            )
    potential = target_mass - log_sum_exp([gathered[k] for k in range(gathered.shape[0])])
    return scaling, potential


def over_src(partial):
    both = lax.all_gather(partial, "c")
    return exchanged(copies(log_sum_exp([both[0], both[1]]), "z"), "z")


def copying_kernel(source, target, sources, targets, near_source, near_target, arrived):
    moves = fetches((source, target), (near_source, near_target), arrived)
    for move in moves:
        move.wait()
    sources[...] = jnp.broadcast_to(near_source[...][None], sources.shape)
    flat = near_target[...].astype(jnp.float32).reshape(targets.shape[1:])
    targets[...] = jnp.broadcast_to(flat.astype(targets.dtype)[None], targets.shape)


def copies_of_both(source, target):
    across, rings = lax.axis_size(TGT), lax.axis_size("z")
    lines = target.shape[0] * target.shape[1]
    return pl.pallas_call(
        copying_kernel,
        out_shape=[
            pltpu.VMEM((across, *source.shape), source.dtype),
            jax.ShapeDtypeStruct((rings, lines, target.shape[2]), target.dtype),
        ],
        in_specs=[pl.BlockSpec(memory_space=pl.ANY)] * 2,
        out_specs=[pl.BlockSpec(memory_space=pltpu.VMEM)] * 2,
        scratch_shapes=[
            pltpu.VMEM(source.shape, source.dtype),
            pltpu.VMEM(target.shape, target.dtype),
            pltpu.SemaphoreType.DMA((2,)),
        ],
    )(*(pltpu.with_memory_space_constraint(one, pltpu.HBM) for one in (source, target)))


def on_device(
    source_embed, target_embed, source_mass, target_mass, target_start, block_pairs, counts
):
    pairs = block_pairs.reshape(block_pairs.shape[2], 2).T
    sources, targets = copies_of_both(
        jnp.swapaxes(source_embed, 1, 2), jnp.swapaxes(target_embed, 1, 2)
    )
    source = exchanged(sources, TGT)
    target = lax.all_gather(exchanged(targets, "z"), "c")
    return local_chain(
        source, target, target_start, source_mass, target_mass, pairs, counts.reshape(1),
        lambda partial: exchanged(partial, TGT), over_src,
    )


def solution(mesh):
    split = Mesh(mesh.devices.reshape(16, 2, 4, 4), (*SRC, *TGT))
    placed = (
        P(SRC, None, TGT),
        P(TGT, None, SRC),
        P(SRC, None),
        P(TGT, None),
        P(TGT, None),
        P(SRC, TGT, None, None),
        P(SRC, TGT),
    )
    return jax.shard_map(
        on_device,
        mesh=split,
        in_specs=placed,
        out_specs=(P(SRC, None), P(TGT, None)),
        check_vma=False,
    )
```

```python
import functools
import math

import jax
import jax.numpy as jnp
from jax import lax
from jax.experimental import pallas as pl
from jax.experimental.pallas import tpu as pltpu
from jax.sharding import Mesh
from jax.sharding import PartitionSpec as P

ITERS = 2
SRC = ("z", "c")
TGT = ("y", "x")

smoothing_epsilon = 4.0
empty_peak = -1e30
log2e = 1.0 / math.log(2.0)
to_log2 = log2e / smoothing_epsilon
group = 16
light_group = 8
pot_most = 20.0
sum_least = 4.3e-18
sum_most = 5e34


def log_sum_exp(pieces):
    peak = functools.reduce(jnp.maximum, pieces)
    total = functools.reduce(jnp.add, [jnp.exp(piece - peak) for piece in pieces])
    return peak + jnp.log(total)


def scores(rows, columns):
    return lax.dot_general(
        rows, columns, (((1,), (0,)), ((), ())), preferred_element_type=jnp.float32
    )


def over_slots(count, size, body):
    whole = count // size

    @pl.loop(0, whole)
    def _(step):
        for lane in range(size):
            body(step * size + lane, None)

    @pl.when(whole * size < count)
    def _():
        for lane in range(size):
            slot = whole * size + lane
            body(slot, slot < count)


def kept_only(value, live):
    return value if live is None else jnp.where(live, value, 0.0)


def within(potential, sums):
    fine = (
        (jnp.abs(potential) <= pot_most) & (sums >= sum_least) & (sums <= sum_most)
    )
    return jnp.min(jnp.where(fine, 1.0, 0.0)) > 0.5


def rows_kept(sums, row_of):
    for block in range(sums.shape[0]):
        sums[block : block + 1, :] = row_of(block)


def exact_rows(count, pairs, rows, columns, potential, peak, total, sums):
    peak[...] = jnp.full_like(peak, empty_peak)
    total[...] = jnp.zeros_like(total)

    @pl.loop(0, count)
    def _(slot):
        source, target = pairs[0, slot], pairs[1, slot]
        value = scores(rows[source], columns[target]) * to_log2
        value = value + potential[pl.ds(target, 1), :] * log2e
        raised = jnp.maximum(peak[source], value)
        total[source] = total[source] * jnp.exp2(peak[source] - raised) + jnp.exp2(
            value - raised
        )
        peak[source] = raised

    def one(block):
        tall, across = peak[block].T, total[block].T
        most = jnp.max(tall, axis=0, keepdims=True)
        summed = jnp.sum(across * jnp.exp2(tall - most), axis=0, keepdims=True)
        return most / log2e + jnp.log(summed)

    rows_kept(sums, one)


def exact_columns(count, pairs, rows, columns, potential, wide, peak, total, sums):
    peak[...] = jnp.full_like(peak, empty_peak)
    total[...] = jnp.zeros_like(total)
    for block in range(wide.shape[0]):
        wide[block] = jnp.broadcast_to(potential[block : block + 1, :], wide.shape[1:]).T

    @pl.loop(0, count)
    def _(slot):
        source, target = pairs[0, slot], pairs[1, slot]
        value = scores(rows[source], columns[target]) * to_log2
        value = value + wide[source] * log2e
        raised = jnp.maximum(peak[target], value)
        total[target] = total[target] * jnp.exp2(peak[target] - raised) + jnp.exp2(
            value - raised
        )
        peak[target] = raised

    def one(block):
        most = jnp.max(peak[block], axis=0, keepdims=True)
        summed = jnp.sum(total[block] * jnp.exp2(peak[block] - most), axis=0, keepdims=True)
        return most / log2e + jnp.log(summed)

    rows_kept(sums, one)


def spread(partial, sums):
    partial[...] = jnp.broadcast_to(sums[...][None], partial.shape)


def row_pass(size, count, pairs, rows, columns, potential, kernel_of, weights, total, peak, sums, partial):
    weights[...] = jnp.exp(potential[...])
    total[...] = jnp.zeros_like(total)

    def body(slot, live):
        source, target = pairs[0, slot], pairs[1, slot]
        value = kernel_of(slot, source, target) * weights[pl.ds(target, 1), :]
        total[source] = total[source] + kept_only(value, live)

    over_slots(count, size, body)
    rows_kept(sums, lambda block: jnp.sum(total[block].T, axis=0, keepdims=True))
    fine = within(potential[...], sums[...])

    @pl.when(fine)
    def _():
        sums[...] = jnp.log(sums[...])

    @pl.when(jnp.logical_not(fine))
    def _():
        exact_rows(count, pairs, rows, columns, potential, peak, total, sums)

    spread(partial, sums)


def first_kernel(
    far_pairs, far_start, far_source_mass, far_target_mass, count_ref, source, target,
    cached, rows, columns, pairs, source_mass, target_mass, partial,
    start, arrived, wide_source, wide_target, weights, total, peak, sums,
):
    moves = fetches(
        (far_pairs, far_start, far_source_mass, far_target_mass),
        (pairs, start, source_mass, target_mass),
        arrived,
    )
    blocks = source.shape[1]
    features = source.shape[2]
    for device in range(source.shape[0]):
        wide_source[:, pl.ds(device * features, features), :] = source[device].astype(
            jnp.float32
        )
    cores, rings, lines, frames = target.shape
    parts = lines // blocks
    for ring in range(rings):
        for core in range(cores):
            at = (ring * cores + core) * parts
            piece = target[core, ring].astype(jnp.float32)
            wide_target[:, pl.ds(at, parts), :] = piece.reshape(blocks, parts, frames)
    for block in range(blocks):
        rows[block] = wide_source[block].T.astype(jnp.bfloat16)
        columns[block] = wide_target[block].astype(jnp.bfloat16)

    for move in moves[:2]:
        move.wait()

    def kernel_of(slot, source, target):
        value = jnp.exp2(scores(rows[source], columns[target]) * to_log2)
        cached[slot] = value
        return value

    row_pass(
        group, count_ref[0], pairs, rows, columns, start, kernel_of,
        weights, total, peak, sums, partial,
    )
    for move in moves[2:]:
        move.wait()


def column_kernel(
    count_ref, pairs, mass, cached, rows, columns, gathered, partial, *refs,
):
    *result, scaling, wide, slim, total, peak, sums, arrived = refs
    count = count_ref[0]
    reached = log_sum_exp([gathered[k] for k in range(gathered.shape[0])])
    scaling[...] = mass[...] - reached
    moves = fetches([scaling] * len(result), result, arrived)
    weights = jnp.exp(scaling[...])
    for block in range(wide.shape[0]):
        wide[block] = jnp.broadcast_to(weights[block : block + 1, :], wide.shape[1:]).T
    slim[...] = jnp.zeros_like(slim)

    def body(slot, live):
        source, target = pairs[0, slot], pairs[1, slot]
        value = cached[slot] * wide[source]
        value = jnp.sum(value.reshape(-1, 8, value.shape[-1]), axis=0)
        slim[target] = slim[target] + kept_only(value, live)

    over_slots(count, light_group, body)
    rows_kept(sums, lambda block: jnp.sum(slim[block], axis=0, keepdims=True))
    fine = within(scaling[...], sums[...])

    @pl.when(fine)
    def _():
        sums[...] = jnp.log(sums[...])

    @pl.when(jnp.logical_not(fine))
    def _():
        exact_columns(count, pairs, rows, columns, scaling, wide, peak, total, sums)

    partial[...] = sums[...]
    for move in moves:
        move.wait()


def row_kernel(
    count_ref, pairs, mass, cached, rows, columns, gathered, partial,
    potential, weights, total, peak, sums,
):
    reached = log_sum_exp([gathered[k] for k in range(gathered.shape[0])])
    potential[...] = mass[...] - reached
    row_pass(
        light_group, count_ref[0], pairs, rows, columns, potential,
        lambda slot, source, target: cached[slot],
        weights, total, peak, sums, partial,
    )


def spaces_of(out):
    space = getattr(out, "memory_space", pltpu.VMEM)
    return pl.ANY if space == pltpu.HBM else space


def called(body, outs, scratch, *operands, far=0):
    places = [
        pltpu.HBM if k < far else pltpu.SMEM if jnp.issubdtype(x.dtype, jnp.integer) else pltpu.VMEM
        for k, x in enumerate(operands)
    ]
    held = [
        x if x.size == 1 else pltpu.with_memory_space_constraint(x, place)
        for x, place in zip(operands, places)
    ]
    return pl.pallas_call(
        body,
        out_shape=outs,
        in_specs=[pl.BlockSpec(memory_space=pl.ANY if x is pltpu.HBM else x) for x in places],
        out_specs=[pl.BlockSpec(memory_space=spaces_of(x)) for x in outs],
        scratch_shapes=scratch,
        compiler_params=pltpu.CompilerParams(vmem_limit_bytes=40 * 1024 * 1024),
    )(*held)


def fetches(sources, places, arrived):
    moves = [
        pltpu.make_async_copy(source, place, arrived.at[k])
        for k, (source, place) in enumerate(zip(sources, places))
    ]
    for move in moves:
        move.start()
    return moves


def copies(x, axis):
    return jnp.broadcast_to(x[None], (lax.axis_size(axis), *x.shape))


def exchanged(x, axis):
    return lax.all_to_all(x, axis, 0, 0, tiled=True)


def local_chain(source, target, start, source_mass, target_mass, pairs, count, over_tgt, over_src):
    f32, bf16 = jnp.float32, jnp.bfloat16
    slots = pairs.shape[1]
    across, source_blocks, depth, frames = source.shape
    features = across * depth
    target_blocks = target.shape[0] * target.shape[1] * target.shape[2] // features
    many = jax.ShapeDtypeStruct((across, source_blocks, frames), f32)
    square = pltpu.VMEM((source_blocks, frames, frames), f32)
    flat = pltpu.VMEM((source_blocks, frames), f32)
    listed = pltpu.SMEM(pairs.shape, jnp.int32)
    arrivals = pltpu.SemaphoreType.DMA
    *kept, pairs, source_mass, target_mass, partial = called(
        first_kernel,
        [
            pltpu.VMEM((slots, frames, frames), f32),
            pltpu.VMEM((source_blocks, frames, features), bf16),
            pltpu.VMEM((target_blocks, features, frames), bf16),
            listed, flat, flat, many,
        ],
        [
            flat, arrivals((4,)),
            pltpu.VMEM((source_blocks, features, frames), f32),
            pltpu.VMEM((target_blocks, features, frames), f32),
            flat, square, square, flat,
        ],
        pairs, start, source_mass, target_mass, count, source, target,
        far=4,
    )
    for iteration in range(ITERS):
        last = iteration == ITERS - 1
        results = called(
            column_kernel,
            [flat, pltpu.HBM((source_blocks, frames), f32)] if last else [flat],
            [
                flat, square, pltpu.VMEM((target_blocks, 8, frames), f32), square, square,
                flat, arrivals((1,)),
            ],
            count, pairs, source_mass, *kept, over_tgt(partial),
        )
        partial, scaling = results[0], results[-1]
        gathered = over_src(partial)
        if not last:
            (partial,) = called(
                row_kernel,
                [many],
                [flat, flat, square, square, flat],
                count, pairs, target_mass, *kept, gathered,
            )
    potential = target_mass - log_sum_exp([gathered[k] for k in range(gathered.shape[0])])
    return scaling, potential


def over_src(partial):
    both = lax.all_gather(partial, "c")
    return exchanged(copies(log_sum_exp([both[0], both[1]]), "z"), "z")


def copying_kernel(far, copied, near, arrived):
    (move,) = fetches((far,), (near,), arrived)
    move.wait()
    lines = near[...].astype(jnp.float32).reshape(copied.shape[1:]).astype(copied.dtype)
    copied[...] = jnp.broadcast_to(lines[None], copied.shape)


def line_copies(x, axis):
    blocks, features, frames = x.shape
    lines = jax.ShapeDtypeStruct((lax.axis_size(axis), blocks * features, frames), x.dtype)
    (copied,) = called(
        copying_kernel,
        [lines],
        [pltpu.VMEM(x.shape, x.dtype), pltpu.SemaphoreType.DMA((1,))],
        x,
        far=1,
    )
    return copied


def on_device(
    source_embed, target_embed, source_mass, target_mass, target_start, block_pairs, counts
):
    pairs = block_pairs.reshape(block_pairs.shape[2], 2).T
    columns = exchanged(line_copies(jnp.swapaxes(target_embed, 1, 2), "z"), "z")
    source = lax.all_gather(jnp.swapaxes(source_embed, 1, 2), TGT)
    target = lax.all_gather(columns, "c")
    return local_chain(
        source, target, target_start, source_mass, target_mass, pairs, counts.reshape(1),
        lambda partial: exchanged(partial, TGT), over_src,
    )


def solution(mesh):
    split = Mesh(mesh.devices.reshape(16, 2, 4, 4), (*SRC, *TGT))
    placed = (
        P(SRC, None, TGT),
        P(TGT, None, SRC),
        P(SRC, None),
        P(TGT, None),
        P(TGT, None),
        P(SRC, TGT, None, None),
        P(SRC, TGT),
    )
    return jax.shard_map(
        on_device,
        mesh=split,
        in_specs=placed,
        out_specs=(P(SRC, None), P(TGT, None)),
        check_vma=False,
    )
```

```python
import functools
import math

import jax
import jax.numpy as jnp
from jax import lax
from jax.experimental import pallas as pl
from jax.experimental.pallas import tpu as pltpu
from jax.sharding import Mesh
from jax.sharding import PartitionSpec as P

ITERS = 2
SRC = ("z", "c")
TGT = ("y", "x")

smoothing_epsilon = 4.0
empty_peak = -1e30
log2e = 1.0 / math.log(2.0)
to_log2 = log2e / smoothing_epsilon
gather_first = 10
sums_first = (2, 0)
group = 16
light_group = 8
pot_most = 20.0
sum_least = 4.3e-18
sum_most = 5e34


def log_sum_exp(pieces):
    peak = functools.reduce(jnp.maximum, pieces)
    total = functools.reduce(jnp.add, [jnp.exp(piece - peak) for piece in pieces])
    return peak + jnp.log(total)


def scores(rows, columns):
    return lax.dot_general(
        rows, columns, (((1,), (0,)), ((), ())), preferred_element_type=jnp.float32
    )


def over_slots(count, size, body):
    whole = count // size

    @pl.loop(0, whole)
    def _(step):
        for lane in range(size):
            body(step * size + lane, None)

    @pl.when(whole * size < count)
    def _():
        for lane in range(size):
            slot = whole * size + lane
            body(slot, slot < count)


def kept_only(value, live):
    return value if live is None else jnp.where(live, value, 0.0)


def within(potential, sums):
    fine = (
        (jnp.abs(potential) <= pot_most) & (sums >= sum_least) & (sums <= sum_most)
    )
    return jnp.min(jnp.where(fine, 1.0, 0.0)) > 0.5


def rows_kept(sums, row_of):
    for block in range(sums.shape[0]):
        sums[block : block + 1, :] = row_of(block)


def exact_rows(count, pairs, rows, columns, potential, peak, total, sums):
    peak[...] = jnp.full_like(peak, empty_peak)
    total[...] = jnp.zeros_like(total)

    @pl.loop(0, count)
    def _(slot):
        source, target = pairs[0, slot], pairs[1, slot]
        value = scores(rows[source], columns[target]) * to_log2
        value = value + potential[pl.ds(target, 1), :] * log2e
        raised = jnp.maximum(peak[source], value)
        total[source] = total[source] * jnp.exp2(peak[source] - raised) + jnp.exp2(
            value - raised
        )
        peak[source] = raised

    def one(block):
        tall, across = peak[block].T, total[block].T
        most = jnp.max(tall, axis=0, keepdims=True)
        summed = jnp.sum(across * jnp.exp2(tall - most), axis=0, keepdims=True)
        return most / log2e + jnp.log(summed)

    rows_kept(sums, one)


def exact_columns(count, pairs, rows, columns, potential, wide, peak, total, sums):
    peak[...] = jnp.full_like(peak, empty_peak)
    total[...] = jnp.zeros_like(total)
    for block in range(wide.shape[0]):
        wide[block] = jnp.broadcast_to(potential[block : block + 1, :], wide.shape[1:]).T

    @pl.loop(0, count)
    def _(slot):
        source, target = pairs[0, slot], pairs[1, slot]
        value = scores(rows[source], columns[target]) * to_log2
        value = value + wide[source] * log2e
        raised = jnp.maximum(peak[target], value)
        total[target] = total[target] * jnp.exp2(peak[target] - raised) + jnp.exp2(
            value - raised
        )
        peak[target] = raised

    def one(block):
        most = jnp.max(peak[block], axis=0, keepdims=True)
        summed = jnp.sum(total[block] * jnp.exp2(peak[block] - most), axis=0, keepdims=True)
        return most / log2e + jnp.log(summed)

    rows_kept(sums, one)


def spread(partial, sums):
    partial[...] = jnp.broadcast_to(sums[...][None], partial.shape)


def row_pass(size, count, pairs, rows, columns, potential, kernel_of, weights, total, peak, sums, partial):
    weights[...] = jnp.exp(potential[...])
    total[...] = jnp.zeros_like(total)

    def body(slot, live):
        source, target = pairs[0, slot], pairs[1, slot]
        value = kernel_of(slot, source, target) * weights[pl.ds(target, 1), :]
        total[source] = total[source] + kept_only(value, live)

    over_slots(count, size, body)
    rows_kept(sums, lambda block: jnp.sum(total[block].T, axis=0, keepdims=True))
    fine = within(potential[...], sums[...])

    @pl.when(fine)
    def _():
        sums[...] = jnp.log(sums[...])

    @pl.when(jnp.logical_not(fine))
    def _():
        exact_rows(count, pairs, rows, columns, potential, peak, total, sums)

    spread(partial, sums)


def first_kernel(
    count_ref, pairs, start, source, target, cached, rows, columns, partial,
    wide_source, wide_target, weights, total, peak, sums,
):
    blocks = source.shape[1]
    features = source.shape[2]
    for device in range(source.shape[0]):
        wide_source[:, pl.ds(device * features, features), :] = source[device].astype(
            jnp.float32
        )
    cores, rings, lines, frames = target.shape
    parts = lines // blocks
    for ring in range(rings):
        for core in range(cores):
            owner = (ring + gather_first) % rings
            at = (owner * cores + core) * parts
            piece = target[core, ring].astype(jnp.float32)
            wide_target[:, pl.ds(at, parts), :] = piece.reshape(blocks, parts, frames)
    for block in range(blocks):
        rows[block] = wide_source[block].T.astype(jnp.bfloat16)
        columns[block] = wide_target[block].astype(jnp.bfloat16)

    def kernel_of(slot, source, target):
        value = jnp.exp2(scores(rows[source], columns[target]) * to_log2)
        cached[slot] = value
        return value

    row_pass(
        group, count_ref[0], pairs, rows, columns, start, kernel_of,
        weights, total, peak, sums, partial,
    )


def column_kernel(
    count_ref, pairs, mass, cached, rows, columns, gathered, partial, *refs,
):
    *result, scaling, wide, slim, total, peak, sums, arrived = refs
    count = count_ref[0]
    reached = log_sum_exp([gathered[k] for k in range(gathered.shape[0])])
    scaling[...] = mass[...] - reached
    moves = fetches([scaling] * len(result), result, arrived)
    weights = jnp.exp(scaling[...])
    for block in range(wide.shape[0]):
        wide[block] = jnp.broadcast_to(weights[block : block + 1, :], wide.shape[1:]).T
    slim[...] = jnp.zeros_like(slim)

    def body(slot, live):
        source, target = pairs[0, slot], pairs[1, slot]
        value = cached[slot] * wide[source]
        value = jnp.sum(value.reshape(-1, 8, value.shape[-1]), axis=0)
        slim[target] = slim[target] + kept_only(value, live)

    over_slots(count, light_group, body)
    rows_kept(sums, lambda block: jnp.sum(slim[block], axis=0, keepdims=True))
    fine = within(scaling[...], sums[...])

    @pl.when(fine)
    def _():
        sums[...] = jnp.log(sums[...])

    @pl.when(jnp.logical_not(fine))
    def _():
        exact_columns(count, pairs, rows, columns, scaling, wide, peak, total, sums)

    partial[...] = sums[...]
    for move in moves:
        move.wait()


def row_kernel(
    count_ref, pairs, mass, cached, rows, columns, gathered, partial,
    potential, weights, total, peak, sums,
):
    reached = log_sum_exp([gathered[k] for k in range(gathered.shape[0])])
    potential[...] = mass[...] - reached
    row_pass(
        light_group, count_ref[0], pairs, rows, columns, potential,
        lambda slot, source, target: cached[slot],
        weights, total, peak, sums, partial,
    )


def spaces_of(out):
    space = getattr(out, "memory_space", pltpu.VMEM)
    return pl.ANY if space == pltpu.HBM else space


def called(body, outs, scratch, *operands, far=0):
    places = [
        pltpu.HBM if k < far else pltpu.SMEM if jnp.issubdtype(x.dtype, jnp.integer) else pltpu.VMEM
        for k, x in enumerate(operands)
    ]
    held = [
        x if x.size == 1 else pltpu.with_memory_space_constraint(x, place)
        for x, place in zip(operands, places)
    ]
    return pl.pallas_call(
        body,
        out_shape=outs,
        in_specs=[pl.BlockSpec(memory_space=pl.ANY if x is pltpu.HBM else x) for x in places],
        out_specs=[pl.BlockSpec(memory_space=spaces_of(x)) for x in outs],
        scratch_shapes=scratch,
        compiler_params=pltpu.CompilerParams(vmem_limit_bytes=40 * 1024 * 1024),
    )(*held)


def fetches(sources, places, arrived):
    moves = [
        pltpu.make_async_copy(source, place, arrived.at[k])
        for k, (source, place) in enumerate(zip(sources, places))
    ]
    for move in moves:
        move.start()
    return moves


def copies(x, axis):
    return jnp.broadcast_to(x[None], (lax.axis_size(axis), *x.shape))


def exchanged(x, axis, first=0):
    if not first:
        return lax.all_to_all(x, axis, 0, 0, tiled=True)
    order = [(k + first) % x.shape[0] for k in range(x.shape[0])]
    return lax.all_to_all(x, axis, 0, 0, axis_index_groups=[order], tiled=True)


def local_chain(source, target, start, source_mass, target_mass, pairs, count, over_tgt, over_src):
    f32, bf16 = jnp.float32, jnp.bfloat16
    slots = pairs.shape[1]
    across, source_blocks, depth, frames = source.shape
    features = across * depth
    target_blocks = target.shape[0] * target.shape[1] * target.shape[2] // features
    many = jax.ShapeDtypeStruct((across, source_blocks, frames), f32)
    square = pltpu.VMEM((source_blocks, frames, frames), f32)
    flat = pltpu.VMEM((source_blocks, frames), f32)
    arrivals = pltpu.SemaphoreType.DMA
    *kept, partial = called(
        first_kernel,
        [
            pltpu.VMEM((slots, frames, frames), f32),
            pltpu.VMEM((source_blocks, frames, features), bf16),
            pltpu.VMEM((target_blocks, features, frames), bf16),
            many,
        ],
        [
            pltpu.VMEM((source_blocks, features, frames), f32),
            pltpu.VMEM((target_blocks, features, frames), f32),
            flat, square, square, flat,
        ],
        count, pairs, start, source, target,
    )
    for iteration in range(ITERS):
        last = iteration == ITERS - 1
        results = called(
            column_kernel,
            [flat, pltpu.HBM((source_blocks, frames), f32)] if last else [flat],
            [
                flat, square, pltpu.VMEM((target_blocks, 8, frames), f32), square, square,
                flat, arrivals((1,)),
            ],
            count, pairs, source_mass, *kept, over_tgt(partial),
        )
        partial, scaling = results[0], results[-1]
        gathered = over_src(partial, sums_first[iteration])
        if not last:
            (partial,) = called(
                row_kernel,
                [many],
                [flat, flat, square, square, flat],
                count, pairs, target_mass, *kept, gathered,
            )
    potential = target_mass - log_sum_exp([gathered[k] for k in range(gathered.shape[0])])
    return scaling, potential


def over_src(partial, first):
    both = lax.all_gather(partial, "c")
    return exchanged(copies(log_sum_exp([both[0], both[1]]), "z"), "z", first)


def copying_kernel(far, *refs):
    small = (len(refs) - 3) // 2
    copied, near, arrived = refs[2 * small :]
    moves = fetches((far, *refs[:small]), (near, *refs[small : 2 * small]), arrived)
    moves[0].wait()
    lines = near[...].astype(jnp.float32).reshape(copied.shape[1:]).astype(copied.dtype)
    copied[...] = jnp.broadcast_to(lines[None], copied.shape)
    for move in moves[1:]:
        move.wait()


def line_copies(x, axis, *small):
    blocks, features, frames = x.shape
    lines = jax.ShapeDtypeStruct((lax.axis_size(axis), blocks * features, frames), x.dtype)
    near = [
        (pltpu.SMEM if jnp.issubdtype(one.dtype, jnp.integer) else pltpu.VMEM)(one.shape, one.dtype)
        for one in small
    ]
    *near, copied = called(
        copying_kernel,
        [*near, lines],
        [pltpu.VMEM(x.shape, x.dtype), pltpu.SemaphoreType.DMA((1 + len(small),))],
        x, *small,
        far=1 + len(small),
    )
    return copied, near


def on_device(
    source_embed, target_embed, source_mass, target_mass, target_start, block_pairs, counts
):
    pairs = block_pairs.reshape(block_pairs.shape[2], 2).T
    copied, (pairs, start, source_mass, target_mass) = line_copies(
        jnp.swapaxes(target_embed, 1, 2), "z", pairs, target_start, source_mass, target_mass
    )
    columns = exchanged(copied, "z", gather_first)
    source = lax.all_gather(jnp.swapaxes(source_embed, 1, 2), TGT)
    target = lax.all_gather(columns, "c")
    return local_chain(
        source, target, start, source_mass, target_mass, pairs, counts.reshape(1),
        lambda partial: exchanged(partial, TGT), over_src,
    )


def solution(mesh):
    split = Mesh(mesh.devices.reshape(16, 2, 4, 4), (*SRC, *TGT))
    placed = (
        P(SRC, None, TGT),
        P(TGT, None, SRC),
        P(SRC, None),
        P(TGT, None),
        P(TGT, None),
        P(SRC, TGT, None, None),
        P(SRC, TGT),
    )
    return jax.shard_map(
        on_device,
        mesh=split,
        in_specs=placed,
        out_specs=(P(SRC, None), P(TGT, None)),
        check_vma=False,
    )
```

```python
import functools
import math

import jax
import jax.numpy as jnp
from jax import lax
from jax.experimental import pallas as pl
from jax.experimental.pallas import tpu as pltpu
from jax.sharding import Mesh
from jax.sharding import PartitionSpec as P

ITERS = 2
SRC = ("z", "c")
TGT = ("y", "x")

smoothing_epsilon = 4.0
empty_peak = -1e30
log2e = 1.0 / math.log(2.0)
to_log2 = log2e / smoothing_epsilon
gather_first = 10
sums_first = (2, 2)
group = 16
light_group = 8
pot_most = 20.0
sum_least = 4.3e-18
sum_most = 5e34


def log_sum_exp(pieces):
    peak = functools.reduce(jnp.maximum, pieces)
    total = functools.reduce(jnp.add, [jnp.exp(piece - peak) for piece in pieces])
    return peak + jnp.log(total)


def scores(rows, columns):
    return lax.dot_general(
        rows, columns, (((1,), (0,)), ((), ())), preferred_element_type=jnp.float32
    )


def over_slots(count, size, body):
    whole = count // size

    @pl.loop(0, whole)
    def _(step):
        for lane in range(size):
            body(step * size + lane, None)

    @pl.when(whole * size < count)
    def _():
        for lane in range(size):
            slot = whole * size + lane
            body(slot, slot < count)


def kept_only(value, live):
    return value if live is None else jnp.where(live, value, 0.0)


def within(potential, sums):
    fine = (
        (jnp.abs(potential) <= pot_most) & (sums >= sum_least) & (sums <= sum_most)
    )
    return jnp.min(jnp.where(fine, 1.0, 0.0)) > 0.5


def rows_kept(sums, row_of):
    for block in range(sums.shape[0]):
        sums[block : block + 1, :] = row_of(block)


def exact_rows(count, pairs, rows, columns, potential, peak, total, sums):
    peak[...] = jnp.full_like(peak, empty_peak)
    total[...] = jnp.zeros_like(total)

    @pl.loop(0, count)
    def _(slot):
        source, target = pairs[0, slot], pairs[1, slot]
        value = scores(rows[source], columns[target]) * to_log2
        value = value + potential[pl.ds(target, 1), :] * log2e
        raised = jnp.maximum(peak[source], value)
        total[source] = total[source] * jnp.exp2(peak[source] - raised) + jnp.exp2(
            value - raised
        )
        peak[source] = raised

    def one(block):
        tall, across = peak[block].T, total[block].T
        most = jnp.max(tall, axis=0, keepdims=True)
        summed = jnp.sum(across * jnp.exp2(tall - most), axis=0, keepdims=True)
        return most / log2e + jnp.log(summed)

    rows_kept(sums, one)


def exact_columns(count, pairs, rows, columns, potential, wide, peak, total, sums):
    peak[...] = jnp.full_like(peak, empty_peak)
    total[...] = jnp.zeros_like(total)
    for block in range(wide.shape[0]):
        wide[block] = jnp.broadcast_to(potential[block : block + 1, :], wide.shape[1:]).T

    @pl.loop(0, count)
    def _(slot):
        source, target = pairs[0, slot], pairs[1, slot]
        value = scores(rows[source], columns[target]) * to_log2
        value = value + wide[source] * log2e
        raised = jnp.maximum(peak[target], value)
        total[target] = total[target] * jnp.exp2(peak[target] - raised) + jnp.exp2(
            value - raised
        )
        peak[target] = raised

    def one(block):
        most = jnp.max(peak[block], axis=0, keepdims=True)
        summed = jnp.sum(total[block] * jnp.exp2(peak[block] - most), axis=0, keepdims=True)
        return most / log2e + jnp.log(summed)

    rows_kept(sums, one)


def spread(partial, sums):
    partial[...] = jnp.broadcast_to(sums[...][None], partial.shape)


def row_pass(size, count, pairs, rows, columns, potential, kernel_of, weights, total, peak, sums, partial):
    weights[...] = jnp.exp(potential[...])
    total[...] = jnp.zeros_like(total)

    def body(slot, live):
        source, target = pairs[0, slot], pairs[1, slot]
        value = kernel_of(slot, source, target) * weights[pl.ds(target, 1), :]
        total[source] = total[source] + kept_only(value, live)

    over_slots(count, size, body)
    rows_kept(sums, lambda block: jnp.sum(total[block].T, axis=0, keepdims=True))
    fine = within(potential[...], sums[...])

    @pl.when(fine)
    def _():
        sums[...] = jnp.log(sums[...])

    @pl.when(jnp.logical_not(fine))
    def _():
        exact_rows(count, pairs, rows, columns, potential, peak, total, sums)

    spread(partial, sums)


def first_kernel(
    count_ref, pairs, start, source, target, cached, rows, columns, partial,
    wide_source, wide_target, weights, total, peak, sums,
):
    blocks = source.shape[1]
    features = source.shape[2]
    for device in range(source.shape[0]):
        wide_source[:, pl.ds(device * features, features), :] = source[device].astype(
            jnp.float32
        )
    cores, rings, lines, frames = target.shape
    parts = lines // blocks
    for ring in range(rings):
        for core in range(cores):
            owner = (ring + gather_first) % rings
            at = (owner * cores + core) * parts
            piece = target[core, ring].astype(jnp.float32)
            wide_target[:, pl.ds(at, parts), :] = piece.reshape(blocks, parts, frames)
    for block in range(blocks):
        rows[block] = wide_source[block].T.astype(jnp.bfloat16)
        columns[block] = wide_target[block].astype(jnp.bfloat16)

    def kernel_of(slot, source, target):
        value = jnp.exp2(scores(rows[source], columns[target]) * to_log2)
        cached[slot] = value
        return value

    row_pass(
        group, count_ref[0], pairs, rows, columns, start, kernel_of,
        weights, total, peak, sums, partial,
    )


def column_kernel(
    count_ref, pairs, mass, cached, rows, columns, gathered, partial, *refs,
):
    *result, scaling, wide, slim, total, peak, sums, arrived = refs
    count = count_ref[0]
    reached = log_sum_exp([gathered[k] for k in range(gathered.shape[0])])
    scaling[...] = mass[...] - reached
    moves = fetches([scaling] * len(result), result, arrived)
    weights = jnp.exp(scaling[...])
    for block in range(wide.shape[0]):
        wide[block] = jnp.broadcast_to(weights[block : block + 1, :], wide.shape[1:]).T
    slim[...] = jnp.zeros_like(slim)

    def body(slot, live):
        source, target = pairs[0, slot], pairs[1, slot]
        value = cached[slot] * wide[source]
        value = jnp.sum(value.reshape(-1, 8, value.shape[-1]), axis=0)
        slim[target] = slim[target] + kept_only(value, live)

    over_slots(count, light_group, body)
    rows_kept(sums, lambda block: jnp.sum(slim[block], axis=0, keepdims=True))
    fine = within(scaling[...], sums[...])

    @pl.when(fine)
    def _():
        sums[...] = jnp.log(sums[...])

    @pl.when(jnp.logical_not(fine))
    def _():
        exact_columns(count, pairs, rows, columns, scaling, wide, peak, total, sums)

    partial[...] = sums[...]
    for move in moves:
        move.wait()


def row_kernel(
    count_ref, pairs, mass, cached, rows, columns, gathered, partial,
    potential, weights, total, peak, sums,
):
    reached = log_sum_exp([gathered[k] for k in range(gathered.shape[0])])
    potential[...] = mass[...] - reached
    row_pass(
        light_group, count_ref[0], pairs, rows, columns, potential,
        lambda slot, source, target: cached[slot],
        weights, total, peak, sums, partial,
    )


def spaces_of(out):
    space = getattr(out, "memory_space", pltpu.VMEM)
    return pl.ANY if space == pltpu.HBM else space


def called(body, outs, scratch, *operands, far=0):
    places = [
        pltpu.HBM if k < far else pltpu.SMEM if jnp.issubdtype(x.dtype, jnp.integer) else pltpu.VMEM
        for k, x in enumerate(operands)
    ]
    held = [
        x if x.size == 1 else pltpu.with_memory_space_constraint(x, place)
        for x, place in zip(operands, places)
    ]
    return pl.pallas_call(
        body,
        out_shape=outs,
        in_specs=[pl.BlockSpec(memory_space=pl.ANY if x is pltpu.HBM else x) for x in places],
        out_specs=[pl.BlockSpec(memory_space=spaces_of(x)) for x in outs],
        scratch_shapes=scratch,
        compiler_params=pltpu.CompilerParams(vmem_limit_bytes=40 * 1024 * 1024),
    )(*held)


def fetches(sources, places, arrived):
    moves = [
        pltpu.make_async_copy(source, place, arrived.at[k])
        for k, (source, place) in enumerate(zip(sources, places))
    ]
    for move in moves:
        move.start()
    return moves


def copies(x, axis):
    return jnp.broadcast_to(x[None], (lax.axis_size(axis), *x.shape))


def exchanged(x, axis, first=0):
    if not first:
        return lax.all_to_all(x, axis, 0, 0, tiled=True)
    order = [(k + first) % x.shape[0] for k in range(x.shape[0])]
    return lax.all_to_all(x, axis, 0, 0, axis_index_groups=[order], tiled=True)


def local_chain(source, target, start, source_mass, target_mass, pairs, count, over_tgt, over_src):
    f32, bf16 = jnp.float32, jnp.bfloat16
    slots = pairs.shape[1]
    across, source_blocks, depth, frames = source.shape
    features = across * depth
    target_blocks = target.shape[0] * target.shape[1] * target.shape[2] // features
    many = jax.ShapeDtypeStruct((across, source_blocks, frames), f32)
    square = pltpu.VMEM((source_blocks, frames, frames), f32)
    flat = pltpu.VMEM((source_blocks, frames), f32)
    arrivals = pltpu.SemaphoreType.DMA
    *kept, partial = called(
        first_kernel,
        [
            pltpu.VMEM((slots, frames, frames), f32),
            pltpu.VMEM((source_blocks, frames, features), bf16),
            pltpu.VMEM((target_blocks, features, frames), bf16),
            many,
        ],
        [
            pltpu.VMEM((source_blocks, features, frames), f32),
            pltpu.VMEM((target_blocks, features, frames), f32),
            flat, square, square, flat,
        ],
        count, pairs, start, source, target,
    )
    for iteration in range(ITERS):
        last = iteration == ITERS - 1
        results = called(
            column_kernel,
            [flat, pltpu.HBM((source_blocks, frames), f32)] if last else [flat],
            [
                flat, square, pltpu.VMEM((target_blocks, 8, frames), f32), square, square,
                flat, arrivals((1,)),
            ],
            count, pairs, source_mass, *kept, over_tgt(partial),
        )
        partial, scaling = results[0], results[-1]
        gathered = over_src(partial, sums_first[iteration])
        if not last:
            (partial,) = called(
                row_kernel,
                [many],
                [flat, flat, square, square, flat],
                count, pairs, target_mass, *kept, gathered,
            )
    potential = target_mass - log_sum_exp([gathered[k] for k in range(gathered.shape[0])])
    return scaling, potential


def over_src(partial, first):
    both = lax.all_gather(partial, "c")
    return exchanged(copies(log_sum_exp([both[0], both[1]]), "z"), "z", first)


def copying_kernel(far, *refs):
    small = (len(refs) - 3) // 2
    copied, near, arrived = refs[2 * small :]
    moves = fetches((far, *refs[:small]), (near, *refs[small : 2 * small]), arrived)
    moves[0].wait()
    lines = near[...].astype(jnp.float32).reshape(copied.shape[1:]).astype(copied.dtype)
    copied[...] = jnp.broadcast_to(lines[None], copied.shape)
    for move in moves[1:]:
        move.wait()


def line_copies(x, axis, *small):
    blocks, features, frames = x.shape
    lines = jax.ShapeDtypeStruct((lax.axis_size(axis), blocks * features, frames), x.dtype)
    near = [
        (pltpu.SMEM if jnp.issubdtype(one.dtype, jnp.integer) else pltpu.VMEM)(one.shape, one.dtype)
        for one in small
    ]
    *near, copied = called(
        copying_kernel,
        [*near, lines],
        [pltpu.VMEM(x.shape, x.dtype), pltpu.SemaphoreType.DMA((1 + len(small),))],
        x, *small,
        far=1 + len(small),
    )
    return copied, near


def on_device(
    source_embed, target_embed, source_mass, target_mass, target_start, block_pairs, counts
):
    pairs = block_pairs.reshape(block_pairs.shape[2], 2).T
    copied, (pairs, start, source_mass, target_mass) = line_copies(
        jnp.swapaxes(target_embed, 1, 2), "z", pairs, target_start, source_mass, target_mass
    )
    columns = exchanged(copied, "z", gather_first)
    source = lax.all_gather(jnp.swapaxes(source_embed, 1, 2), TGT)
    target = lax.all_gather(columns, "c")
    return local_chain(
        source, target, start, source_mass, target_mass, pairs, counts.reshape(1),
        lambda partial: exchanged(partial, TGT), over_src,
    )


def solution(mesh):
    split = Mesh(mesh.devices.reshape(16, 2, 4, 4), (*SRC, *TGT))
    placed = (
        P(SRC, None, TGT),
        P(TGT, None, SRC),
        P(SRC, None),
        P(TGT, None),
        P(TGT, None),
        P(SRC, TGT, None, None),
        P(SRC, TGT),
    )
    return jax.shard_map(
        on_device,
        mesh=split,
        in_specs=placed,
        out_specs=(P(SRC, None), P(TGT, None)),
        check_vma=False,
    )
```

```python
import functools
import math

import jax
import jax.numpy as jnp
from jax import lax
from jax.experimental import pallas as pl
from jax.experimental.pallas import tpu as pltpu
from jax.sharding import Mesh
from jax.sharding import PartitionSpec as P

ITERS = 2
SRC = ("z", "c")

smoothing_epsilon = 4.0
empty_peak = -1e30
log2e = 1.0 / math.log(2.0)
to_log2 = log2e / smoothing_epsilon
gather_first = 10
sums_first = (2, 2)
across_first = 10
group = 16
light_group = 8
pot_most = 20.0
sum_least = 4.3e-18
sum_most = 5e34


def log_sum_exp(pieces):
    peak = functools.reduce(jnp.maximum, pieces)
    total = functools.reduce(jnp.add, [jnp.exp(piece - peak) for piece in pieces])
    return peak + jnp.log(total)


def scores(rows, columns):
    return lax.dot_general(
        rows, columns, (((1,), (0,)), ((), ())), preferred_element_type=jnp.float32
    )


def over_slots(count, size, body):
    whole = count // size

    @pl.loop(0, whole)
    def _(step):
        for lane in range(size):
            body(step * size + lane, None)

    @pl.when(whole * size < count)
    def _():
        for lane in range(size):
            slot = whole * size + lane
            body(slot, slot < count)


def kept_only(value, live):
    return value if live is None else jnp.where(live, value, 0.0)


def within(potential, sums):
    fine = (
        (jnp.abs(potential) <= pot_most) & (sums >= sum_least) & (sums <= sum_most)
    )
    return jnp.min(jnp.where(fine, 1.0, 0.0)) > 0.5


def rows_kept(sums, row_of):
    for block in range(sums.shape[0]):
        sums[block : block + 1, :] = row_of(block)


def exact_rows(count, pairs, rows, columns, potential, peak, total, sums):
    peak[...] = jnp.full_like(peak, empty_peak)
    total[...] = jnp.zeros_like(total)

    @pl.loop(0, count)
    def _(slot):
        source, target = pairs[0, slot], pairs[1, slot]
        value = scores(rows[source], columns[target]) * to_log2
        value = value + potential[pl.ds(target, 1), :] * log2e
        raised = jnp.maximum(peak[source], value)
        total[source] = total[source] * jnp.exp2(peak[source] - raised) + jnp.exp2(
            value - raised
        )
        peak[source] = raised

    def one(block):
        tall, across = peak[block].T, total[block].T
        most = jnp.max(tall, axis=0, keepdims=True)
        summed = jnp.sum(across * jnp.exp2(tall - most), axis=0, keepdims=True)
        return most / log2e + jnp.log(summed)

    rows_kept(sums, one)


def exact_columns(count, pairs, rows, columns, potential, wide, peak, total, sums):
    peak[...] = jnp.full_like(peak, empty_peak)
    total[...] = jnp.zeros_like(total)
    for block in range(wide.shape[0]):
        wide[block] = jnp.broadcast_to(potential[block : block + 1, :], wide.shape[1:]).T

    @pl.loop(0, count)
    def _(slot):
        source, target = pairs[0, slot], pairs[1, slot]
        value = scores(rows[source], columns[target]) * to_log2
        value = value + wide[source] * log2e
        raised = jnp.maximum(peak[target], value)
        total[target] = total[target] * jnp.exp2(peak[target] - raised) + jnp.exp2(
            value - raised
        )
        peak[target] = raised

    def one(block):
        most = jnp.max(peak[block], axis=0, keepdims=True)
        summed = jnp.sum(total[block] * jnp.exp2(peak[block] - most), axis=0, keepdims=True)
        return most / log2e + jnp.log(summed)

    rows_kept(sums, one)


def spread(partial, sums):
    partial[...] = jnp.broadcast_to(sums[...][None], partial.shape)


def row_pass(size, count, pairs, rows, columns, potential, kernel_of, weights, total, peak, sums, partial):
    weights[...] = jnp.exp(potential[...])
    total[...] = jnp.zeros_like(total)

    def body(slot, live):
        source, target = pairs[0, slot], pairs[1, slot]
        value = kernel_of(slot, source, target) * weights[pl.ds(target, 1), :]
        total[source] = total[source] + kept_only(value, live)

    over_slots(count, size, body)
    rows_kept(sums, lambda block: jnp.sum(total[block].T, axis=0, keepdims=True))
    fine = within(potential[...], sums[...])

    @pl.when(fine)
    def _():
        sums[...] = jnp.log(sums[...])

    @pl.when(jnp.logical_not(fine))
    def _():
        exact_rows(count, pairs, rows, columns, potential, peak, total, sums)

    spread(partial, sums)


def first_kernel(
    count_ref, pairs, start, source, target, cached, rows, columns, partial,
    wide_source, wide_target, weights, total, peak, sums,
):
    blocks = source.shape[1]
    features = source.shape[2]
    for device in range(source.shape[0]):
        wide_source[:, pl.ds(device * features, features), :] = source[device].astype(
            jnp.float32
        )
    cores, rings, lines, frames = target.shape
    parts = lines // blocks
    for ring in range(rings):
        for core in range(cores):
            owner = (ring + gather_first) % rings
            at = (owner * cores + core) * parts
            piece = target[core, ring].astype(jnp.float32)
            wide_target[:, pl.ds(at, parts), :] = piece.reshape(blocks, parts, frames)
    for block in range(blocks):
        rows[block] = wide_source[block].T.astype(jnp.bfloat16)
        columns[block] = wide_target[block].astype(jnp.bfloat16)

    def kernel_of(slot, source, target):
        value = jnp.exp2(scores(rows[source], columns[target]) * to_log2)
        cached[slot] = value
        return value

    row_pass(
        group, count_ref[0], pairs, rows, columns, start, kernel_of,
        weights, total, peak, sums, partial,
    )


def column_kernel(
    count_ref, pairs, mass, cached, rows, columns, gathered, partial, *refs,
):
    *result, scaling, wide, slim, total, peak, sums, arrived = refs
    count = count_ref[0]
    reached = log_sum_exp([gathered[k] for k in range(gathered.shape[0])])
    scaling[...] = mass[...] - reached
    moves = fetches([scaling] * len(result), result, arrived)
    weights = jnp.exp(scaling[...])
    for block in range(wide.shape[0]):
        wide[block] = jnp.broadcast_to(weights[block : block + 1, :], wide.shape[1:]).T
    slim[...] = jnp.zeros_like(slim)

    def body(slot, live):
        source, target = pairs[0, slot], pairs[1, slot]
        value = cached[slot] * wide[source]
        value = jnp.sum(value.reshape(-1, 8, value.shape[-1]), axis=0)
        slim[target] = slim[target] + kept_only(value, live)

    over_slots(count, light_group, body)
    rows_kept(sums, lambda block: jnp.sum(slim[block], axis=0, keepdims=True))
    fine = within(scaling[...], sums[...])

    @pl.when(fine)
    def _():
        sums[...] = jnp.log(sums[...])

    @pl.when(jnp.logical_not(fine))
    def _():
        exact_columns(count, pairs, rows, columns, scaling, wide, peak, total, sums)

    partial[...] = sums[...]
    for move in moves:
        move.wait()


def row_kernel(
    count_ref, pairs, mass, cached, rows, columns, gathered, partial,
    potential, weights, total, peak, sums,
):
    reached = log_sum_exp([gathered[k] for k in range(gathered.shape[0])])
    potential[...] = mass[...] - reached
    row_pass(
        light_group, count_ref[0], pairs, rows, columns, potential,
        lambda slot, source, target: cached[slot],
        weights, total, peak, sums, partial,
    )


def spaces_of(out):
    space = getattr(out, "memory_space", pltpu.VMEM)
    return pl.ANY if space == pltpu.HBM else space


def called(body, outs, scratch, *operands, far=0):
    places = [
        pltpu.HBM if k < far else pltpu.SMEM if jnp.issubdtype(x.dtype, jnp.integer) else pltpu.VMEM
        for k, x in enumerate(operands)
    ]
    held = [
        x if x.size == 1 else pltpu.with_memory_space_constraint(x, place)
        for x, place in zip(operands, places)
    ]
    return pl.pallas_call(
        body,
        out_shape=outs,
        in_specs=[pl.BlockSpec(memory_space=pl.ANY if x is pltpu.HBM else x) for x in places],
        out_specs=[pl.BlockSpec(memory_space=spaces_of(x)) for x in outs],
        scratch_shapes=scratch,
        compiler_params=pltpu.CompilerParams(vmem_limit_bytes=40 * 1024 * 1024),
    )(*held)


def fetches(sources, places, arrived):
    moves = [
        pltpu.make_async_copy(source, place, arrived.at[k])
        for k, (source, place) in enumerate(zip(sources, places))
    ]
    for move in moves:
        move.start()
    return moves


def copies(x, axis):
    return jnp.broadcast_to(x[None], (lax.axis_size(axis), *x.shape))


def exchanged(x, axis, first=0):
    if not first:
        return lax.all_to_all(x, axis, 0, 0, tiled=True)
    order = [(k + first) % x.shape[0] for k in range(x.shape[0])]
    return lax.all_to_all(x, axis, 0, 0, axis_index_groups=[order], tiled=True)


def local_chain(source, target, start, source_mass, target_mass, pairs, count, over_tgt, over_src):
    f32, bf16 = jnp.float32, jnp.bfloat16
    slots = pairs.shape[1]
    across, source_blocks, depth, frames = source.shape
    features = across * depth
    target_blocks = target.shape[0] * target.shape[1] * target.shape[2] // features
    many = jax.ShapeDtypeStruct((across, source_blocks, frames), f32)
    square = pltpu.VMEM((source_blocks, frames, frames), f32)
    flat = pltpu.VMEM((source_blocks, frames), f32)
    arrivals = pltpu.SemaphoreType.DMA
    *kept, partial = called(
        first_kernel,
        [
            pltpu.VMEM((slots, frames, frames), f32),
            pltpu.VMEM((source_blocks, frames, features), bf16),
            pltpu.VMEM((target_blocks, features, frames), bf16),
            many,
        ],
        [
            pltpu.VMEM((source_blocks, features, frames), f32),
            pltpu.VMEM((target_blocks, features, frames), f32),
            flat, square, square, flat,
        ],
        count, pairs, start, source, target,
    )
    for iteration in range(ITERS):
        last = iteration == ITERS - 1
        results = called(
            column_kernel,
            [flat, pltpu.HBM((source_blocks, frames), f32)] if last else [flat],
            [
                flat, square, pltpu.VMEM((target_blocks, 8, frames), f32), square, square,
                flat, arrivals((1,)),
            ],
            count, pairs, source_mass, *kept, over_tgt(partial),
        )
        partial, scaling = results[0], results[-1]
        gathered = over_src(partial, sums_first[iteration])
        if not last:
            (partial,) = called(
                row_kernel,
                [many],
                [flat, flat, square, square, flat],
                count, pairs, target_mass, *kept, gathered,
            )
    potential = target_mass - log_sum_exp([gathered[k] for k in range(gathered.shape[0])])
    return scaling, potential


def over_src(partial, first):
    both = lax.all_gather(partial, "c")
    return exchanged(copies(log_sum_exp([both[0], both[1]]), "z"), "z", first)


def copying_kernel(far, *refs):
    small = (len(refs) - 3) // 2
    copied, near, arrived = refs[2 * small :]
    moves = fetches((far, *refs[:small]), (near, *refs[small : 2 * small]), arrived)
    moves[0].wait()
    lines = near[...].astype(jnp.float32).reshape(copied.shape[1:]).astype(copied.dtype)
    copied[...] = jnp.broadcast_to(lines[None], copied.shape)
    for move in moves[1:]:
        move.wait()


def line_copies(x, axis, *small):
    blocks, features, frames = x.shape
    lines = jax.ShapeDtypeStruct((lax.axis_size(axis), blocks * features, frames), x.dtype)
    near = [
        (pltpu.SMEM if jnp.issubdtype(one.dtype, jnp.integer) else pltpu.VMEM)(one.shape, one.dtype)
        for one in small
    ]
    *near, copied = called(
        copying_kernel,
        [*near, lines],
        [pltpu.VMEM(x.shape, x.dtype), pltpu.SemaphoreType.DMA((1 + len(small),))],
        x, *small,
        far=1 + len(small),
    )
    return copied, near


def on_device(
    source_embed, target_embed, source_mass, target_mass, target_start, block_pairs, counts
):
    pairs = block_pairs.reshape(block_pairs.shape[2], 2).T
    copied, (pairs, start, source_mass, target_mass) = line_copies(
        jnp.swapaxes(target_embed, 1, 2), "z", pairs, target_start, source_mass, target_mass
    )
    columns = exchanged(copied, "z", gather_first)
    source = lax.all_gather(jnp.swapaxes(source_embed, 1, 2), "tgt")
    target = lax.all_gather(columns, "c")
    return local_chain(
        source, target, start, source_mass, target_mass, pairs, counts.reshape(1),
        lambda partial: exchanged(partial, "tgt", across_first), over_src,
    )


def solution(mesh):
    split = Mesh(mesh.devices.reshape(16, 2, 16), (*SRC, "tgt"))
    placed = (
        P(SRC, None, "tgt"),
        P("tgt", None, SRC),
        P(SRC, None),
        P("tgt", None),
        P("tgt", None),
        P(SRC, "tgt", None, None),
        P(SRC, "tgt"),
    )
    return jax.shard_map(
        on_device,
        mesh=split,
        in_specs=placed,
        out_specs=(P(SRC, None), P("tgt", None)),
        check_vma=False,
    )
```

```python
import functools
import math

import jax
import jax.numpy as jnp
from jax import lax
from jax.experimental import pallas as pl
from jax.experimental.pallas import tpu as pltpu
from jax.sharding import Mesh
from jax.sharding import PartitionSpec as P

ITERS = 2
SRC = ("z", "c")

smoothing_epsilon = 4.0
empty_peak = -1e30
log2e = 1.0 / math.log(2.0)
to_log2 = log2e / smoothing_epsilon
ring_first = 10
across_first = 10
group = 16
light_group = 8
pot_most = 20.0
sum_least = 4.3e-18
sum_most = 5e34


def log_sum_exp(pieces):
    peak = functools.reduce(jnp.maximum, pieces)
    total = functools.reduce(jnp.add, [jnp.exp(piece - peak) for piece in pieces])
    return peak + jnp.log(total)


def scores(rows, columns):
    return lax.dot_general(
        rows, columns, (((1,), (0,)), ((), ())), preferred_element_type=jnp.float32
    )


def over_slots(count, size, body):
    whole = count // size

    @pl.loop(0, whole)
    def _(step):
        for lane in range(size):
            body(step * size + lane, None)

    @pl.when(whole * size < count)
    def _():
        for lane in range(size):
            slot = whole * size + lane
            body(slot, slot < count)


def kept_only(value, live):
    return value if live is None else jnp.where(live, value, 0.0)


def within(potential, sums):
    fine = (
        (jnp.abs(potential) <= pot_most) & (sums >= sum_least) & (sums <= sum_most)
    )
    return jnp.min(jnp.where(fine, 1.0, 0.0)) > 0.5


def rows_kept(sums, row_of):
    for block in range(sums.shape[0]):
        sums[block : block + 1, :] = row_of(block)


def exact_rows(count, pairs, rows, columns, potential, peak, total, sums):
    peak[...] = jnp.full_like(peak, empty_peak)
    total[...] = jnp.zeros_like(total)

    @pl.loop(0, count)
    def _(slot):
        source, target = pairs[0, slot], pairs[1, slot]
        value = scores(rows[source], columns[target]) * to_log2
        value = value + potential[pl.ds(target, 1), :] * log2e
        raised = jnp.maximum(peak[source], value)
        total[source] = total[source] * jnp.exp2(peak[source] - raised) + jnp.exp2(
            value - raised
        )
        peak[source] = raised

    def one(block):
        tall, across = peak[block].T, total[block].T
        most = jnp.max(tall, axis=0, keepdims=True)
        summed = jnp.sum(across * jnp.exp2(tall - most), axis=0, keepdims=True)
        return most / log2e + jnp.log(summed)

    rows_kept(sums, one)


def exact_columns(count, pairs, rows, columns, potential, wide, peak, total, sums):
    peak[...] = jnp.full_like(peak, empty_peak)
    total[...] = jnp.zeros_like(total)
    for block in range(wide.shape[0]):
        wide[block] = jnp.broadcast_to(potential[block : block + 1, :], wide.shape[1:]).T

    @pl.loop(0, count)
    def _(slot):
        source, target = pairs[0, slot], pairs[1, slot]
        value = scores(rows[source], columns[target]) * to_log2
        value = value + wide[source] * log2e
        raised = jnp.maximum(peak[target], value)
        total[target] = total[target] * jnp.exp2(peak[target] - raised) + jnp.exp2(
            value - raised
        )
        peak[target] = raised

    def one(block):
        most = jnp.max(peak[block], axis=0, keepdims=True)
        summed = jnp.sum(total[block] * jnp.exp2(peak[block] - most), axis=0, keepdims=True)
        return most / log2e + jnp.log(summed)

    rows_kept(sums, one)


def spread(partial, sums):
    partial[...] = jnp.broadcast_to(sums[...][None], partial.shape)


def row_pass(size, count, pairs, rows, columns, potential, kernel_of, weights, total, peak, sums, partial):
    weights[...] = jnp.exp(potential[...])
    total[...] = jnp.zeros_like(total)

    def body(slot, live):
        source, target = pairs[0, slot], pairs[1, slot]
        value = kernel_of(slot, source, target) * weights[pl.ds(target, 1), :]
        total[source] = total[source] + kept_only(value, live)

    over_slots(count, size, body)
    rows_kept(sums, lambda block: jnp.sum(total[block].T, axis=0, keepdims=True))
    fine = within(potential[...], sums[...])

    @pl.when(fine)
    def _():
        sums[...] = jnp.log(sums[...])

    @pl.when(jnp.logical_not(fine))
    def _():
        exact_rows(count, pairs, rows, columns, potential, peak, total, sums)

    spread(partial, sums)


def source_kernel(
    far_pairs, far_start, far_source_mass, far_target_mass, source,
    rows, pairs, start, source_mass, target_mass, wide, arrived,
):
    moves = fetches(
        (far_pairs, far_start, far_source_mass, far_target_mass),
        (pairs, start, source_mass, target_mass),
        arrived,
    )
    features = source.shape[2]
    across = source.shape[0]
    for device in range(across):
        at = (device + across_first) % across * features
        wide[:, pl.ds(at, features), :] = source[device].astype(jnp.float32)
    for block in range(source.shape[1]):
        rows[block] = wide[block].T.astype(rows.dtype)
    for move in moves:
        move.wait()


def first_kernel(
    count_ref, pairs, start, rows, target, cached, columns, partial,
    wide, weights, total, peak, sums,
):
    cores, rings, lines, frames = target.shape
    blocks = columns.shape[0]
    parts = lines // blocks
    for ring in range(rings):
        for core in range(cores):
            owner = (ring + ring_first) % rings
            at = (owner * cores + core) * parts
            piece = target[core, ring].astype(jnp.float32)
            wide[:, pl.ds(at, parts), :] = piece.reshape(blocks, parts, frames)
    for block in range(blocks):
        columns[block] = wide[block].astype(columns.dtype)

    def kernel_of(slot, source, target):
        value = jnp.exp2(scores(rows[source], columns[target]) * to_log2)
        cached[slot] = value
        return value

    row_pass(
        group, count_ref[0], pairs, rows, columns, start, kernel_of,
        weights, total, peak, sums, partial,
    )


def column_kernel(
    count_ref, pairs, mass, cached, rows, columns, gathered, partial, *refs,
):
    *result, scaling, wide, slim, total, peak, sums, arrived = refs
    count = count_ref[0]
    reached = log_sum_exp([gathered[k] for k in range(gathered.shape[0])])
    scaling[...] = mass[...] - reached
    moves = fetches([scaling] * len(result), result, arrived)
    weights = jnp.exp(scaling[...])
    for block in range(wide.shape[0]):
        wide[block] = jnp.broadcast_to(weights[block : block + 1, :], wide.shape[1:]).T
    slim[...] = jnp.zeros_like(slim)

    def body(slot, live):
        source, target = pairs[0, slot], pairs[1, slot]
        value = cached[slot] * wide[source]
        value = jnp.sum(value.reshape(-1, 8, value.shape[-1]), axis=0)
        slim[target] = slim[target] + kept_only(value, live)

    over_slots(count, light_group, body)
    rows_kept(sums, lambda block: jnp.sum(slim[block], axis=0, keepdims=True))
    fine = within(scaling[...], sums[...])

    @pl.when(fine)
    def _():
        sums[...] = jnp.log(sums[...])

    @pl.when(jnp.logical_not(fine))
    def _():
        exact_columns(count, pairs, rows, columns, scaling, wide, peak, total, sums)

    partial[...] = sums[...]
    for move in moves:
        move.wait()


def row_kernel(
    count_ref, pairs, mass, cached, rows, columns, gathered, partial,
    potential, weights, total, peak, sums,
):
    reached = log_sum_exp([gathered[k] for k in range(gathered.shape[0])])
    potential[...] = mass[...] - reached
    row_pass(
        light_group, count_ref[0], pairs, rows, columns, potential,
        lambda slot, source, target: cached[slot],
        weights, total, peak, sums, partial,
    )


def spaces_of(out):
    space = getattr(out, "memory_space", pltpu.VMEM)
    return pl.ANY if space == pltpu.HBM else space


def called(body, outs, scratch, *operands, far=0):
    places = [
        pltpu.HBM if k < far else pltpu.SMEM if jnp.issubdtype(x.dtype, jnp.integer) else pltpu.VMEM
        for k, x in enumerate(operands)
    ]
    held = [
        x if x.size == 1 else pltpu.with_memory_space_constraint(x, place)
        for x, place in zip(operands, places)
    ]
    return pl.pallas_call(
        body,
        out_shape=outs,
        in_specs=[pl.BlockSpec(memory_space=pl.ANY if x is pltpu.HBM else x) for x in places],
        out_specs=[pl.BlockSpec(memory_space=spaces_of(x)) for x in outs],
        scratch_shapes=scratch,
        compiler_params=pltpu.CompilerParams(vmem_limit_bytes=40 * 1024 * 1024),
    )(*held)


def fetches(sources, places, arrived):
    moves = [
        pltpu.make_async_copy(source, place, arrived.at[k])
        for k, (source, place) in enumerate(zip(sources, places))
    ]
    for move in moves:
        move.start()
    return moves


def copies(x, axis):
    return jnp.broadcast_to(x[None], (lax.axis_size(axis), *x.shape))


def exchanged(x, axis, first):
    order = [(k + first) % x.shape[0] for k in range(x.shape[0])]
    return lax.all_to_all(x, axis, 0, 0, axis_index_groups=[order], tiled=True)


def local_chain(source, target, start, source_mass, target_mass, pairs, count, over_tgt, over_src):
    f32, bf16 = jnp.float32, jnp.bfloat16
    slots = pairs.shape[1]
    across, source_blocks, depth, frames = source.shape
    features = across * depth
    target_blocks = target.shape[0] * target.shape[1] * target.shape[2] // features
    many = jax.ShapeDtypeStruct((across, source_blocks, frames), f32)
    square = pltpu.VMEM((source_blocks, frames, frames), f32)
    flat = pltpu.VMEM((source_blocks, frames), f32)
    listed = pltpu.SMEM(pairs.shape, jnp.int32)
    arrivals = pltpu.SemaphoreType.DMA
    rows, pairs, start, source_mass, target_mass = called(
        source_kernel,
        [pltpu.VMEM((source_blocks, frames, features), bf16), listed, flat, flat, flat],
        [pltpu.VMEM((source_blocks, features, frames), f32), arrivals((4,))],
        pairs, start, source_mass, target_mass, source,
        far=4,
    )
    cached, columns, partial = called(
        first_kernel,
        [
            pltpu.VMEM((slots, frames, frames), f32),
            pltpu.VMEM((target_blocks, features, frames), bf16),
            many,
        ],
        [
            pltpu.VMEM((target_blocks, features, frames), f32),
            flat, square, square, flat,
        ],
        count, pairs, start, rows, target,
    )
    kept = [cached, rows, columns]
    for iteration in range(ITERS):
        last = iteration == ITERS - 1
        results = called(
            column_kernel,
            [flat, pltpu.HBM((source_blocks, frames), f32)] if last else [flat],
            [
                flat, square, pltpu.VMEM((target_blocks, 8, frames), f32), square, square,
                flat, arrivals((1,)),
            ],
            count, pairs, source_mass, *kept, over_tgt(partial),
        )
        partial, scaling = results[0], results[-1]
        gathered = over_src(partial)
        if not last:
            (partial,) = called(
                row_kernel,
                [many],
                [flat, flat, square, square, flat],
                count, pairs, target_mass, *kept, gathered,
            )
    potential = target_mass - log_sum_exp([gathered[k] for k in range(gathered.shape[0])])
    return scaling, potential


def over_src(partial):
    both = lax.all_gather(partial, "c")
    return exchanged(copies(log_sum_exp([both[0], both[1]]), "z"), "z", ring_first)


def copying_kernel(source, target, sources, targets, near_source, near_target, arrived):
    moves = fetches((source, target), (near_source, near_target), arrived)
    for move in moves:
        move.wait()
    sources[...] = jnp.broadcast_to(near_source[...][None], sources.shape)
    flat = near_target[...].astype(jnp.float32).reshape(targets.shape[1:])
    targets[...] = jnp.broadcast_to(flat.astype(targets.dtype)[None], targets.shape)


def copies_of_both(source, target):
    across, rings = lax.axis_size("tgt"), lax.axis_size("z")
    lines = target.shape[0] * target.shape[1]
    return pl.pallas_call(
        copying_kernel,
        out_shape=[
            pltpu.VMEM((across, *source.shape), source.dtype),
            jax.ShapeDtypeStruct((rings, lines, target.shape[2]), target.dtype),
        ],
        in_specs=[pl.BlockSpec(memory_space=pl.ANY)] * 2,
        out_specs=[pl.BlockSpec(memory_space=pltpu.VMEM)] * 2,
        scratch_shapes=[
            pltpu.VMEM(source.shape, source.dtype),
            pltpu.VMEM(target.shape, target.dtype),
            pltpu.SemaphoreType.DMA((2,)),
        ],
    )(*(pltpu.with_memory_space_constraint(one, pltpu.HBM) for one in (source, target)))


def on_device(
    source_embed, target_embed, source_mass, target_mass, target_start, block_pairs, counts
):
    pairs = block_pairs.reshape(block_pairs.shape[2], 2).T
    sources, targets = copies_of_both(
        jnp.swapaxes(source_embed, 1, 2), jnp.swapaxes(target_embed, 1, 2)
    )
    source = exchanged(sources, "tgt", across_first)
    target = lax.all_gather(exchanged(targets, "z", ring_first), "c")
    return local_chain(
        source, target, target_start, source_mass, target_mass, pairs, counts.reshape(1),
        lambda partial: exchanged(partial, "tgt", across_first), over_src,
    )


def solution(mesh):
    split = Mesh(mesh.devices.reshape(16, 2, 16), (*SRC, "tgt"))
    placed = (
        P(SRC, None, "tgt"),
        P("tgt", None, SRC),
        P(SRC, None),
        P("tgt", None),
        P("tgt", None),
        P(SRC, "tgt", None, None),
        P(SRC, "tgt"),
    )
    return jax.shard_map(
        on_device,
        mesh=split,
        in_specs=placed,
        out_specs=(P(SRC, None), P("tgt", None)),
        check_vma=False,
    )
```

```python
import functools
import math

import jax
import jax.numpy as jnp
from jax import lax
from jax.experimental import pallas as pl
from jax.experimental.pallas import tpu as pltpu
from jax.sharding import Mesh
from jax.sharding import PartitionSpec as P

ITERS = 2
SRC = ("z", "c")

smoothing_epsilon = 4.0
empty_peak = -1e30
log2e = 1.0 / math.log(2.0)
to_log2 = log2e / smoothing_epsilon
gather_first = 10
sums_first = (9, 9)
across_first = 10
group = 16
light_group = 8
pot_most = 20.0
sum_least = 4.3e-18
sum_most = 5e34


def log_sum_exp(pieces):
    peak = functools.reduce(jnp.maximum, pieces)
    total = functools.reduce(jnp.add, [jnp.exp(piece - peak) for piece in pieces])
    return peak + jnp.log(total)


def scores(rows, columns):
    return lax.dot_general(
        rows, columns, (((1,), (0,)), ((), ())), preferred_element_type=jnp.float32
    )


def over_slots(count, size, body):
    whole = count // size

    @pl.loop(0, whole)
    def _(step):
        for lane in range(size):
            body(step * size + lane, None)

    @pl.when(whole * size < count)
    def _():
        for lane in range(size):
            slot = whole * size + lane
            body(slot, slot < count)


def kept_only(value, live):
    return value if live is None else jnp.where(live, value, 0.0)


def within(potential, sums):
    fine = (
        (jnp.abs(potential) <= pot_most) & (sums >= sum_least) & (sums <= sum_most)
    )
    return jnp.min(jnp.where(fine, 1.0, 0.0)) > 0.5


def rows_kept(sums, row_of):
    for block in range(sums.shape[0]):
        sums[block : block + 1, :] = row_of(block)


def exact_rows(count, pairs, rows, columns, potential, peak, total, sums):
    peak[...] = jnp.full_like(peak, empty_peak)
    total[...] = jnp.zeros_like(total)

    @pl.loop(0, count)
    def _(slot):
        source, target = pairs[0, slot], pairs[1, slot]
        value = scores(rows[source], columns[target]) * to_log2
        value = value + potential[pl.ds(target, 1), :] * log2e
        raised = jnp.maximum(peak[source], value)
        total[source] = total[source] * jnp.exp2(peak[source] - raised) + jnp.exp2(
            value - raised
        )
        peak[source] = raised

    def one(block):
        tall, across = peak[block].T, total[block].T
        most = jnp.max(tall, axis=0, keepdims=True)
        summed = jnp.sum(across * jnp.exp2(tall - most), axis=0, keepdims=True)
        return most / log2e + jnp.log(summed)

    rows_kept(sums, one)


def exact_columns(count, pairs, rows, columns, potential, wide, peak, total, sums):
    peak[...] = jnp.full_like(peak, empty_peak)
    total[...] = jnp.zeros_like(total)
    for block in range(wide.shape[0]):
        wide[block] = jnp.broadcast_to(potential[block : block + 1, :], wide.shape[1:]).T

    @pl.loop(0, count)
    def _(slot):
        source, target = pairs[0, slot], pairs[1, slot]
        value = scores(rows[source], columns[target]) * to_log2
        value = value + wide[source] * log2e
        raised = jnp.maximum(peak[target], value)
        total[target] = total[target] * jnp.exp2(peak[target] - raised) + jnp.exp2(
            value - raised
        )
        peak[target] = raised

    def one(block):
        most = jnp.max(peak[block], axis=0, keepdims=True)
        summed = jnp.sum(total[block] * jnp.exp2(peak[block] - most), axis=0, keepdims=True)
        return most / log2e + jnp.log(summed)

    rows_kept(sums, one)


def spread(partial, sums):
    partial[...] = jnp.broadcast_to(sums[...][None], partial.shape)


def row_pass(size, count, pairs, rows, columns, potential, kernel_of, weights, total, peak, sums, partial):
    weights[...] = jnp.exp(potential[...])
    total[...] = jnp.zeros_like(total)

    def body(slot, live):
        source, target = pairs[0, slot], pairs[1, slot]
        value = kernel_of(slot, source, target) * weights[pl.ds(target, 1), :]
        total[source] = total[source] + kept_only(value, live)

    over_slots(count, size, body)
    rows_kept(sums, lambda block: jnp.sum(total[block].T, axis=0, keepdims=True))
    fine = within(potential[...], sums[...])

    @pl.when(fine)
    def _():
        sums[...] = jnp.log(sums[...])

    @pl.when(jnp.logical_not(fine))
    def _():
        exact_rows(count, pairs, rows, columns, potential, peak, total, sums)

    spread(partial, sums)


def first_kernel(
    count_ref, pairs, start, source, target, cached, rows, columns, partial,
    wide_source, wide_target, weights, total, peak, sums,
):
    blocks = source.shape[1]
    features = source.shape[2]
    for device in range(source.shape[0]):
        wide_source[:, pl.ds(device * features, features), :] = source[device].astype(
            jnp.float32
        )
    cores, rings, lines, frames = target.shape
    parts = lines // blocks
    for ring in range(rings):
        for core in range(cores):
            owner = (ring + gather_first) % rings
            at = (owner * cores + core) * parts
            piece = target[core, ring].astype(jnp.float32)
            wide_target[:, pl.ds(at, parts), :] = piece.reshape(blocks, parts, frames)
    for block in range(blocks):
        rows[block] = wide_source[block].T.astype(jnp.bfloat16)
        columns[block] = wide_target[block].astype(jnp.bfloat16)

    def kernel_of(slot, source, target):
        value = jnp.exp2(scores(rows[source], columns[target]) * to_log2)
        cached[slot] = value
        return value

    row_pass(
        group, count_ref[0], pairs, rows, columns, start, kernel_of,
        weights, total, peak, sums, partial,
    )


def column_kernel(
    count_ref, pairs, mass, cached, rows, columns, gathered, partial, *refs,
):
    *result, scaling, wide, slim, total, peak, sums, arrived = refs
    count = count_ref[0]
    reached = log_sum_exp([gathered[k] for k in range(gathered.shape[0])])
    scaling[...] = mass[...] - reached
    moves = fetches([scaling] * len(result), result, arrived)
    weights = jnp.exp(scaling[...])
    for block in range(wide.shape[0]):
        wide[block] = jnp.broadcast_to(weights[block : block + 1, :], wide.shape[1:]).T
    slim[...] = jnp.zeros_like(slim)

    def body(slot, live):
        source, target = pairs[0, slot], pairs[1, slot]
        value = cached[slot] * wide[source]
        value = jnp.sum(value.reshape(-1, 8, value.shape[-1]), axis=0)
        slim[target] = slim[target] + kept_only(value, live)

    over_slots(count, light_group, body)
    rows_kept(sums, lambda block: jnp.sum(slim[block], axis=0, keepdims=True))
    fine = within(scaling[...], sums[...])

    @pl.when(fine)
    def _():
        sums[...] = jnp.log(sums[...])

    @pl.when(jnp.logical_not(fine))
    def _():
        exact_columns(count, pairs, rows, columns, scaling, wide, peak, total, sums)

    partial[...] = sums[...]
    for move in moves:
        move.wait()


def row_kernel(
    count_ref, pairs, mass, cached, rows, columns, gathered, partial,
    potential, weights, total, peak, sums,
):
    reached = log_sum_exp([gathered[k] for k in range(gathered.shape[0])])
    potential[...] = mass[...] - reached
    row_pass(
        light_group, count_ref[0], pairs, rows, columns, potential,
        lambda slot, source, target: cached[slot],
        weights, total, peak, sums, partial,
    )


def spaces_of(out):
    space = getattr(out, "memory_space", pltpu.VMEM)
    return pl.ANY if space == pltpu.HBM else space


def called(body, outs, scratch, *operands, far=0):
    places = [
        pltpu.HBM if k < far else pltpu.SMEM if jnp.issubdtype(x.dtype, jnp.integer) else pltpu.VMEM
        for k, x in enumerate(operands)
    ]
    held = [
        x if x.size == 1 else pltpu.with_memory_space_constraint(x, place)
        for x, place in zip(operands, places)
    ]
    return pl.pallas_call(
        body,
        out_shape=outs,
        in_specs=[pl.BlockSpec(memory_space=pl.ANY if x is pltpu.HBM else x) for x in places],
        out_specs=[pl.BlockSpec(memory_space=spaces_of(x)) for x in outs],
        scratch_shapes=scratch,
        compiler_params=pltpu.CompilerParams(vmem_limit_bytes=40 * 1024 * 1024),
    )(*held)


def fetches(sources, places, arrived):
    moves = [
        pltpu.make_async_copy(source, place, arrived.at[k])
        for k, (source, place) in enumerate(zip(sources, places))
    ]
    for move in moves:
        move.start()
    return moves


def copies(x, axis):
    return jnp.broadcast_to(x[None], (lax.axis_size(axis), *x.shape))


def exchanged(x, axis, first=0):
    if not first:
        return lax.all_to_all(x, axis, 0, 0, tiled=True)
    order = [(k + first) % x.shape[0] for k in range(x.shape[0])]
    return lax.all_to_all(x, axis, 0, 0, axis_index_groups=[order], tiled=True)


def local_chain(source, target, start, source_mass, target_mass, pairs, count, over_tgt, over_src):
    f32, bf16 = jnp.float32, jnp.bfloat16
    slots = pairs.shape[1]
    across, source_blocks, depth, frames = source.shape
    features = across * depth
    target_blocks = target.shape[0] * target.shape[1] * target.shape[2] // features
    many = jax.ShapeDtypeStruct((across, source_blocks, frames), f32)
    square = pltpu.VMEM((source_blocks, frames, frames), f32)
    flat = pltpu.VMEM((source_blocks, frames), f32)
    arrivals = pltpu.SemaphoreType.DMA
    *kept, partial = called(
        first_kernel,
        [
            pltpu.VMEM((slots, frames, frames), f32),
            pltpu.VMEM((source_blocks, frames, features), bf16),
            pltpu.VMEM((target_blocks, features, frames), bf16),
            many,
        ],
        [
            pltpu.VMEM((source_blocks, features, frames), f32),
            pltpu.VMEM((target_blocks, features, frames), f32),
            flat, square, square, flat,
        ],
        count, pairs, start, source, target,
    )
    for iteration in range(ITERS):
        last = iteration == ITERS - 1
        results = called(
            column_kernel,
            [flat, pltpu.HBM((source_blocks, frames), f32)] if last else [flat],
            [
                flat, square, pltpu.VMEM((target_blocks, 8, frames), f32), square, square,
                flat, arrivals((1,)),
            ],
            count, pairs, source_mass, *kept, over_tgt(partial),
        )
        partial, scaling = results[0], results[-1]
        gathered = over_src(partial, sums_first[iteration])
        if not last:
            (partial,) = called(
                row_kernel,
                [many],
                [flat, flat, square, square, flat],
                count, pairs, target_mass, *kept, gathered,
            )
    potential = target_mass - log_sum_exp([gathered[k] for k in range(gathered.shape[0])])
    return scaling, potential


def over_src(partial, first):
    both = lax.all_gather(partial, "c")
    return exchanged(copies(log_sum_exp([both[0], both[1]]), "z"), "z", first)


def copying_kernel(far, *refs):
    small = (len(refs) - 3) // 2
    copied, near, arrived = refs[2 * small :]
    moves = fetches((far, *refs[:small]), (near, *refs[small : 2 * small]), arrived)
    moves[0].wait()
    lines = near[...].astype(jnp.float32).reshape(copied.shape[1:]).astype(copied.dtype)
    copied[...] = jnp.broadcast_to(lines[None], copied.shape)
    for move in moves[1:]:
        move.wait()


def line_copies(x, axis, *small):
    blocks, features, frames = x.shape
    lines = jax.ShapeDtypeStruct((lax.axis_size(axis), blocks * features, frames), x.dtype)
    near = [
        (pltpu.SMEM if jnp.issubdtype(one.dtype, jnp.integer) else pltpu.VMEM)(one.shape, one.dtype)
        for one in small
    ]
    *near, copied = called(
        copying_kernel,
        [*near, lines],
        [pltpu.VMEM(x.shape, x.dtype), pltpu.SemaphoreType.DMA((1 + len(small),))],
        x, *small,
        far=1 + len(small),
    )
    return copied, near


def on_device(
    source_embed, target_embed, source_mass, target_mass, target_start, block_pairs, counts
):
    pairs = block_pairs.reshape(block_pairs.shape[2], 2).T
    copied, (pairs, start, source_mass, target_mass) = line_copies(
        jnp.swapaxes(target_embed, 1, 2), "z", pairs, target_start, source_mass, target_mass
    )
    columns = exchanged(copied, "z", gather_first)
    source = lax.all_gather(jnp.swapaxes(source_embed, 1, 2), "tgt")
    target = lax.all_gather(columns, "c")
    return local_chain(
        source, target, start, source_mass, target_mass, pairs, counts.reshape(1),
        lambda partial: exchanged(partial, "tgt", across_first), over_src,
    )


def solution(mesh):
    split = Mesh(mesh.devices.reshape(16, 2, 16), (*SRC, "tgt"))
    placed = (
        P(SRC, None, "tgt"),
        P("tgt", None, SRC),
        P(SRC, None),
        P("tgt", None),
        P("tgt", None),
        P(SRC, "tgt", None, None),
        P(SRC, "tgt"),
    )
    return jax.shard_map(
        on_device,
        mesh=split,
        in_specs=placed,
        out_specs=(P(SRC, None), P("tgt", None)),
        check_vma=False,
    )
```

```python
import functools
import math

import jax
import jax.numpy as jnp
from jax import lax
from jax.experimental import pallas as pl
from jax.experimental.pallas import tpu as pltpu
from jax.sharding import Mesh
from jax.sharding import PartitionSpec as P

ITERS = 2
SRC = ("z", "c")

smoothing_epsilon = 4.0
empty_peak = -1e30
log2e = 1.0 / math.log(2.0)
to_log2 = log2e / smoothing_epsilon
gather_first = 10
sums_first = (2, 2)
across_first = 10
side = 4
turn = 2
group = 16
light_group = 8
pot_most = 20.0
sum_least = 4.3e-18
sum_most = 5e34


def log_sum_exp(pieces):
    peak = functools.reduce(jnp.maximum, pieces)
    total = functools.reduce(jnp.add, [jnp.exp(piece - peak) for piece in pieces])
    return peak + jnp.log(total)


def scores(rows, columns):
    return lax.dot_general(
        rows, columns, (((1,), (0,)), ((), ())), preferred_element_type=jnp.float32
    )


def over_slots(count, size, body):
    whole = count // size

    @pl.loop(0, whole)
    def _(step):
        for lane in range(size):
            body(step * size + lane, None)

    @pl.when(whole * size < count)
    def _():
        for lane in range(size):
            slot = whole * size + lane
            body(slot, slot < count)


def kept_only(value, live):
    return value if live is None else jnp.where(live, value, 0.0)


def within(potential, sums):
    fine = (
        (jnp.abs(potential) <= pot_most) & (sums >= sum_least) & (sums <= sum_most)
    )
    return jnp.min(jnp.where(fine, 1.0, 0.0)) > 0.5


def rows_kept(sums, row_of):
    for block in range(sums.shape[0]):
        sums[block : block + 1, :] = row_of(block)


def exact_rows(count, pairs, rows, columns, potential, peak, total, sums):
    peak[...] = jnp.full_like(peak, empty_peak)
    total[...] = jnp.zeros_like(total)

    @pl.loop(0, count)
    def _(slot):
        source, target = pairs[0, slot], pairs[1, slot]
        value = scores(rows[source], columns[target]) * to_log2
        value = value + potential[pl.ds(target, 1), :] * log2e
        raised = jnp.maximum(peak[source], value)
        total[source] = total[source] * jnp.exp2(peak[source] - raised) + jnp.exp2(
            value - raised
        )
        peak[source] = raised

    def one(block):
        tall, across = peak[block].T, total[block].T
        most = jnp.max(tall, axis=0, keepdims=True)
        summed = jnp.sum(across * jnp.exp2(tall - most), axis=0, keepdims=True)
        return most / log2e + jnp.log(summed)

    rows_kept(sums, one)


def exact_columns(count, pairs, rows, columns, potential, wide, peak, total, sums):
    peak[...] = jnp.full_like(peak, empty_peak)
    total[...] = jnp.zeros_like(total)
    for block in range(wide.shape[0]):
        wide[block] = jnp.broadcast_to(potential[block : block + 1, :], wide.shape[1:]).T

    @pl.loop(0, count)
    def _(slot):
        source, target = pairs[0, slot], pairs[1, slot]
        value = scores(rows[source], columns[target]) * to_log2
        value = value + wide[source] * log2e
        raised = jnp.maximum(peak[target], value)
        total[target] = total[target] * jnp.exp2(peak[target] - raised) + jnp.exp2(
            value - raised
        )
        peak[target] = raised

    def one(block):
        most = jnp.max(peak[block], axis=0, keepdims=True)
        summed = jnp.sum(total[block] * jnp.exp2(peak[block] - most), axis=0, keepdims=True)
        return most / log2e + jnp.log(summed)

    rows_kept(sums, one)


def spread(partial, sums):
    partial[...] = jnp.broadcast_to(sums[...][None], partial.shape)


def row_pass(size, count, pairs, rows, columns, potential, kernel_of, weights, total, peak, sums, partial):
    weights[...] = jnp.exp(potential[...])
    total[...] = jnp.zeros_like(total)

    def body(slot, live):
        source, target = pairs[0, slot], pairs[1, slot]
        value = kernel_of(slot, source, target) * weights[pl.ds(target, 1), :]
        total[source] = total[source] + kept_only(value, live)

    over_slots(count, size, body)
    rows_kept(sums, lambda block: jnp.sum(total[block].T, axis=0, keepdims=True))
    fine = within(potential[...], sums[...])

    @pl.when(fine)
    def _():
        sums[...] = jnp.log(sums[...])

    @pl.when(jnp.logical_not(fine))
    def _():
        exact_rows(count, pairs, rows, columns, potential, peak, total, sums)

    spread(partial, sums)


def first_kernel(
    count_ref, pairs, start, source, target, cached, rows, columns, partial,
    wide_source, wide_target, weights, total, peak, sums,
):
    blocks = source.shape[1]
    features = source.shape[2]
    for device in range(source.shape[0]):
        owner = device // side * side + (device + turn) % side
        wide_source[:, pl.ds(owner * features, features), :] = source[device].astype(
            jnp.float32
        )
    cores, rings, lines, frames = target.shape
    parts = lines // blocks
    for ring in range(rings):
        for core in range(cores):
            owner = (ring + gather_first) % rings
            at = (owner * cores + core) * parts
            piece = target[core, ring].astype(jnp.float32)
            wide_target[:, pl.ds(at, parts), :] = piece.reshape(blocks, parts, frames)
    for block in range(blocks):
        rows[block] = wide_source[block].T.astype(jnp.bfloat16)
        columns[block] = wide_target[block].astype(jnp.bfloat16)

    def kernel_of(slot, source, target):
        value = jnp.exp2(scores(rows[source], columns[target]) * to_log2)
        cached[slot] = value
        return value

    row_pass(
        group, count_ref[0], pairs, rows, columns, start, kernel_of,
        weights, total, peak, sums, partial,
    )


def column_kernel(
    count_ref, pairs, mass, cached, rows, columns, gathered, partial, *refs,
):
    *result, scaling, wide, slim, total, peak, sums, arrived = refs
    count = count_ref[0]
    reached = log_sum_exp([gathered[k] for k in range(gathered.shape[0])])
    scaling[...] = mass[...] - reached
    moves = fetches([scaling] * len(result), result, arrived)
    weights = jnp.exp(scaling[...])
    for block in range(wide.shape[0]):
        wide[block] = jnp.broadcast_to(weights[block : block + 1, :], wide.shape[1:]).T
    slim[...] = jnp.zeros_like(slim)

    def body(slot, live):
        source, target = pairs[0, slot], pairs[1, slot]
        value = cached[slot] * wide[source]
        value = jnp.sum(value.reshape(-1, 8, value.shape[-1]), axis=0)
        slim[target] = slim[target] + kept_only(value, live)

    over_slots(count, light_group, body)
    rows_kept(sums, lambda block: jnp.sum(slim[block], axis=0, keepdims=True))
    fine = within(scaling[...], sums[...])

    @pl.when(fine)
    def _():
        sums[...] = jnp.log(sums[...])

    @pl.when(jnp.logical_not(fine))
    def _():
        exact_columns(count, pairs, rows, columns, scaling, wide, peak, total, sums)

    partial[...] = sums[...]
    for move in moves:
        move.wait()


def row_kernel(
    count_ref, pairs, mass, cached, rows, columns, gathered, partial,
    potential, weights, total, peak, sums,
):
    reached = log_sum_exp([gathered[k] for k in range(gathered.shape[0])])
    potential[...] = mass[...] - reached
    row_pass(
        light_group, count_ref[0], pairs, rows, columns, potential,
        lambda slot, source, target: cached[slot],
        weights, total, peak, sums, partial,
    )


def spaces_of(out):
    space = getattr(out, "memory_space", pltpu.VMEM)
    return pl.ANY if space == pltpu.HBM else space


def called(body, outs, scratch, *operands, far=0):
    places = [
        pltpu.HBM if k < far else pltpu.SMEM if jnp.issubdtype(x.dtype, jnp.integer) else pltpu.VMEM
        for k, x in enumerate(operands)
    ]
    held = [
        x if x.size == 1 else pltpu.with_memory_space_constraint(x, place)
        for x, place in zip(operands, places)
    ]
    return pl.pallas_call(
        body,
        out_shape=outs,
        in_specs=[pl.BlockSpec(memory_space=pl.ANY if x is pltpu.HBM else x) for x in places],
        out_specs=[pl.BlockSpec(memory_space=spaces_of(x)) for x in outs],
        scratch_shapes=scratch,
        compiler_params=pltpu.CompilerParams(vmem_limit_bytes=40 * 1024 * 1024),
    )(*held)


def fetches(sources, places, arrived):
    moves = [
        pltpu.make_async_copy(source, place, arrived.at[k])
        for k, (source, place) in enumerate(zip(sources, places))
    ]
    for move in moves:
        move.start()
    return moves


def copies(x, axis):
    return jnp.broadcast_to(x[None], (lax.axis_size(axis), *x.shape))


def exchanged(x, axis, first=0):
    if not first:
        return lax.all_to_all(x, axis, 0, 0, tiled=True)
    order = [(k + first) % x.shape[0] for k in range(x.shape[0])]
    return lax.all_to_all(x, axis, 0, 0, axis_index_groups=[order], tiled=True)


def local_chain(source, target, start, source_mass, target_mass, pairs, count, over_tgt, over_src):
    f32, bf16 = jnp.float32, jnp.bfloat16
    slots = pairs.shape[1]
    across, source_blocks, depth, frames = source.shape
    features = across * depth
    target_blocks = target.shape[0] * target.shape[1] * target.shape[2] // features
    many = jax.ShapeDtypeStruct((across, source_blocks, frames), f32)
    square = pltpu.VMEM((source_blocks, frames, frames), f32)
    flat = pltpu.VMEM((source_blocks, frames), f32)
    arrivals = pltpu.SemaphoreType.DMA
    *kept, partial = called(
        first_kernel,
        [
            pltpu.VMEM((slots, frames, frames), f32),
            pltpu.VMEM((source_blocks, frames, features), bf16),
            pltpu.VMEM((target_blocks, features, frames), bf16),
            many,
        ],
        [
            pltpu.VMEM((source_blocks, features, frames), f32),
            pltpu.VMEM((target_blocks, features, frames), f32),
            flat, square, square, flat,
        ],
        count, pairs, start, source, target,
    )
    for iteration in range(ITERS):
        last = iteration == ITERS - 1
        results = called(
            column_kernel,
            [flat, pltpu.HBM((source_blocks, frames), f32)] if last else [flat],
            [
                flat, square, pltpu.VMEM((target_blocks, 8, frames), f32), square, square,
                flat, arrivals((1,)),
            ],
            count, pairs, source_mass, *kept, over_tgt(partial),
        )
        partial, scaling = results[0], results[-1]
        gathered = over_src(partial, sums_first[iteration])
        if not last:
            (partial,) = called(
                row_kernel,
                [many],
                [flat, flat, square, square, flat],
                count, pairs, target_mass, *kept, gathered,
            )
    potential = target_mass - log_sum_exp([gathered[k] for k in range(gathered.shape[0])])
    return scaling, potential


def over_src(partial, first):
    both = lax.all_gather(partial, "c")
    return exchanged(copies(log_sum_exp([both[0], both[1]]), "z"), "z", first)


def copying_kernel(target, source, *refs):
    small = (len(refs) - 5) // 2
    copied, sources, near, near_source, arrived = refs[2 * small :]
    moves = fetches(
        (target, source, *refs[:small]), (near, near_source, *refs[small : 2 * small]), arrived
    )
    moves[0].wait()
    lines = near[...].astype(jnp.float32).reshape(copied.shape[1:]).astype(copied.dtype)
    copied[...] = jnp.broadcast_to(lines[None], copied.shape)
    moves[1].wait()
    sources[...] = jnp.broadcast_to(near_source[...][None], sources.shape)
    for move in moves[2:]:
        move.wait()


def line_copies(target, source, *small):
    blocks, features, frames = target.shape
    lines = jax.ShapeDtypeStruct((lax.axis_size("z"), blocks * features, frames), target.dtype)
    near = [
        (pltpu.SMEM if jnp.issubdtype(one.dtype, jnp.integer) else pltpu.VMEM)(one.shape, one.dtype)
        for one in small
    ]
    *near, copied, sources = called(
        copying_kernel,
        [*near, lines, pltpu.VMEM((side, *source.shape), source.dtype)],
        [
            pltpu.VMEM(target.shape, target.dtype), pltpu.VMEM(source.shape, source.dtype),
            pltpu.SemaphoreType.DMA((2 + len(small),)),
        ],
        target, source, *small,
        far=2 + len(small),
    )
    return copied, sources, near


def source_gathered(sources):
    rows = [[y * side + (x + turn) % side for x in range(side)] for y in range(side)]
    columns = [[y * side + x for y in range(side)] for x in range(side)]
    across = lax.all_to_all(sources, "tgt", 0, 0, axis_index_groups=rows, tiled=True)
    return lax.all_gather(across, "tgt", axis_index_groups=columns, tiled=True)


def on_device(
    source_embed, target_embed, source_mass, target_mass, target_start, block_pairs, counts
):
    pairs = block_pairs.reshape(block_pairs.shape[2], 2).T
    copied, sources, (pairs, start, source_mass, target_mass) = line_copies(
        jnp.swapaxes(target_embed, 1, 2), jnp.swapaxes(source_embed, 1, 2),
        pairs, target_start, source_mass, target_mass,
    )
    columns = exchanged(copied, "z", gather_first)
    source = source_gathered(sources)
    target = lax.all_gather(columns, "c")
    return local_chain(
        source, target, start, source_mass, target_mass, pairs, counts.reshape(1),
        lambda partial: exchanged(partial, "tgt", across_first), over_src,
    )


def solution(mesh):
    split = Mesh(mesh.devices.reshape(16, 2, 16), (*SRC, "tgt"))
    placed = (
        P(SRC, None, "tgt"),
        P("tgt", None, SRC),
        P(SRC, None),
        P("tgt", None),
        P("tgt", None),
        P(SRC, "tgt", None, None),
        P(SRC, "tgt"),
    )
    return jax.shard_map(
        on_device,
        mesh=split,
        in_specs=placed,
        out_specs=(P(SRC, None), P("tgt", None)),
        check_vma=False,
    )
```

```python
import functools
import math

import jax
import jax.numpy as jnp
from jax import lax
from jax.experimental import pallas as pl
from jax.experimental.pallas import tpu as pltpu
from jax.sharding import Mesh
from jax.sharding import PartitionSpec as P

ITERS = 2
SRC = ("z", "c")

smoothing_epsilon = 4.0
empty_peak = -1e30
log2e = 1.0 / math.log(2.0)
to_log2 = log2e / smoothing_epsilon
gather_first = 10
sums_first = (2, 2)
across_first = 10
walk = (0, 1, 2, 3, 7, 6, 5, 4, 8, 9, 10, 11, 15, 14, 13, 12)
group = 16
light_group = 8
pot_most = 20.0
sum_least = 4.3e-18
sum_most = 5e34


def log_sum_exp(pieces):
    peak = functools.reduce(jnp.maximum, pieces)
    total = functools.reduce(jnp.add, [jnp.exp(piece - peak) for piece in pieces])
    return peak + jnp.log(total)


def scores(rows, columns):
    return lax.dot_general(
        rows, columns, (((1,), (0,)), ((), ())), preferred_element_type=jnp.float32
    )


def over_slots(count, size, body):
    whole = count // size

    @pl.loop(0, whole)
    def _(step):
        for lane in range(size):
            body(step * size + lane, None)

    @pl.when(whole * size < count)
    def _():
        for lane in range(size):
            slot = whole * size + lane
            body(slot, slot < count)


def kept_only(value, live):
    return value if live is None else jnp.where(live, value, 0.0)


def within(potential, sums):
    fine = (
        (jnp.abs(potential) <= pot_most) & (sums >= sum_least) & (sums <= sum_most)
    )
    return jnp.min(jnp.where(fine, 1.0, 0.0)) > 0.5


def rows_kept(sums, row_of):
    for block in range(sums.shape[0]):
        sums[block : block + 1, :] = row_of(block)


def exact_rows(count, pairs, rows, columns, potential, peak, total, sums):
    peak[...] = jnp.full_like(peak, empty_peak)
    total[...] = jnp.zeros_like(total)

    @pl.loop(0, count)
    def _(slot):
        source, target = pairs[0, slot], pairs[1, slot]
        value = scores(rows[source], columns[target]) * to_log2
        value = value + potential[pl.ds(target, 1), :] * log2e
        raised = jnp.maximum(peak[source], value)
        total[source] = total[source] * jnp.exp2(peak[source] - raised) + jnp.exp2(
            value - raised
        )
        peak[source] = raised

    def one(block):
        tall, across = peak[block].T, total[block].T
        most = jnp.max(tall, axis=0, keepdims=True)
        summed = jnp.sum(across * jnp.exp2(tall - most), axis=0, keepdims=True)
        return most / log2e + jnp.log(summed)

    rows_kept(sums, one)


def exact_columns(count, pairs, rows, columns, potential, wide, peak, total, sums):
    peak[...] = jnp.full_like(peak, empty_peak)
    total[...] = jnp.zeros_like(total)
    for block in range(wide.shape[0]):
        wide[block] = jnp.broadcast_to(potential[block : block + 1, :], wide.shape[1:]).T

    @pl.loop(0, count)
    def _(slot):
        source, target = pairs[0, slot], pairs[1, slot]
        value = scores(rows[source], columns[target]) * to_log2
        value = value + wide[source] * log2e
        raised = jnp.maximum(peak[target], value)
        total[target] = total[target] * jnp.exp2(peak[target] - raised) + jnp.exp2(
            value - raised
        )
        peak[target] = raised

    def one(block):
        most = jnp.max(peak[block], axis=0, keepdims=True)
        summed = jnp.sum(total[block] * jnp.exp2(peak[block] - most), axis=0, keepdims=True)
        return most / log2e + jnp.log(summed)

    rows_kept(sums, one)


def spread(partial, sums):
    partial[...] = jnp.broadcast_to(sums[...][None], partial.shape)


def row_pass(size, count, pairs, rows, columns, potential, kernel_of, weights, total, peak, sums, partial):
    weights[...] = jnp.exp(potential[...])
    total[...] = jnp.zeros_like(total)

    def body(slot, live):
        source, target = pairs[0, slot], pairs[1, slot]
        value = kernel_of(slot, source, target) * weights[pl.ds(target, 1), :]
        total[source] = total[source] + kept_only(value, live)

    over_slots(count, size, body)
    rows_kept(sums, lambda block: jnp.sum(total[block].T, axis=0, keepdims=True))
    fine = within(potential[...], sums[...])

    @pl.when(fine)
    def _():
        sums[...] = jnp.log(sums[...])

    @pl.when(jnp.logical_not(fine))
    def _():
        exact_rows(count, pairs, rows, columns, potential, peak, total, sums)

    spread(partial, sums)


def first_kernel(
    count_ref, pairs, start, source, target, cached, rows, columns, partial,
    wide_source, wide_target, weights, total, peak, sums,
):
    blocks = source.shape[1]
    features = source.shape[2]
    for device in range(source.shape[0]):
        wide_source[:, pl.ds(walk[device] * features, features), :] = source[device].astype(
            jnp.float32
        )
    cores, rings, lines, frames = target.shape
    parts = lines // blocks
    for ring in range(rings):
        for core in range(cores):
            owner = (ring + gather_first) % rings
            at = (owner * cores + core) * parts
            piece = target[core, ring].astype(jnp.float32)
            wide_target[:, pl.ds(at, parts), :] = piece.reshape(blocks, parts, frames)
    for block in range(blocks):
        rows[block] = wide_source[block].T.astype(jnp.bfloat16)
        columns[block] = wide_target[block].astype(jnp.bfloat16)

    def kernel_of(slot, source, target):
        value = jnp.exp2(scores(rows[source], columns[target]) * to_log2)
        cached[slot] = value
        return value

    row_pass(
        group, count_ref[0], pairs, rows, columns, start, kernel_of,
        weights, total, peak, sums, partial,
    )


def column_kernel(
    count_ref, pairs, mass, cached, rows, columns, gathered, partial, *refs,
):
    *result, scaling, wide, slim, total, peak, sums, arrived = refs
    count = count_ref[0]
    reached = log_sum_exp([gathered[k] for k in range(gathered.shape[0])])
    scaling[...] = mass[...] - reached
    moves = fetches([scaling] * len(result), result, arrived)
    weights = jnp.exp(scaling[...])
    for block in range(wide.shape[0]):
        wide[block] = jnp.broadcast_to(weights[block : block + 1, :], wide.shape[1:]).T
    slim[...] = jnp.zeros_like(slim)

    def body(slot, live):
        source, target = pairs[0, slot], pairs[1, slot]
        value = cached[slot] * wide[source]
        value = jnp.sum(value.reshape(-1, 8, value.shape[-1]), axis=0)
        slim[target] = slim[target] + kept_only(value, live)

    over_slots(count, light_group, body)
    rows_kept(sums, lambda block: jnp.sum(slim[block], axis=0, keepdims=True))
    fine = within(scaling[...], sums[...])

    @pl.when(fine)
    def _():
        sums[...] = jnp.log(sums[...])

    @pl.when(jnp.logical_not(fine))
    def _():
        exact_columns(count, pairs, rows, columns, scaling, wide, peak, total, sums)

    partial[...] = sums[...]
    for move in moves:
        move.wait()


def row_kernel(
    count_ref, pairs, mass, cached, rows, columns, gathered, partial,
    potential, weights, total, peak, sums,
):
    reached = log_sum_exp([gathered[k] for k in range(gathered.shape[0])])
    potential[...] = mass[...] - reached
    row_pass(
        light_group, count_ref[0], pairs, rows, columns, potential,
        lambda slot, source, target: cached[slot],
        weights, total, peak, sums, partial,
    )


def spaces_of(out):
    space = getattr(out, "memory_space", pltpu.VMEM)
    return pl.ANY if space == pltpu.HBM else space


def called(body, outs, scratch, *operands, far=0):
    places = [
        pltpu.HBM if k < far else pltpu.SMEM if jnp.issubdtype(x.dtype, jnp.integer) else pltpu.VMEM
        for k, x in enumerate(operands)
    ]
    held = [
        x if x.size == 1 else pltpu.with_memory_space_constraint(x, place)
        for x, place in zip(operands, places)
    ]
    return pl.pallas_call(
        body,
        out_shape=outs,
        in_specs=[pl.BlockSpec(memory_space=pl.ANY if x is pltpu.HBM else x) for x in places],
        out_specs=[pl.BlockSpec(memory_space=spaces_of(x)) for x in outs],
        scratch_shapes=scratch,
        compiler_params=pltpu.CompilerParams(vmem_limit_bytes=40 * 1024 * 1024),
    )(*held)


def fetches(sources, places, arrived):
    moves = [
        pltpu.make_async_copy(source, place, arrived.at[k])
        for k, (source, place) in enumerate(zip(sources, places))
    ]
    for move in moves:
        move.start()
    return moves


def copies(x, axis):
    return jnp.broadcast_to(x[None], (lax.axis_size(axis), *x.shape))


def exchanged(x, axis, first=0):
    if not first:
        return lax.all_to_all(x, axis, 0, 0, tiled=True)
    order = [(k + first) % x.shape[0] for k in range(x.shape[0])]
    return lax.all_to_all(x, axis, 0, 0, axis_index_groups=[order], tiled=True)


def local_chain(source, target, start, source_mass, target_mass, pairs, count, over_tgt, over_src):
    f32, bf16 = jnp.float32, jnp.bfloat16
    slots = pairs.shape[1]
    across, source_blocks, depth, frames = source.shape
    features = across * depth
    target_blocks = target.shape[0] * target.shape[1] * target.shape[2] // features
    many = jax.ShapeDtypeStruct((across, source_blocks, frames), f32)
    square = pltpu.VMEM((source_blocks, frames, frames), f32)
    flat = pltpu.VMEM((source_blocks, frames), f32)
    arrivals = pltpu.SemaphoreType.DMA
    *kept, partial = called(
        first_kernel,
        [
            pltpu.VMEM((slots, frames, frames), f32),
            pltpu.VMEM((source_blocks, frames, features), bf16),
            pltpu.VMEM((target_blocks, features, frames), bf16),
            many,
        ],
        [
            pltpu.VMEM((source_blocks, features, frames), f32),
            pltpu.VMEM((target_blocks, features, frames), f32),
            flat, square, square, flat,
        ],
        count, pairs, start, source, target,
    )
    for iteration in range(ITERS):
        last = iteration == ITERS - 1
        results = called(
            column_kernel,
            [flat, pltpu.HBM((source_blocks, frames), f32)] if last else [flat],
            [
                flat, square, pltpu.VMEM((target_blocks, 8, frames), f32), square, square,
                flat, arrivals((1,)),
            ],
            count, pairs, source_mass, *kept, over_tgt(partial),
        )
        partial, scaling = results[0], results[-1]
        gathered = over_src(partial, sums_first[iteration])
        if not last:
            (partial,) = called(
                row_kernel,
                [many],
                [flat, flat, square, square, flat],
                count, pairs, target_mass, *kept, gathered,
            )
    potential = target_mass - log_sum_exp([gathered[k] for k in range(gathered.shape[0])])
    return scaling, potential


def over_src(partial, first):
    both = lax.all_gather(partial, "c")
    return exchanged(copies(log_sum_exp([both[0], both[1]]), "z"), "z", first)


def copying_kernel(far, *refs):
    small = (len(refs) - 3) // 2
    copied, near, arrived = refs[2 * small :]
    moves = fetches((far, *refs[:small]), (near, *refs[small : 2 * small]), arrived)
    moves[0].wait()
    lines = near[...].astype(jnp.float32).reshape(copied.shape[1:]).astype(copied.dtype)
    copied[...] = jnp.broadcast_to(lines[None], copied.shape)
    for move in moves[1:]:
        move.wait()


def line_copies(x, axis, *small):
    blocks, features, frames = x.shape
    lines = jax.ShapeDtypeStruct((lax.axis_size(axis), blocks * features, frames), x.dtype)
    near = [
        (pltpu.SMEM if jnp.issubdtype(one.dtype, jnp.integer) else pltpu.VMEM)(one.shape, one.dtype)
        for one in small
    ]
    *near, copied = called(
        copying_kernel,
        [*near, lines],
        [pltpu.VMEM(x.shape, x.dtype), pltpu.SemaphoreType.DMA((1 + len(small),))],
        x, *small,
        far=1 + len(small),
    )
    return copied, near


def on_device(
    source_embed, target_embed, source_mass, target_mass, target_start, block_pairs, counts
):
    pairs = block_pairs.reshape(block_pairs.shape[2], 2).T
    copied, (pairs, start, source_mass, target_mass) = line_copies(
        jnp.swapaxes(target_embed, 1, 2), "z", pairs, target_start, source_mass, target_mass
    )
    columns = exchanged(copied, "z", gather_first)
    source = lax.all_gather(
        jnp.swapaxes(source_embed, 1, 2), "tgt", axis_index_groups=[list(walk)]
    )
    target = lax.all_gather(columns, "c")
    return local_chain(
        source, target, start, source_mass, target_mass, pairs, counts.reshape(1),
        lambda partial: exchanged(partial, "tgt", across_first), over_src,
    )


def solution(mesh):
    split = Mesh(mesh.devices.reshape(16, 2, 16), (*SRC, "tgt"))
    placed = (
        P(SRC, None, "tgt"),
        P("tgt", None, SRC),
        P(SRC, None),
        P("tgt", None),
        P("tgt", None),
        P(SRC, "tgt", None, None),
        P(SRC, "tgt"),
    )
    return jax.shard_map(
        on_device,
        mesh=split,
        in_specs=placed,
        out_specs=(P(SRC, None), P("tgt", None)),
        check_vma=False,
    )
```
